32 devices in a mesh: dp: 16 (over z, x, core), tensor: 2 (over y).
Axes of the slice: x: 2, y: 2, z: 4, core: 2. Of those that a mesh axis runs over, the one named last changes fastest.
Arguments:
- inputs: bfloat16 [21920, 384], P('dp'), may hold values from -6 to 6
- cotangent: bfloat16 [21920, 384], P('dp'), may hold values from -6 to 6
- w_qkv: float32 [384, 3, 384], P('dp', None, 'tensor'), may hold values from -0.4375 to 0.4375
- w_out: float32 [384, 384], P('tensor', 'dp'), may hold values from -1.25 to 1.25
- w_up: float32 [384, 1536], P('dp', 'tensor'), may hold values from -0.3125 to 0.3125
- w_down: float32 [1536, 384], P('tensor', 'dp'), may hold values from -0.15625 to 0.15625
- vectors: float32 [8, 384], P(None, 'dp'), may hold values from -0.9 to 2, as said below
- head_bias: float32 [2, 6, 64], P(None, 'tensor', 'dp'), may hold values from -0.4 to 0.4
- up_bias: float32 [12, 128], P('tensor', 'dp'), may hold values from -1.2 to 1.2
- mom_qkv: float32 [384, 3, 384], P('dp', None, 'tensor'), may hold values from -1280 to 1280
- mom_out: float32 [384, 384], P('tensor', 'dp'), may hold values from -384 to 384
- mom_up: float32 [384, 1536], P('dp', 'tensor'), may hold values from -320 to 320
- mom_down: float32 [1536, 384], P('tensor', 'dp'), may hold values from -640 to 640
- vec_first: float32 [8, 384], P(None, 'dp'), may hold values from -96 to 96
- vec_second: float32 [8, 384], P(None, 'dp'), may hold values from 10.96 to 175.36
- head_first: float32 [2, 6, 64], P(None, 'tensor', 'dp'), may hold values from -192 to 192
- head_second: float32 [2, 6, 64], P(None, 'tensor', 'dp'), may hold values from 43.84 to 657.6
- unit_first: float32 [12, 128], P('tensor', 'dp'), may hold values from -32 to 32
- unit_second: float32 [12, 128], P('tensor', 'dp'), may hold values from 1.096 to 19.728
Outputs:
- output: bfloat16 [21920, 384], P('dp')
- grad_in: bfloat16 [21920, 384], P('dp')
- grad_qkv: float32 [384, 3, 384], P('dp', None, 'tensor')
- grad_out: float32 [384, 384], P('tensor', 'dp')
- grad_up: float32 [384, 1536], P('dp', 'tensor')
- grad_down: float32 [1536, 384], P('tensor', 'dp')
- moment_qkv: float32 [384, 3, 384], P('dp', None, 'tensor')
- moment_out: float32 [384, 384], P('tensor', 'dp')
- moment_up: float32 [384, 1536], P('dp', 'tensor')
- moment_down: float32 [1536, 384], P('tensor', 'dp')
- new_qkv: float32 [384, 3, 384], P('dp', None, 'tensor')
- new_out: float32 [384, 384], P('tensor', 'dp')
- new_up: float32 [384, 1536], P('dp', 'tensor')
- new_down: float32 [1536, 384], P('tensor', 'dp')
- vec_grad: float32 [8, 384], P(None, 'dp')
- vec_second_new: float32 [8, 384], P(None, 'dp')
- vec_new: float32 [8, 384], P(None, 'dp')
- head_grad: float32 [2, 6, 64], P(None, 'tensor', 'dp')
- head_second_new: float32 [2, 6, 64], P(None, 'tensor', 'dp')
- head_new: float32 [2, 6, 64], P(None, 'tensor', 'dp')
- unit_grad: float32 [12, 128], P('tensor', 'dp')
- unit_second_new: float32 [12, 128], P('tensor', 'dp')
- unit_new: float32 [12, 128], P('tensor', 'dp')
The draws below stay inside these ranges and needn't reach their ends.
Inputs may be any that keep to these rules, and one draw needn't show every extreme that they name: `vectors`: rows in order: the first norm's gain and shift, the attention output bias, its layer scale, the second norm's gain and shift, the feed-forward output bias, its layer scale; gains and layer scales are positive.
All inputs are finite; a program needn't handle non-finite values.
Results may differ from the reference program's by a relative error of at most 0.017.
The reference program's roundings to bfloat16 on the way count: a program that leaves them out, or rounds other values in their place, can miss the bound.
Values may be sent and summed in bfloat16 or wider, within the bound.
No kernel may reach another device: no remote copies, remote signals or barrier semaphores. Data moves between devices by JAX's collectives and lax.ppermute only.
A program may use at most 128 MiB of HBM per device.

```python
import math
from functools import partial
import jax
import jax.numpy as jnp
from jax import lax

D = 384
FF = 1536
HD = 64
HEADS = 6
SEQ = 1370
STEP = 10
TOKENS = 21920


def draw_vectors(key, part):
    key = jax.random.fold_in(key, 11)
    gain_key, shift_key, scale_key = jax.random.split(key, 3)
    gains = 0.7 + 0.6 * jax.random.uniform(gain_key, (2, D), dtype=jnp.float32)
    shifts = 0.3 * jax.random.truncated_normal(shift_key, -3.0, 3.0, (4, D), dtype=jnp.float32)
    scales = jnp.exp(jax.random.uniform(scale_key, (2, D), dtype=jnp.float32, minval=math.log(0.5), maxval=math.log(2.0)))
    stacked = jnp.stack([gains[0], shifts[0], shifts[1], scales[0], gains[1], shifts[2], shifts[3], scales[1]])
    return stacked.astype(jnp.float32)


def levels(own_key, shape, shards, low, largest):
    def one(axis_at, parts):
        draws = jax.random.uniform(jax.random.fold_in(jax.random.fold_in(own_key, 6), axis_at), (parts,), jnp.float32, low / len(shards), largest / len(shards))
        return jnp.repeat(jnp.exp(draws), shape[axis_at] // parts).reshape((-1,) + (1,) * (len(shape) - axis_at - 1))

    loudness = one(*shards[0])
    for cut in shards[1:]:
        loudness = loudness * one(*cut)
    return loudness


def normal_values(rng, dims, width, most, pieces=(), kind=jnp.bfloat16):
    entries = jax.random.normal(rng, dims, jnp.float32) * width
    if len(pieces) > 0:
        entries = levels(rng, dims, pieces, -0.22, 0.18) * entries
    return jnp.clip(entries, min=-most, max=most).astype(kind)


def setup_inputs(seed: int = 0) -> dict:
    key_of = jax.random.split(jax.random.key(seed), 20)
    return {
        "inputs": normal_values(key_of[0], (TOKENS, D), 1.0, 6.0, ((0, 16),)),
        "cotangent": normal_values(key_of[1], (TOKENS, D), 1.0, 6.0, ((0, 16),)),
        "w_qkv": normal_values(key_of[2], (D, 3, D), (D // 2) ** -0.5, 0.4375, ((0, 16), (2, 2)), jnp.float32),
        "w_out": normal_values(key_of[3], (D, D), (D // 16) ** -0.5, 1.25, ((0, 2), (1, 16)), jnp.float32),
        "w_up": normal_values(key_of[4], (D, FF), D ** -0.5, 0.3125, ((0, 16), (1, 2)), jnp.float32),
        "w_down": normal_values(key_of[5], (FF, D), FF ** -0.5, 0.15625, ((0, 2), (1, 16)), jnp.float32),
        "vectors": draw_vectors(jax.random.fold_in(key_of[19], 71), 0),
        "head_bias": normal_values(key_of[7], (2, HEADS, HD), 0.1, 0.4, ((1, 2), (2, 16)), jnp.float32),
        "up_bias": normal_values(key_of[8], (FF // 128, 128), 0.3, 1.2, ((0, 2), (1, 16)), jnp.float32),
        "mom_qkv": normal_values(key_of[9], (D, 3, D), (1.5 * TOKENS ** 0.5), 1280.0, ((0, 16), (2, 2)), jnp.float32),
        "mom_out": normal_values(key_of[10], (D, D), (0.4 * TOKENS ** 0.5), 384.0, ((0, 2), (1, 16)), jnp.float32),
        "mom_up": normal_values(key_of[11], (D, FF), (0.35 * TOKENS ** 0.5), 320.0, ((0, 16), (1, 2)), jnp.float32),
        "mom_down": normal_values(key_of[12], (FF, D), (0.7 * TOKENS ** 0.5), 640.0, ((0, 2), (1, 16)), jnp.float32),
        "vec_first": normal_values(key_of[13], (8, D), (0.11 * TOKENS ** 0.5), 96.0, ((1, 16),), jnp.float32),
        "vec_second": jnp.clip(jnp.exp(math.log(175.36) - 2.7725887 * jax.random.uniform(key_of[14], (8, D), jnp.float32) ** levels(key_of[14], (8, D), ((1, 16),), -0.2, 0.2)), 10.96, 175.36),
        "head_first": normal_values(key_of[15], (2, HEADS, HD), (0.2 * TOKENS ** 0.5), 192.0, ((1, 2), (2, 16)), jnp.float32),
        "head_second": jnp.clip(jnp.exp(math.log(657.6) - 2.7080502 * jax.random.uniform(key_of[16], (2, HEADS, HD), jnp.float32) ** levels(key_of[16], (2, HEADS, HD), ((1, 2), (2, 16)), -0.2, 0.2)), 43.84, 657.6),
        "unit_first": normal_values(key_of[17], (FF // 128, 128), (0.035 * TOKENS ** 0.5), 32.0, ((0, 2), (1, 16)), jnp.float32),
        "unit_second": jnp.clip(jnp.exp(math.log(19.728) - 2.8903718 * jax.random.uniform(key_of[18], (FF // 128, 128), jnp.float32) ** levels(key_of[18], (FF // 128, 128), ((0, 2), (1, 16)), -0.2, 0.2)), 1.096, 19.728),
    }


@jax.custom_vjp
def low(v):
    return lax.optimization_barrier(v.astype(jnp.bfloat16)).astype(jnp.float32)

@jax.custom_vjp
def low_back(v):
    return v

def low_keep(v):
    return (low(v), None)

def low_pass(kept, grad):
    return (grad,)

def back_keep(v):
    return (v, None)

def back_low(kept, grad):
    return (low(grad),)
low.defvjp(low_keep, low_pass)
low_back.defvjp(back_keep, back_low)
COEFF_A = 3.4445
COEFF_B = -4.775
COEFF_C = 2.0315
STEP_RATES = (2.7, 4.4, 2.2, 1.1)
MOMENTUM_DECAY = 0.95
WEIGHT_KEEP = 0.999
ADAM_ONE = 0.9
ADAM_TWO = 0.999
ADAM_RATE = 0.6

def normalize(values, gain_row, shift_row):
    center = values - lax.optimization_barrier(jnp.mean(values, axis=-1, keepdims=True))
    spread = lax.optimization_barrier(jnp.mean(center * center, axis=-1, keepdims=True))
    return center * lax.rsqrt(spread + 1e-06) * gain_row + shift_row

def orthogonalize(matrix):
    is_tall = matrix.shape[0] > matrix.shape[1]
    iterate = matrix.T if is_tall else matrix
    iterate = iterate / (jnp.sqrt(jnp.sum(iterate * iterate)) + 1e-07)
    for sweep_index in range(5):
        gram_matrix = jnp.dot(iterate, iterate.T, precision=lax.Precision.HIGHEST)
        polynomial = COEFF_B * gram_matrix + COEFF_C * jnp.dot(gram_matrix, gram_matrix, precision=lax.Precision.HIGHEST)
        iterate = COEFF_A * iterate + jnp.dot(polynomial, iterate, precision=lax.Precision.HIGHEST)
    return iterate.T if is_tall else iterate

def adam_update(parameter, gradient, first, second):
    first_new = ADAM_ONE * first + (1.0 - ADAM_ONE) * gradient
    second_new = ADAM_TWO * second + (1.0 - ADAM_TWO) * gradient * gradient
    first_hat = first_new / (1.0 - ADAM_ONE ** STEP)
    second_hat = second_new / (1.0 - ADAM_TWO ** STEP)
    return (second_new, parameter - ADAM_RATE * first_hat / (jnp.sqrt(second_hat) + 1e-08))

def forward_image(params, one_image):
    w_qkv, w_out, w_up, w_down, vectors, head_bias, up_bias = params
    gain_one, shift_one, out_shift, scale_one = (vectors[0], vectors[1], vectors[2], vectors[3])
    gain_two, shift_two, down_shift, scale_two = (vectors[4], vectors[5], vectors[6], vectors[7])
    normed = low(normalize(one_image, gain_one, shift_one))
    projected = jnp.dot(normed, w_qkv.reshape(D, 3 * D), precision=lax.Precision.HIGHEST)
    queries = low_back(low(projected[:, :D] + head_bias[0].reshape(D)))
    key_rows = low_back(low(projected[:, D:2 * D]))
    values = low_back(low(projected[:, 2 * D:] + head_bias[1].reshape(D)))
    shaped = (SEQ, HEADS, HD)
    scores = low_back(jnp.einsum('qhd,khd->hqk', queries.reshape(shaped), key_rows.reshape(shaped), precision=lax.Precision.HIGHEST) * 0.125)
    probabilities = low(jax.nn.softmax(scores, axis=-1))
    attended = jnp.einsum('hqk,khd->qhd', probabilities, values.reshape(shaped), precision=lax.Precision.HIGHEST)
    attended = low_back(low(attended.reshape(SEQ, D)))
    attn_out = low_back(jnp.dot(attended, w_out, precision=lax.Precision.HIGHEST)) + out_shift
    middle = one_image + scale_one * attn_out
    normed_two = low(normalize(middle, gain_two, shift_two))
    preact = low_back(jnp.dot(normed_two, w_up, precision=lax.Precision.HIGHEST)) + up_bias.reshape(FF)
    gelu_out = low(jax.nn.gelu(preact, approximate=False))
    mlp_out = low_back(jnp.dot(gelu_out, w_down, precision=lax.Precision.HIGHEST)) + down_shift
    return middle + scale_two * mlp_out

def reference(inputs, cotangent, w_qkv, w_out, w_up, w_down, vectors, head_bias, up_bias, mom_qkv, mom_out, mom_up, mom_down, vec_first, vec_second, head_first, head_second, unit_first, unit_second):
    images = inputs.astype(jnp.float32).reshape(TOKENS // SEQ, SEQ, D)

    def forward(image_rows, *params):
        rounded = tuple((low(parameter) for parameter in params))
        step_fn = jax.checkpoint(partial(forward_image, rounded))
        return lax.map(step_fn, image_rows)
    params = (w_qkv, w_out, w_up, w_down, vectors, head_bias, up_bias)
    outputs, pullback = jax.vjp(forward, images, *params)
    gradients = pullback(cotangent.astype(jnp.float32).reshape(images.shape))
    output = outputs.reshape(TOKENS, D).astype(jnp.bfloat16)
    grad_in = gradients[0].reshape(TOKENS, D).astype(jnp.bfloat16)
    weight_grads = gradients[1:5]
    moments = []
    new_weights = []
    for weight, moment_old, gradient, step_rate in zip(params[:4], (mom_qkv, mom_out, mom_up, mom_down), weight_grads, STEP_RATES):
        moment = MOMENTUM_DECAY * moment_old + gradient
        orthogonal = orthogonalize(moment.reshape(moment.shape[0], -1)).reshape(moment.shape)
        moments.append(moment)
        new_weights.append(WEIGHT_KEEP * weight - step_rate * orthogonal)
    vec_second_new, vec_new = adam_update(vectors, gradients[5], vec_first, vec_second)
    head_second_new, head_new = adam_update(head_bias, gradients[6], head_first, head_second)
    unit_second_new, unit_new = adam_update(up_bias, gradients[7], unit_first, unit_second)
    return (output, grad_in, weight_grads[0], weight_grads[1], weight_grads[2], weight_grads[3], moments[0], moments[1], moments[2], moments[3], new_weights[0], new_weights[1], new_weights[2], new_weights[3], gradients[5], vec_second_new, vec_new, gradients[6], head_second_new, head_new, gradients[7], unit_second_new, unit_new)
```

```python
from functools import partial

import jax
import jax.numpy as jnp
from jax import lax
from jax.experimental import pallas as pl
from jax.experimental.pallas import tpu as pltpu
from jax.sharding import PartitionSpec as P

HD = 64
SEQ = 1370
STEP = 10
PAD = 1408
HALF = 704
BLOCK = 352
MASKED = -1e30
LANES = 128

COEFF_A = 3.4445
COEFF_B = -4.775
COEFF_C = 2.0315
STEP_RATES = (2.7, 4.4, 2.2, 1.1)
MOMENTUM_DECAY = 0.95
WEIGHT_KEEP = 0.999
ADAM_ONE = 0.9
ADAM_TWO = 0.999
ADAM_RATE = 0.6
AXES = ("dp", "tensor")
F32 = jnp.float32
BF16 = jnp.bfloat16
NT = (((1,), (1,)), ((), ()))
TN = (((0,), (0,)), ((), ()))
VMEM_LIMIT = 56 * 1024 * 1024


def params():
    return pltpu.CompilerParams(vmem_limit_bytes=VMEM_LIMIT)


def dot(a, b, dims=(((1,), (0,)), ((), ()))):
    return lax.dot_general(a, b, dims, preferred_element_type=F32)


def normalize(values, gain_row, shift_row):
    center = values - jnp.mean(values, axis=-1, keepdims=True)
    spread = jnp.mean(center * center, axis=-1, keepdims=True)
    return center * lax.rsqrt(spread + 1e-06) * gain_row + shift_row


def adam_update(parameter, gradient, first, second):
    first_new = ADAM_ONE * first + (1.0 - ADAM_ONE) * gradient
    second_new = ADAM_TWO * second + (1.0 - ADAM_TWO) * gradient * gradient
    first_hat = first_new / (1.0 - ADAM_ONE**STEP)
    second_hat = second_new / (1.0 - ADAM_TWO**STEP)
    return (second_new, parameter - ADAM_RATE * first_hat / (jnp.sqrt(second_hat) + 1e-08))


def three_pieces(column):
    high = column.astype(BF16)
    rest = column - high.astype(F32)
    middle = rest.astype(BF16)
    low = (rest - middle.astype(F32)).astype(BF16)
    return high.astype(F32), middle.astype(F32), low.astype(F32)


def lanes_of(rows):
    return lax.broadcasted_iota(jnp.int32, (rows, HD), 1)


def with_column(extra, rows):
    lane = lanes_of(rows)
    high, middle, low = three_pieces(extra)
    return jnp.where(lane == 1, high, jnp.where(lane == 2, middle, jnp.where(lane == 3, low, 0.0)))


def qkv_kernel(x_ref, w_ref, vec_ref, bias_ref, q_ref, k_ref, v_ref):
    heads = q_ref.shape[0]
    width = heads * HD
    rows = x_ref.shape[0]
    normed = normalize(x_ref[...].astype(F32), vec_ref[0:1, :], vec_ref[1:2, :]).astype(BF16)
    projected = dot(normed, w_ref[...])
    lane = lanes_of(rows)
    token = pl.program_id(0) * rows + lax.broadcasted_iota(jnp.int32, (rows, HD), 0)
    one = jnp.where(lane == 0, 1.0, 0.0)
    pieces = jnp.where((lane >= 1) & (lane <= 3), 1.0, 0.0)
    mask = jnp.where((lane == 0) & (token >= SEQ), MASKED, pieces)
    for head in range(heads):
        at = head * HD
        query = projected[:, at : at + HD] + bias_ref[0:1, at : at + HD]
        key = projected[:, width + at : width + at + HD]
        value = projected[:, 2 * width + at : 2 * width + at + HD] + bias_ref[1:2, at : at + HD]
        query = query.astype(BF16).astype(F32) * 0.125
        q_ref[head] = jnp.concatenate([query, one], axis=1).astype(BF16)
        k_ref[head] = jnp.concatenate([key, mask], axis=1).astype(BF16)
        v_ref[head] = jnp.concatenate([value, one + pieces], axis=1).astype(BF16)


def qkv_call(x, weights, vectors, bias):
    heads = weights.shape[1] // (3 * HD)
    whole = lambda shape: pl.BlockSpec(shape, lambda i: (0,) * len(shape))
    out = jax.ShapeDtypeStruct((heads, PAD, LANES), BF16)
    spec = pl.BlockSpec((heads, BLOCK, LANES), lambda i: (0, i, 0))
    return pl.pallas_call(
        qkv_kernel,
        grid=(PAD // BLOCK,),
        in_specs=[
            pl.BlockSpec((BLOCK, x.shape[1]), lambda i: (i, 0)),
            whole(weights.shape),
            whole(vectors.shape),
            whole(bias.shape),
        ],
        out_specs=[spec] * 3,
        out_shape=[out] * 3,
        compiler_params=params(),
        name="qkv",
    )(x, weights, vectors, bias)


def attend_kernel(q_ref, k_ref, v_ref, att_ref, qs_ref):
    heads, rows, _ = q_ref.shape
    parts = []
    for head in range(heads):
        query = q_ref[head]
        scores = dot(query, k_ref[head], NT)
        largest = jnp.max(scores, axis=-1, keepdims=True)
        exponent = jnp.exp(scores - largest).astype(BF16)
        total = dot(exponent, v_ref[head])
        denominator = total[:, HD : HD + 1]
        parts.append((total[:, :HD] / denominator).astype(BF16))
        logsum = largest + jnp.log(denominator)
        extra = with_column(-logsum, rows)
        lane = lanes_of(rows)
        extra = jnp.where(lane == 0, 1.0, extra)
        qs_ref[head] = jnp.concatenate([query[:, :HD].astype(F32), extra], axis=1).astype(BF16)
    att_ref[...] = jnp.concatenate(parts, axis=1)


def attend_call(q, k, v):
    heads = q.shape[0]
    blocked = pl.BlockSpec((heads, BLOCK, LANES), lambda i: (0, i, 0))
    whole = pl.BlockSpec((heads, PAD, LANES), lambda i: (0, 0, 0))
    return pl.pallas_call(
        attend_kernel,
        grid=(PAD // BLOCK,),
        in_specs=[blocked, whole, whole],
        out_specs=[pl.BlockSpec((BLOCK, heads * HD), lambda i: (i, 0)), blocked],
        out_shape=[
            jax.ShapeDtypeStruct((PAD, heads * HD), BF16),
            jax.ShapeDtypeStruct((heads, PAD, LANES), BF16),
        ],
        compiler_params=params(),
        cost_estimate=pl.CostEstimate(
            flops=heads * 4 * PAD * PAD * LANES * 4, bytes_accessed=8 * PAD * LANES * heads, transcendentals=0
        ),
        name="attend",
    )(q, k, v)


def attend_back_kernel(q_ref, k_ref, v_ref, att_ref, up_ref, dq_ref, dk_ref, dv_ref, upstream, total):
    heads = q_ref.shape[0]
    rows = k_ref.shape[1]
    step = pl.program_id(0)

    @pl.when(step == 0)
    def _():
        for head in range(heads):
            at = head * HD
            grad = up_ref[:, at : at + HD].astype(F32)
            dots = jnp.sum(grad * att_ref[:, at : at + HD].astype(F32), axis=1, keepdims=True)
            upstream[head] = jnp.concatenate([grad, with_column(-dots, PAD)], axis=1).astype(BF16)
        total[...] = jnp.zeros_like(total)

    key_parts, value_parts = [], []
    for head in range(heads):
        query, grad = q_ref[head], upstream[head]
        key, value = k_ref[head], v_ref[head]
        weight = jnp.exp(dot(key, query, NT))
        value_parts.append(dot(weight.astype(BF16), grad)[:, :HD].astype(BF16))
        score = (weight * dot(value, grad, NT)).astype(BF16)
        key_parts.append(dot(score, query)[:, :HD].astype(BF16))
        total[head] += dot(key, score, TN)
    dk_ref[...] = jnp.concatenate(key_parts, axis=1)
    dv_ref[...] = jnp.concatenate(value_parts, axis=1)

    @pl.when(step == pl.num_programs(0) - 1)
    def _():
        dq_ref[...] = jnp.concatenate(
            [(total[head][:HD, :] * 0.125).T.astype(BF16) for head in range(heads)], axis=1
        )


def attend_back_call(qs, k, v, attended, upstream):
    heads = qs.shape[0]
    width = heads * HD
    blocked = pl.BlockSpec((heads, BLOCK, LANES), lambda i: (0, i, 0))
    whole = pl.BlockSpec((heads, PAD, LANES), lambda i: (0, 0, 0))
    flat = pl.BlockSpec((PAD, width), lambda i: (0, 0))
    rows = pl.BlockSpec((BLOCK, width), lambda i: (i, 0))
    out = jax.ShapeDtypeStruct((PAD, width), BF16)
    return pl.pallas_call(
        attend_back_kernel,
        grid=(PAD // BLOCK,),
        in_specs=[whole, blocked, blocked, flat, flat],
        out_specs=[flat, rows, rows],
        out_shape=[out] * 3,
        scratch_shapes=[pltpu.VMEM((heads, PAD, LANES), BF16), pltpu.VMEM((heads, LANES, PAD), F32)],
        compiler_params=params(),
        cost_estimate=pl.CostEstimate(
            flops=heads * 10 * PAD * PAD * LANES * 4, bytes_accessed=8 * PAD * LANES * heads, transcendentals=0
        ),
        name="attend_back",
    )(qs, k, v, attended, upstream)


def split_two(value):
    high = value.astype(BF16)
    return high, (value - high.astype(F32)).astype(BF16)


def dot_three(a, b):
    (a_high, a_low), (b_high, b_low) = a, b
    return dot(a_high, b_high) + (dot(a_high, b_low) + dot(a_low, b_high))


def ortho_kernel(m_ref, o_ref):
    halves, size, _ = m_ref.shape
    gram = sum(dot(m_ref[t], m_ref[t], NT) for t in range(halves))
    row = lax.broadcasted_iota(jnp.int32, (size, size), 0)
    column = lax.broadcasted_iota(jnp.int32, (size, size), 1)
    eye = row == column
    square = jnp.sum(jnp.where(eye, gram, 0.0), axis=(0, 1), keepdims=True)
    scale = 1.0 / (jnp.sqrt(square) + 1e-07)
    gram = gram * scale * scale
    product = None
    for sweep_index in range(5):
        parts = split_two(gram)
        poly = COEFF_B * gram + COEFF_C * dot_three(parts, parts)
        poly = jnp.where(eye, poly + COEFF_A, poly)
        poly_parts = split_two(poly)
        product = poly if product is None else dot_three(poly_parts, split_two(product))
        if sweep_index < 4:
            gram = dot_three(poly_parts, split_two(dot_three(parts, poly_parts)))
    high, low = split_two(product * scale)
    for t in range(halves):
        o_ref[t] = (dot(high, m_ref[t]) + dot(low, m_ref[t])).astype(BF16)


def ortho_call(matrix):
    return pl.pallas_call(
        ortho_kernel,
        out_shape=jax.ShapeDtypeStruct(matrix.shape, BF16),
        compiler_params=params(),
        name="ortho",
    )(matrix)


def bit_of(bit):
    index = lax.axis_index(AXES)
    return (index >> bit) & 1


def swap(value, bit, count):
    return lax.ppermute(value, AXES, [(i, i ^ (1 << bit)) for i in range(count)])


def is_home(i):
    return (i & 1) == ((i >> 1) & 1)


def home_send(value, bit, count):
    return lax.ppermute(value, AXES, [(i, i ^ (1 << bit)) for i in range(count) if is_home(i)])


def gather_tree(shard, count):
    bits = count.bit_length() - 1
    value = shard.reshape((1,) * bits + shard.shape)
    order = [*range(bits - 1, 1, -1), 0, 1]
    for bit in order:
        other = swap(value, bit, count)
        axis = bits - 1 - bit
        mine = bit_of(bit) == 0
        value = jnp.concatenate(
            [jnp.where(mine, value, other), jnp.where(mine, other, value)], axis=axis
        )
    return value.reshape((count,) + shard.shape)


def scatter_tree(value, count):
    bits = count.bit_length() - 1
    shape = value.shape[1:]
    value = value.reshape((2,) * bits + shape)
    order = [1, 0, *range(2, bits)]
    for bit in order:
        axis = bits - 1 - bit
        first = lax.slice_in_dim(value, 0, 1, axis=axis)
        second = lax.slice_in_dim(value, 1, 2, axis=axis)
        mine = bit_of(bit) == 0
        sent = jnp.where(mine, second, first).astype(BF16)
        kept = jnp.where(mine, first, second)
        value = kept.astype(F32) + swap(sent, bit, count).astype(F32)
        if bit != order[-1]:
            value = value.astype(BF16)
    return value.reshape(shape)


def shards(
    inputs,
    cotangent,
    w_qkv,
    w_out,
    w_up,
    w_down,
    vectors,
    head_bias,
    up_bias,
    mom_qkv,
    mom_out,
    mom_up,
    mom_down,
    vec_first,
    vec_second,
    head_first,
    head_second,
    unit_first,
    unit_second,
):
    dp = lax.axis_size("dp")
    tensor = lax.axis_size("tensor")
    count = dp * tensor
    model = inputs.shape[1]
    rows = w_qkv.shape[0]
    third = w_qkv.shape[2]
    qkv_width = 3 * third
    packed_width = -(-(qkv_width + 11) // LANES) * LANES
    up_width = w_up.shape[1]
    out_width = w_out.shape[0]
    group_width = up_width
    core = lax.axis_index("dp") & 1
    home = core == lax.axis_index("tensor")
    core_first = core == 0

    small = jnp.concatenate(
        [vectors.T, head_bias.reshape(rows, 1), up_bias.reshape(rows, 2)], axis=1
    )
    first = jnp.concatenate(
        [
            w_qkv.reshape(rows, qkv_width).astype(BF16),
            jnp.pad(small.astype(BF16), ((0, 0), (0, packed_width - qkv_width - 11))),
        ],
        axis=1,
    )
    first_all = lax.all_to_all(
        jnp.broadcast_to(first[None], (count,) + first.shape), AXES, 0, 0
    ).reshape(dp, tensor, rows, packed_width)
    later = jnp.concatenate(
        [w_up.astype(BF16), w_down.T.astype(BF16), w_out.T.astype(BF16)], axis=1
    )
    later_width = later.shape[1]

    other_inputs = home_send(inputs, 1, count)
    image = jnp.pad(jnp.where(home, inputs, other_inputs), ((0, PAD - SEQ), (0, 0)))
    other_cotangent = home_send(cotangent, 1, count)
    image_cotangent = jnp.pad(
        jnp.where(home, cotangent, other_cotangent), ((0, PAD - SEQ), (0, 0))
    )
    later_all = (
        gather_tree(later, count)
        .reshape(dp, tensor, rows, later_width)
        .transpose(1, 0, 2, 3)
        .reshape(tensor, model, later_width)
    )

    qkv_all = first_all[..., :qkv_width].transpose(1, 0, 2, 3).reshape(tensor, model, qkv_width)
    qkv_mine = jnp.where(core_first, qkv_all[0], qkv_all[1])
    vec_full = first_all[:, 0, :, qkv_width : qkv_width + 8].reshape(model, 8).T.astype(F32)
    head_mine = first_all[..., qkv_width + 8]
    head_mine = jnp.where(core_first, head_mine[:, 0], head_mine[:, 1])
    head_mine = (
        head_mine.reshape((dp,) + head_bias.shape)
        .transpose(1, 2, 0, 3)
        .reshape(2, third)
        .astype(F32)
    )
    unit_shift = (
        first_all[..., qkv_width + 9 : qkv_width + 11]
        .reshape((dp, tensor) + up_bias.shape)
        .transpose(1, 2, 0, 3)
        .reshape(tensor, up_width)
        .astype(F32)
    )
    gain_one, shift_one, out_shift, scale_one = (vec_full[0], vec_full[1], vec_full[2], vec_full[3])
    gain_two, shift_two, down_shift, scale_two = (
        vec_full[4],
        vec_full[5],
        vec_full[6],
        vec_full[7],
    )

    q, k, v = qkv_call(image, qkv_mine, vec_full, head_mine)
    attended, qs = attend_call(q, k, v)

    def own_rows(value):
        return jnp.where(core_first, value[:HALF], value[HALF:])

    def other_rows(value):
        return jnp.where(core_first, value[HALF:], value[:HALF])

    def in_order(mine, other):
        return jnp.where(core_first, mine, other), jnp.where(core_first, other, mine)

    def to_tokens(value):
        return in_order(own_rows(value), swap(other_rows(value), 1, count))

    def to_heads(parts):
        mine = jnp.where(core_first, parts[0], parts[1])
        other = jnp.where(core_first, parts[1], parts[0])
        return jnp.concatenate(in_order(mine, swap(other, 1, count)), axis=0)

    attended_rows = jnp.concatenate(to_tokens(attended), axis=1)

    up_halves = later_all[:, :, :up_width]
    down_halves = later_all[:, :, up_width : 2 * up_width]
    out_halves = later_all[:, :, 2 * up_width :]
    up_matrix = jnp.concatenate([up_halves[0], up_halves[1]], axis=1)
    down_matrix = jnp.concatenate([down_halves[0], down_halves[1]], axis=1)
    out_matrix = jnp.concatenate([out_halves[0], out_halves[1]], axis=1)
    unit_row = unit_shift.reshape(-1)

    residual = own_rows(image).astype(F32)
    incoming = own_rows(image_cotangent).astype(F32)
    attn_out = dot(attended_rows, out_matrix, NT) + out_shift
    middle = residual + scale_one * attn_out
    normed_two = normalize(middle, gain_two, shift_two).astype(BF16)
    preact = dot(normed_two, up_matrix) + unit_row
    activated, gelu_pull = jax.vjp(partial(jax.nn.gelu, approximate=False), preact)
    gelu_out = activated.astype(BF16)
    mlp_out = dot(gelu_out, down_matrix, NT) + down_shift
    output_rows = (middle + scale_two * mlp_out).astype(BF16)
    grad_scale_two = jnp.sum(incoming * mlp_out, axis=0)
    mlp_grad = scale_two * incoming
    grad_down_shift = jnp.sum(mlp_grad, axis=0)
    mlp_grad_low = mlp_grad.astype(BF16)
    grad_down = dot(mlp_grad_low, gelu_out, TN)
    gelu_grad = dot(mlp_grad_low, down_matrix)
    preact_grad = gelu_pull(gelu_grad)[0]
    grad_unit = jnp.sum(preact_grad, axis=0)
    preact_low = preact_grad.astype(BF16)
    grad_up = dot(normed_two, preact_low, TN)
    normed_two_grad = dot(preact_low, up_matrix, NT)
    norm_pull_two = jax.vjp(normalize, middle, gain_two, shift_two)[1]
    middle_back, grad_gain_two, grad_shift_two = norm_pull_two(normed_two_grad)
    middle_grad = incoming + middle_back
    grad_scale_one = jnp.sum(middle_grad * attn_out, axis=0)
    attn_grad = scale_one * middle_grad
    grad_out_shift = jnp.sum(attn_grad, axis=0)
    attn_grad_low = attn_grad.astype(BF16)
    grad_out = dot(attn_grad_low, attended_rows, TN)
    attended_grad = dot(attn_grad_low, out_matrix).astype(BF16)

    later_grad = jnp.stack(
        [
            jnp.concatenate(
                [
                    grad_up[:, t * up_width : (t + 1) * up_width].astype(BF16),
                    grad_down[:, t * up_width : (t + 1) * up_width].astype(BF16),
                    grad_out[:, t * out_width : (t + 1) * out_width].astype(BF16),
                ],
                axis=1,
            ).reshape(dp, rows, later_width)
            for t in range(tensor)
        ],
        axis=1,
    ).reshape(count, rows, later_width)
    later_red = scatter_tree(later_grad, count)
    red_up = later_red[:, :up_width]
    red_down_t = later_red[:, up_width : 2 * up_width]
    red_out_t = later_red[:, 2 * up_width :]

    upstream = to_heads((attended_grad[:, :third], attended_grad[:, third:]))
    dq, dk, dv = attend_back_call(qs, k, v, attended, upstream)
    halves = to_tokens(jnp.concatenate([dq, dk, dv], axis=1))
    normed = normalize(residual, gain_one, shift_one).astype(BF16)
    grad_qkv = [dot(normed, half, TN) for half in halves]
    normed_grad = dot(halves[0], qkv_all[0], NT) + dot(halves[1], qkv_all[1], NT)
    norm_pull_one = jax.vjp(normalize, residual, gain_one, shift_one)[1]
    residual_back, grad_gain_one, grad_shift_one = norm_pull_one(normed_grad)
    grad_in_rows = (middle_grad + residual_back).astype(BF16)
    head_sums = [jnp.sum(half.astype(F32), axis=0) for half in halves]
    grad_heads = jnp.stack(
        [jnp.stack([sums[:third], sums[2 * third :]]) for sums in head_sums]
    )
    grad_vectors = jnp.stack(
        [
            grad_gain_one,
            grad_shift_one,
            grad_out_shift,
            grad_scale_one,
            grad_gain_two,
            grad_shift_two,
            grad_down_shift,
            grad_scale_two,
        ]
    )
    vec_part = jnp.broadcast_to(grad_vectors.T.reshape(dp, 1, rows, 8), (dp, tensor, rows, 8))
    head_part = (
        grad_heads.reshape(tensor, 2, third // HD, dp, HD // dp)
        .transpose(3, 0, 1, 2, 4)
        .reshape(dp, tensor, rows, 1)
    )
    unit_part = (
        grad_unit.reshape(tensor, up_bias.shape[0], dp, up_bias.shape[1])
        .transpose(2, 0, 1, 3)
        .reshape(dp, tensor, rows, 2)
    )
    qkv_part = jnp.stack([half.reshape(dp, rows, qkv_width) for half in grad_qkv], axis=1)
    first_grad = jnp.concatenate(
        [
            qkv_part.astype(BF16),
            jnp.pad(
                jnp.concatenate([vec_part, head_part, unit_part], axis=3).astype(BF16),
                ((0, 0), (0, 0), (0, 0), (0, packed_width - qkv_width - 11)),
            ),
        ],
        axis=3,
    ).reshape(count, rows, packed_width)
    first_red = jnp.sum(lax.all_to_all(first_grad, AXES, 0, 0).astype(F32), axis=0)
    red_qkv = first_red[:, :qkv_width].reshape(w_qkv.shape)
    red_vec = first_red[:, qkv_width : qkv_width + 8].T
    red_head = first_red[:, qkv_width + 8].reshape(head_bias.shape)
    red_unit = first_red[:, qkv_width + 9 : qkv_width + 11].reshape(up_bias.shape)

    red_out, red_down = red_out_t.T, red_down_t.T
    moment_qkv = MOMENTUM_DECAY * mom_qkv + red_qkv
    moment_out = MOMENTUM_DECAY * mom_out + red_out
    moment_up = MOMENTUM_DECAY * mom_up + red_up
    moment_down = MOMENTUM_DECAY * mom_down + red_down

    def widen(value):
        return jnp.pad(value.astype(BF16), ((0, 0), (0, group_width - value.shape[1])))

    chunks = jnp.stack(
        [
            widen(moment_up),
            widen(moment_down.T),
            widen(moment_out.T),
            widen(moment_qkv.reshape(rows, qkv_width)),
        ]
    )
    sent = jnp.broadcast_to(chunks[None], (count // 4,) + chunks.shape)
    whole = (
        lax.all_to_all(sent.reshape(count, rows, group_width), AXES, 0, 0)
        .reshape(dp, tensor, rows, group_width)
        .transpose(1, 0, 2, 3)
        .reshape(tensor, model, group_width)
    )
    result = ortho_call(whole)
    pair = lax.dynamic_slice_in_dim(result, (lax.axis_index("dp") // 2) * 2 * rows, 2 * rows, axis=1)
    local = pair.reshape(tensor, 2, rows, group_width).transpose(1, 0, 2, 3)
    mine = lax.all_to_all(
        local.reshape(4, rows, group_width),
        AXES,
        0,
        0,
        axis_index_groups=[[4 * i + j for j in range(4)] for i in range(count // 4)],
    ).astype(F32)
    new_up = WEIGHT_KEEP * w_up - STEP_RATES[2] * mine[0]
    new_down = WEIGHT_KEEP * w_down - STEP_RATES[3] * mine[1].T
    new_out = WEIGHT_KEEP * w_out - STEP_RATES[1] * mine[2, :, :out_width].T
    new_qkv = WEIGHT_KEEP * w_qkv - STEP_RATES[0] * mine[3, :, :qkv_width].reshape(w_qkv.shape)
    vec_second_new, vec_new = adam_update(vectors, red_vec, vec_first, vec_second)
    head_second_new, head_new = adam_update(head_bias, red_head, head_first, head_second)
    unit_second_new, unit_new = adam_update(up_bias, red_unit, unit_first, unit_second)

    def to_image(value):
        full = jnp.concatenate(in_order(value, swap(value, 1, count)), axis=0)[:SEQ]
        return jnp.where(home, full, home_send(full, 0, count))

    output = to_image(output_rows)
    grad_in = to_image(grad_in_rows)
    return (
        output,
        grad_in,
        red_qkv,
        red_out,
        red_up,
        red_down,
        moment_qkv,
        moment_out,
        moment_up,
        moment_down,
        new_qkv,
        new_out,
        new_up,
        new_down,
        red_vec,
        vec_second_new,
        vec_new,
        red_head,
        head_second_new,
        head_new,
        red_unit,
        unit_second_new,
        unit_new,
    )


def solution(mesh):
    token = P("dp", None)
    specs = (
        P("dp", None, "tensor"),
        P("tensor", "dp"),
        P("dp", "tensor"),
        P("tensor", "dp"),
    )
    vec, head, unit = P(None, "dp"), P(None, "tensor", "dp"), P("tensor", "dp")
    return jax.shard_map(
        shards,
        mesh=mesh,
        in_specs=(token, token)
        + specs
        + (vec, head, unit)
        + specs
        + (vec, vec, head, head, unit, unit),
        out_specs=(token, token) + specs * 3 + (vec,) * 3 + (head,) * 3 + (unit,) * 3,
        check_vma=False,
    )
```

```python
from functools import partial

import jax
import jax.numpy as jnp
from jax import lax
from jax.experimental import pallas as pl
from jax.experimental.pallas import tpu as pltpu
from jax.sharding import PartitionSpec as P

HD = 64
SEQ = 1370
STEP = 10
PAD = 1408
HALF = 704
BLOCK = 352
MASKED = -1e30
LANES = 128

COEFF_A = 3.4445
COEFF_B = -4.775
COEFF_C = 2.0315
STEP_RATES = (2.7, 4.4, 2.2, 1.1)
MOMENTUM_DECAY = 0.95
WEIGHT_KEEP = 0.999
ADAM_ONE = 0.9
ADAM_TWO = 0.999
ADAM_RATE = 0.6
AXES = ("dp", "tensor")
F32 = jnp.float32
BF16 = jnp.bfloat16
NT = (((1,), (1,)), ((), ()))
TN = (((0,), (0,)), ((), ()))
VMEM_LIMIT = 56 * 1024 * 1024


def params():
    return pltpu.CompilerParams(vmem_limit_bytes=VMEM_LIMIT)


def dot(a, b, dims=(((1,), (0,)), ((), ()))):
    return lax.dot_general(a, b, dims, preferred_element_type=F32)


def normalize(values, gain_row, shift_row):
    center = values - jnp.mean(values, axis=-1, keepdims=True)
    spread = jnp.mean(center * center, axis=-1, keepdims=True)
    return center * lax.rsqrt(spread + 1e-06) * gain_row + shift_row


def adam_update(parameter, gradient, first, second):
    first_new = ADAM_ONE * first + (1.0 - ADAM_ONE) * gradient
    second_new = ADAM_TWO * second + (1.0 - ADAM_TWO) * gradient * gradient
    first_hat = first_new / (1.0 - ADAM_ONE**STEP)
    second_hat = second_new / (1.0 - ADAM_TWO**STEP)
    return (second_new, parameter - ADAM_RATE * first_hat / (jnp.sqrt(second_hat) + 1e-08))


def three_pieces(column):
    high = column.astype(BF16)
    rest = column - high.astype(F32)
    middle = rest.astype(BF16)
    low = (rest - middle.astype(F32)).astype(BF16)
    return high.astype(F32), middle.astype(F32), low.astype(F32)


def lanes_of(rows):
    return lax.broadcasted_iota(jnp.int32, (rows, HD), 1)


def with_column(extra, rows):
    lane = lanes_of(rows)
    high, middle, low = three_pieces(extra)
    return jnp.where(lane == 1, high, jnp.where(lane == 2, middle, jnp.where(lane == 3, low, 0.0)))


def whole_spec(shape):
    return pl.BlockSpec(shape, lambda *_: (0,) * len(shape))


def qkv_kernel(core_ref, x_ref, w_ref, vec_ref, bias_ref, q_ref, k_ref, v_ref):
    heads = q_ref.shape[0]
    width = heads * HD
    rows = x_ref.shape[0]
    normed = normalize(x_ref[...].astype(F32), vec_ref[0:1, :], vec_ref[1:2, :]).astype(BF16)
    projected = dot(normed, w_ref[0, :, : 3 * width])
    lane = lanes_of(rows)
    token = pl.program_id(0) * rows + lax.broadcasted_iota(jnp.int32, (rows, HD), 0)
    token = token + core_ref[0] * HALF
    token = jnp.where(token >= PAD, token - PAD, token)
    one = jnp.where(lane == 0, 1.0, 0.0)
    pieces = jnp.where((lane >= 1) & (lane <= 3), 1.0, 0.0)
    mask = jnp.where((lane == 0) & (token >= SEQ), MASKED, pieces)
    for head in range(heads):
        at = head * HD
        query = projected[:, at : at + HD] + bias_ref[0, 0:1, at : at + HD]
        key = projected[:, width + at : width + at + HD]
        value = projected[:, 2 * width + at : 2 * width + at + HD] + bias_ref[0, 1:2, at : at + HD]
        query = query.astype(BF16).astype(F32) * 0.125
        q_ref[head] = jnp.concatenate([query, one], axis=1).astype(BF16)
        k_ref[head] = jnp.concatenate([key, mask], axis=1).astype(BF16)
        v_ref[head] = jnp.concatenate([value, one + pieces], axis=1).astype(BF16)


def qkv_call(core, x, weights, vectors, bias):
    heads = bias.shape[2] // HD
    out = jax.ShapeDtypeStruct((heads, PAD, LANES), BF16)
    spec = pl.BlockSpec((heads, BLOCK, LANES), lambda i, core: (0, i, 0))
    return pl.pallas_call(
        qkv_kernel,
        grid_spec=pltpu.PrefetchScalarGridSpec(
            num_scalar_prefetch=1,
            grid=(PAD // BLOCK,),
            in_specs=[
                pl.BlockSpec((BLOCK, x.shape[1]), lambda i, core: (i, 0)),
                pl.BlockSpec((1,) + weights.shape[1:], lambda i, core: (core[0], 0, 0)),
                whole_spec(vectors.shape),
                pl.BlockSpec((1,) + bias.shape[1:], lambda i, core: (core[0], 0, 0)),
            ],
            out_specs=[spec] * 3,
        ),
        out_shape=[out] * 3,
        compiler_params=params(),
        name="qkv",
    )(core, x, weights, vectors, bias)


def attend_kernel(q_ref, k_ref, v_ref, att_ref, qs_ref):
    heads, rows, _ = q_ref.shape
    parts = []
    for head in range(heads):
        query = q_ref[head]
        scores = dot(query, k_ref[head], NT)
        largest = jnp.max(scores, axis=-1, keepdims=True)
        exponent = jnp.exp(scores - largest).astype(BF16)
        total = dot(exponent, v_ref[head])
        denominator = total[:, HD : HD + 1]
        parts.append((total[:, :HD] / denominator).astype(BF16))
        logsum = largest + jnp.log(denominator)
        extra = with_column(-logsum, rows)
        lane = lanes_of(rows)
        extra = jnp.where(lane == 0, 1.0, extra)
        qs_ref[head] = jnp.concatenate([query[:, :HD].astype(F32), extra], axis=1).astype(BF16)
    att_ref[...] = jnp.concatenate(parts, axis=1)


def attend_call(q, k, v, half):
    heads = q.shape[0]
    steps = HALF // BLOCK
    whole = pl.BlockSpec((heads, PAD, LANES), lambda i: (0, 0, 0))
    return pl.pallas_call(
        attend_kernel,
        grid=(steps,),
        in_specs=[
            pl.BlockSpec((heads, BLOCK, LANES), lambda i: (0, i + half * steps, 0)),
            whole,
            whole,
        ],
        out_specs=[
            pl.BlockSpec((BLOCK, heads * HD), lambda i: (i, 0)),
            pl.BlockSpec((heads, BLOCK, LANES), lambda i: (0, i, 0)),
        ],
        out_shape=[
            jax.ShapeDtypeStruct((HALF, heads * HD), BF16),
            jax.ShapeDtypeStruct((heads, HALF, LANES), BF16),
        ],
        compiler_params=params(),
        cost_estimate=pl.CostEstimate(
            flops=heads * 4 * HALF * PAD * LANES * 4, bytes_accessed=8 * PAD * LANES * heads, transcendentals=0
        ),
        name="attend",
    )(q, k, v)


def attend_back_kernel(
    qa_ref, qb_ref, k_ref, v_ref, atta_ref, attb_ref, upa_ref, upb_ref, out_ref, queries, upstream, total
):
    heads = k_ref.shape[0]
    rows = k_ref.shape[1]
    width = heads * HD
    step = pl.program_id(0)

    @pl.when(step == 0)
    def _():
        for at, q_ref, att_ref, up_ref in ((0, qa_ref, atta_ref, upa_ref), (HALF, qb_ref, attb_ref, upb_ref)):
            for head in range(heads):
                lanes = slice(head * HD, head * HD + HD)
                grad = up_ref[:, lanes].astype(F32)
                dots = jnp.sum(grad * att_ref[:, lanes].astype(F32), axis=1, keepdims=True)
                upstream[head, at : at + HALF, :] = jnp.concatenate(
                    [grad, with_column(-dots, HALF)], axis=1
                ).astype(BF16)
                queries[head, at : at + HALF, :] = q_ref[head]
        total[...] = jnp.zeros_like(total)

    key_parts, value_parts = [], []
    for head in range(heads):
        query, grad = queries[head], upstream[head]
        key, value = k_ref[head], v_ref[head]
        weight = jnp.exp(dot(key, query, NT))
        value_parts.append(dot(weight.astype(BF16), grad)[:, :HD].astype(BF16))
        score = (weight * dot(value, grad, NT)).astype(BF16)
        key_parts.append(dot(score, query)[:, :HD].astype(BF16))
        total[head] += dot(key, score, TN)
    out_ref[pl.ds(step * rows, rows), width:] = jnp.concatenate(key_parts + value_parts, axis=1)

    @pl.when(step == pl.num_programs(0) - 1)
    def _():
        out_ref[:, :width] = jnp.concatenate(
            [(total[head][:HD, :] * 0.125).T.astype(BF16) for head in range(heads)], axis=1
        )


def attend_back_call(qs, k, v, attended, upstream):
    heads = k.shape[0]
    width = heads * HD
    blocked = pl.BlockSpec((heads, BLOCK, LANES), lambda i: (0, i, 0))
    q_spec = whole_spec((heads, HALF, LANES))
    flat = whole_spec((HALF, width))
    return pl.pallas_call(
        attend_back_kernel,
        grid=(PAD // BLOCK,),
        in_specs=[q_spec, q_spec, blocked, blocked, flat, flat, flat, flat],
        out_specs=whole_spec((PAD, 3 * width)),
        out_shape=jax.ShapeDtypeStruct((PAD, 3 * width), BF16),
        scratch_shapes=[
            pltpu.VMEM((heads, PAD, LANES), BF16),
            pltpu.VMEM((heads, PAD, LANES), BF16),
            pltpu.VMEM((heads, LANES, PAD), F32),
        ],
        compiler_params=params(),
        cost_estimate=pl.CostEstimate(
            flops=heads * 10 * PAD * PAD * LANES * 4, bytes_accessed=8 * PAD * LANES * heads, transcendentals=0
        ),
        name="attend_back",
    )(*qs, k, v, *attended, *upstream)


ERF_SCALE = 0.3275911
ERF_TERMS = (0.254829592, -0.284496736, 1.421413741, -1.453152027, 1.061405429)


def gelu_both(x):
    size = jnp.abs(x) * (0.5**0.5)
    bell = jnp.exp(-0.5 * x * x)
    t = 1.0 / (1.0 + ERF_SCALE * size)
    poly = t * ERF_TERMS[4] + ERF_TERMS[3]
    for term in ERF_TERMS[2::-1]:
        poly = poly * t + term
    tail = (0.5 * t) * poly * bell
    cumulative = jnp.where(x < 0, tail, 1.0 - tail)
    return x * cumulative, cumulative + x * (bell * 0.3989422804014327)


def norm_stats(values):
    center = values - jnp.mean(values, axis=-1, keepdims=True)
    inverse = lax.rsqrt(jnp.mean(center * center, axis=-1, keepdims=True) + 1e-06)
    return center * inverse, inverse


def norm_back(grad, unit, inverse, gain):
    u = gain * grad
    return inverse * (
        u - jnp.mean(u, axis=-1, keepdims=True) - unit * jnp.mean(u * unit, axis=-1, keepdims=True)
    )


def row_sum(value):
    return jnp.sum(value, axis=0, keepdims=True)


def write_wire(core_ref, totals, keep_ref, send_ref, shard_rows):
    even = core_ref[0] == 0
    for chip in range(keep_ref.shape[0]):
        at = chip * 2 * shard_rows
        for t in range(len(totals)):
            low = totals[t][at : at + shard_rows, :]
            high = totals[t][at + shard_rows : at + 2 * shard_rows, :]
            width = low.shape[1]
            keep_ref[chip, t, :, :width] = jnp.where(even, low, high).astype(BF16)
            send_ref[chip, t, :, :width] = jnp.where(even, high, low).astype(BF16)


def middle_kernel(
    core_ref, x_ref, cot_ref, mine_ref, recv_ref, w_ref, vec_ref, unit_ref,
    out_ref, grad_ref, up_mine_ref, up_send_ref, keep_ref, send_ref, sums_ref, unit_sums_ref,
    total,
):
    step = pl.program_id(0)
    even = core_ref[0] == 0
    wide = unit_ref.shape[1]
    shard_rows = keep_ref.shape[2]

    @pl.when(step == 0)
    def _():
        total[...] = jnp.zeros_like(total)
        sums_ref[...] = jnp.zeros_like(sums_ref)
        unit_sums_ref[...] = jnp.zeros_like(unit_sums_ref)

    vec = vec_ref[...]
    out_shift, scale_one, gain_two = vec[2:3], vec[3:4], vec[4:5]
    shift_two, down_shift, scale_two = vec[5:6], vec[6:7], vec[7:8]
    mine, recv = mine_ref[...].astype(F32), recv_ref[...].astype(F32)
    attended = [
        jnp.where(even, mine, recv).astype(BF16),
        jnp.where(even, recv, mine).astype(BF16),
    ]
    attn_out = sum(dot(attended[t], w_ref[t, :, 2 * wide :], NT) for t in range(2)) + out_shift
    middle = x_ref[...].astype(F32) + scale_one * attn_out
    unit, inverse = norm_stats(middle)
    normed = (unit * gain_two + shift_two).astype(BF16)
    incoming = cot_ref[...].astype(F32)
    mlp_grad = scale_two * incoming
    mlp_grad_low = mlp_grad.astype(BF16)
    mlp_out = down_shift
    normed_grad = 0.0
    for t in range(2):
        preact = dot(normed, w_ref[t, :, :wide]) + unit_ref[t : t + 1, :]
        activated, slope = gelu_both(preact)
        activated = activated.astype(BF16)
        mlp_out = mlp_out + dot(activated, w_ref[t, :, wide : 2 * wide], NT)
        preact_grad = dot(mlp_grad_low, w_ref[t, :, wide : 2 * wide]) * slope
        unit_sums_ref[t : t + 1, :] += row_sum(preact_grad)
        preact_low = preact_grad.astype(BF16)
        normed_grad = normed_grad + dot(preact_low, w_ref[t, :, :wide], NT)
        total[t, :, :wide] += dot(normed, preact_low, TN)
        total[t, :, wide : 2 * wide] += dot(mlp_grad_low, activated, TN)
    out_ref[...] = (middle + scale_two * mlp_out).astype(BF16)
    middle_grad = incoming + norm_back(normed_grad, unit, inverse, gain_two)
    grad_ref[...] = middle_grad
    attn_grad = scale_one * middle_grad
    attn_grad_low = attn_grad.astype(BF16)
    sums_ref[2:3, :] += row_sum(attn_grad)
    sums_ref[3:4, :] += row_sum(middle_grad * attn_out)
    sums_ref[4:5, :] += row_sum(normed_grad * unit)
    sums_ref[5:6, :] += row_sum(normed_grad)
    sums_ref[6:7, :] += row_sum(mlp_grad)
    sums_ref[7:8, :] += row_sum(incoming * mlp_out)
    back = []
    for t in range(2):
        total[t, :, 2 * wide :] += dot(attn_grad_low, attended[t], TN)
        back.append(dot(attn_grad_low, w_ref[t, :, 2 * wide :]))
    up_mine_ref[...] = jnp.where(even, back[0], back[1]).astype(BF16)
    up_send_ref[...] = jnp.where(even, back[1], back[0]).astype(BF16)

    @pl.when(step == pl.num_programs(0) - 1)
    def _():
        write_wire(core_ref, [total.at[t] for t in range(2)], keep_ref, send_ref, shard_rows)


ROWS = 352


def middle_call(core, x, cotangent, mine, recv, weights, vectors, units, chips, shard_rows):
    model = x.shape[1]
    width = mine.shape[1]
    row = lambda w: pl.BlockSpec((ROWS, w), lambda i, core: (i, 0))
    wire = (chips, 2, shard_rows, weights.shape[2])
    return pl.pallas_call(
        middle_kernel,
        grid_spec=pltpu.PrefetchScalarGridSpec(
            num_scalar_prefetch=1,
            grid=(HALF // ROWS,),
            in_specs=[
                row(model),
                row(model),
                row(width),
                row(width),
                whole_spec(weights.shape),
                whole_spec(vectors.shape),
                whole_spec(units.shape),
            ],
            out_specs=[
                row(model),
                row(model),
                row(width),
                row(width),
                whole_spec(wire),
                whole_spec(wire),
                whole_spec(vectors.shape),
                whole_spec(units.shape),
            ],
            scratch_shapes=[pltpu.VMEM(weights.shape, F32)],
        ),
        out_shape=[
            jax.ShapeDtypeStruct((HALF, model), BF16),
            jax.ShapeDtypeStruct((HALF, model), F32),
            jax.ShapeDtypeStruct((HALF, width), BF16),
            jax.ShapeDtypeStruct((HALF, width), BF16),
            jax.ShapeDtypeStruct(wire, BF16),
            jax.ShapeDtypeStruct(wire, BF16),
            jax.ShapeDtypeStruct(vectors.shape, F32),
            jax.ShapeDtypeStruct(units.shape, F32),
        ],
        compiler_params=params(),
        cost_estimate=pl.CostEstimate(
            flops=HALF * model * 12000 * 2, bytes_accessed=2 * 10**7, transcendentals=0
        ),
        name="middle",
    )(core, x, cotangent, mine, recv, weights, vectors, units)


def last_kernel(
    core_ref, x_ref, mine_ref, recv_ref, w_ref, vec_ref, grad_ref, sums_in_ref,
    out_ref, keep_ref, send_ref, sums_ref, head_ref, total,
):
    step = pl.program_id(0)
    even = core_ref[0] == 0
    width = mine_ref.shape[1]

    @pl.when(step == 0)
    def _():
        total[...] = jnp.zeros_like(total)
        sums_ref[...] = sums_in_ref[...]
        head_ref[...] = jnp.zeros_like(head_ref)

    gain, shift = vec_ref[0:1, :], vec_ref[1:2, :]
    unit, inverse = norm_stats(x_ref[...].astype(F32))
    normed = (unit * gain + shift).astype(BF16)
    mine, recv = mine_ref[...].astype(F32), recv_ref[...].astype(F32)
    normed_grad = 0.0
    for t in range(2):
        part = jnp.where(even, mine, recv) if t == 0 else jnp.where(even, recv, mine)
        head_ref[t : t + 1, :] += row_sum(part)
        part = part.astype(BF16)
        normed_grad = normed_grad + dot(part, w_ref[t, :, :width], NT)
        total[t] += dot(normed, part, TN)
    sums_ref[0:1, :] += row_sum(normed_grad * unit)
    sums_ref[1:2, :] += row_sum(normed_grad)
    out_ref[...] = (grad_ref[...] + norm_back(normed_grad, unit, inverse, gain)).astype(BF16)

    @pl.when(step == pl.num_programs(0) - 1)
    def _():
        write_wire(core_ref, [total.at[t] for t in range(2)], keep_ref, send_ref, keep_ref.shape[2])


def last_call(core, x, mine, recv, weights, vectors, middle_grad, sums, chips, shard_rows):
    model = x.shape[1]
    width = mine.shape[1]
    row = lambda w: pl.BlockSpec((ROWS, w), lambda i, core: (i, 0))
    wire = (chips, 2, shard_rows, width)
    return pl.pallas_call(
        last_kernel,
        grid_spec=pltpu.PrefetchScalarGridSpec(
            num_scalar_prefetch=1,
            grid=(HALF // ROWS,),
            in_specs=[
                row(model),
                row(width),
                row(width),
                whole_spec(weights.shape),
                whole_spec(vectors.shape),
                row(model),
                whole_spec(sums.shape),
            ],
            out_specs=[
                row(model),
                whole_spec(wire),
                whole_spec(wire),
                whole_spec(sums.shape),
                whole_spec((2, width)),
            ],
            scratch_shapes=[pltpu.VMEM((2, model, width), F32)],
        ),
        out_shape=[
            jax.ShapeDtypeStruct((HALF, model), BF16),
            jax.ShapeDtypeStruct(wire, BF16),
            jax.ShapeDtypeStruct(wire, BF16),
            jax.ShapeDtypeStruct(sums.shape, F32),
            jax.ShapeDtypeStruct((2, width), F32),
        ],
        compiler_params=params(),
        name="last",
    )(core, x, mine, recv, weights, vectors, middle_grad, sums)


def split_two(value):
    high = value.astype(BF16)
    return high, (value - high.astype(F32)).astype(BF16)


def dot_three(a, b):
    (a_high, a_low), (b_high, b_low) = a, b
    return dot(a_high, b_high) + (dot(a_high, b_low) + dot(a_low, b_high))


def ortho_kernel(m_ref, o_ref):
    halves, size, _ = m_ref.shape
    gram = sum(dot(m_ref[t], m_ref[t], NT) for t in range(halves))
    row = lax.broadcasted_iota(jnp.int32, (size, size), 0)
    column = lax.broadcasted_iota(jnp.int32, (size, size), 1)
    eye = row == column
    square = jnp.sum(jnp.where(eye, gram, 0.0), axis=(0, 1), keepdims=True)
    scale = 1.0 / (jnp.sqrt(square) + 1e-07)
    gram = gram * scale * scale
    product = None
    for sweep_index in range(5):
        parts = split_two(gram)
        poly = COEFF_B * gram + COEFF_C * dot_three(parts, parts)
        poly = jnp.where(eye, poly + COEFF_A, poly)
        poly_parts = split_two(poly)
        product = poly if product is None else dot_three(poly_parts, split_two(product))
        if sweep_index < 4:
            gram = dot_three(poly_parts, split_two(dot_three(parts, poly_parts)))
    high, low = split_two(product * scale)
    for t in range(halves):
        o_ref[t] = (dot(high, m_ref[t]) + dot(low, m_ref[t])).astype(BF16)


def ortho_call(matrix):
    return pl.pallas_call(
        ortho_kernel,
        out_shape=jax.ShapeDtypeStruct(matrix.shape, BF16),
        compiler_params=params(),
        name="ortho",
    )(matrix)


def bit_of(bit):
    index = lax.axis_index(AXES)
    return (index >> bit) & 1


def swap(value, bit, count):
    return lax.ppermute(value, AXES, [(i, i ^ (1 << bit)) for i in range(count)])


def relay(value, offset, count):
    return lax.ppermute(value, AXES, [(i, i ^ offset) for i in range(count)])


def by_place(value):
    size = value.shape[0]
    bits = size.bit_length() - 1
    value = value.reshape((2,) * bits + value.shape[1:])
    for bit in range(bits):
        axis = bits - 1 - bit
        value = jnp.where(bit_of(bit + 2) == 0, value, jnp.flip(value, axis))
    return value.reshape((size,) + value.shape[bits:])


def is_home(i):
    return (i & 1) == ((i >> 1) & 1)


def home_send(value, bit, count):
    return lax.ppermute(value, AXES, [(i, i ^ (1 << bit)) for i in range(count) if is_home(i)])


def same_core(count):
    return [[i for i in range(count) if (i >> 1) & 1 == core] for core in range(2)]


def exchange(value, groups):
    return lax.all_to_all(value, AXES, 0, 0, axis_index_groups=groups)


def spread(shard, groups):
    return exchange(jnp.broadcast_to(shard[None], (len(groups[0]),) + shard.shape), groups)


def shards(
    inputs,
    cotangent,
    w_qkv,
    w_out,
    w_up,
    w_down,
    vectors,
    head_bias,
    up_bias,
    mom_qkv,
    mom_out,
    mom_up,
    mom_down,
    vec_first,
    vec_second,
    head_first,
    head_second,
    unit_first,
    unit_second,
):
    dp = lax.axis_size("dp")
    tensor = lax.axis_size("tensor")
    count = dp * tensor
    model = inputs.shape[1]
    rows = w_qkv.shape[0]
    third = w_qkv.shape[2]
    qkv_width = 3 * third
    packed_width = -(-(qkv_width + 11) // LANES) * LANES
    up_width = w_up.shape[1]
    out_width = w_out.shape[0]
    group_width = up_width
    core = lax.axis_index("dp") & 1
    home = core == lax.axis_index("tensor")

    chips = dp // 2
    even = core == 0
    core_list = core.astype(jnp.int32).reshape(1)
    core_groups = same_core(count)

    def ordered(mine, other, axis):
        return jnp.where(
            even, jnp.stack([mine, other], axis=axis), jnp.stack([other, mine], axis=axis)
        )

    small = jnp.concatenate(
        [vectors.T, head_bias.reshape(rows, 1), up_bias.reshape(rows, 2)], axis=1
    )
    first = jnp.concatenate(
        [
            w_qkv.reshape(rows, qkv_width).astype(BF16),
            jnp.pad(small.astype(BF16), ((0, 0), (0, packed_width - qkv_width - 11))),
        ],
        axis=1,
    )
    later = jnp.concatenate(
        [w_up.astype(BF16), w_down.T.astype(BF16), w_out.T.astype(BF16)], axis=1
    )
    later_width = later.shape[1]
    first_mine = spread(first, core_groups)
    later_part = jnp.stack([later] + [relay(later, offset << 2, count) for offset in range(1, chips)])

    def whole_image(value):
        value = jnp.where(home, value, home_send(value, 1, count))
        padded = jnp.pad(value, ((0, PAD - SEQ), (0, 0)))
        return jnp.where(even, padded, jnp.roll(padded, HALF, axis=0))

    image = whole_image(inputs)
    image_cotangent = whole_image(cotangent)

    first_other = swap(first_mine, 1, count)
    first_shape = (chips, tensor, rows, packed_width)
    first_all = (
        ordered(first_mine.reshape(first_shape), first_other.reshape(first_shape), 1)
        .transpose(2, 0, 1, 3, 4)
        .reshape(tensor, model, packed_width)
    )
    vec_full = first_all[0, :, qkv_width : qkv_width + 8].T.astype(F32)
    head_full = (
        first_all[:, :, qkv_width + 8]
        .reshape((tensor, dp) + head_bias.shape)
        .transpose(0, 2, 3, 1, 4)
        .reshape(tensor, 2, third)
        .astype(F32)
    )
    unit_shift = (
        first_all[:, :, qkv_width + 9 : qkv_width + 11]
        .reshape((tensor, dp) + up_bias.shape)
        .transpose(0, 2, 1, 3)
        .reshape(tensor, up_width)
        .astype(F32)
    )

    q, k, v = qkv_call(core_list, image, first_all, vec_full, head_full)
    q, later_part = lax.optimization_barrier((q, later_part))
    later_across = swap(later_part, 0, count)
    attended_other, qs_other = attend_call(q, k, v, 1)
    attended_recv = swap(attended_other, 1, count)
    attended, qs = attend_call(q, k, v, 0)

    here = lax.axis_index("tensor") == 0
    attended, later_across = lax.optimization_barrier((attended, later_across))
    later_pair = jnp.stack([later_part, later_across], axis=1)
    later_four = ordered(later_pair, swap(later_pair, 1, count), 2)
    later_four = jnp.where(here, later_four, jnp.flip(later_four, 1))
    later_all = (
        by_place(later_four).transpose(1, 0, 2, 3, 4).reshape(tensor, model, later_width)
    )

    (
        output_rows, middle_grad, up_mine, up_send, later_keep, later_send, sums, unit_sums,
    ) = middle_call(
        core_list, image, image_cotangent, attended, attended_recv, later_all, vec_full,
        unit_shift, chips, rows,
    )

    def summed(keep, send):
        return keep.astype(F32) + swap(send, 1, count).astype(F32)

    up_recv = swap(up_send, 1, count)
    later_sum = summed(later_keep, later_send).astype(BF16).reshape(-1, rows, later_width)
    later_sum, up_recv = lax.optimization_barrier((later_sum, up_recv))
    later_parts = exchange(later_sum, core_groups)

    back = attend_back_call((qs, qs_other), k, v, (attended, attended_other), (up_mine, up_recv))
    back_recv = swap(back[HALF:], 1, count)
    grad_in_rows, first_keep, first_send, sums, head_sums = last_call(
        core_list, image, back, back_recv, first_all, vec_full, middle_grad, sums, chips, rows
    )
    head_sums = jnp.stack([head_sums[:, :third], head_sums[:, 2 * third :]], axis=1)
    vec_part = jnp.broadcast_to(sums.T.reshape(dp, 1, rows, 8), (dp, tensor, rows, 8))
    head_part = (
        head_sums.reshape(tensor, 2, third // HD, dp, HD // dp)
        .transpose(3, 0, 1, 2, 4)
        .reshape(dp, tensor, rows, 1)
    )
    unit_part = (
        unit_sums.reshape(tensor, up_bias.shape[0], dp, up_bias.shape[1])
        .transpose(2, 0, 1, 3)
        .reshape(dp, tensor, rows, 2)
    )
    small_part = jnp.pad(
        jnp.concatenate([vec_part, head_part, unit_part], axis=3),
        ((0, 0), (0, 0), (0, 0), (0, packed_width - qkv_width - 11)),
    ).reshape(chips, 2, tensor, rows, packed_width - qkv_width)
    small_sum = summed(
        jnp.where(even, small_part[:, 0], small_part[:, 1]),
        jnp.where(even, small_part[:, 1], small_part[:, 0]),
    )
    first_sum = jnp.concatenate(
        [summed(first_keep, first_send).astype(BF16), small_sum.astype(BF16)], axis=3
    ).reshape(-1, rows, packed_width)
    first_sum, later_parts = lax.optimization_barrier((first_sum, later_parts))
    first_red = jnp.sum(exchange(first_sum, core_groups).astype(F32), axis=0)
    red_qkv = first_red[:, :qkv_width].reshape(w_qkv.shape)
    red_vec = first_red[:, qkv_width : qkv_width + 8].T
    red_head = first_red[:, qkv_width + 8].reshape(head_bias.shape)
    red_unit = first_red[:, qkv_width + 9 : qkv_width + 11].reshape(up_bias.shape)
    later_red = jnp.sum(later_parts.astype(F32), axis=0)
    red_up = later_red[:, :up_width]
    red_down_t = later_red[:, up_width : 2 * up_width]
    red_out_t = later_red[:, 2 * up_width :]

    red_out, red_down = red_out_t.T, red_down_t.T
    moment_qkv = MOMENTUM_DECAY * mom_qkv + red_qkv
    moment_out = MOMENTUM_DECAY * mom_out + red_out
    moment_up = MOMENTUM_DECAY * mom_up + red_up
    moment_down = MOMENTUM_DECAY * mom_down + red_down

    def widen(value):
        return jnp.pad(value.astype(BF16), ((0, 0), (0, group_width - value.shape[1])))

    chunks = jnp.stack(
        [
            widen(moment_up),
            widen(moment_down.T),
            widen(moment_out.T),
            widen(moment_qkv.reshape(rows, qkv_width)),
        ]
    )
    sent = jnp.broadcast_to(chunks[None], (count // 4,) + chunks.shape)
    whole = (
        lax.all_to_all(sent.reshape(count, rows, group_width), AXES, 0, 0)
        .reshape(dp, tensor, rows, group_width)
        .transpose(1, 0, 2, 3)
        .reshape(tensor, model, group_width)
    )
    result = ortho_call(whole)
    pair = lax.dynamic_slice_in_dim(result, (lax.axis_index("dp") // 2) * 2 * rows, 2 * rows, axis=1)
    local = pair.reshape(tensor, 2, rows, group_width).transpose(1, 0, 2, 3)
    mine = lax.all_to_all(
        local.reshape(4, rows, group_width),
        AXES,
        0,
        0,
        axis_index_groups=[[4 * i + j for j in range(4)] for i in range(count // 4)],
    ).astype(F32)
    new_up = WEIGHT_KEEP * w_up - STEP_RATES[2] * mine[0]
    new_down = WEIGHT_KEEP * w_down - STEP_RATES[3] * mine[1].T
    new_out = WEIGHT_KEEP * w_out - STEP_RATES[1] * mine[2, :, :out_width].T
    new_qkv = WEIGHT_KEEP * w_qkv - STEP_RATES[0] * mine[3, :, :qkv_width].reshape(w_qkv.shape)
    vec_second_new, vec_new = adam_update(vectors, red_vec, vec_first, vec_second)
    head_second_new, head_new = adam_update(head_bias, red_head, head_first, head_second)
    unit_second_new, unit_new = adam_update(up_bias, red_unit, unit_first, unit_second)

    def to_image(value):
        full = ordered(value, swap(value, 1, count), 0).reshape(PAD, model)[:SEQ]
        return jnp.where(home, full, home_send(full, 0, count))

    output = to_image(output_rows)
    grad_in = to_image(grad_in_rows)
    return (
        output,
        grad_in,
        red_qkv,
        red_out,
        red_up,
        red_down,
        moment_qkv,
        moment_out,
        moment_up,
        moment_down,
        new_qkv,
        new_out,
        new_up,
        new_down,
        red_vec,
        vec_second_new,
        vec_new,
        red_head,
        head_second_new,
        head_new,
        red_unit,
        unit_second_new,
        unit_new,
    )


def solution(mesh):
    token = P("dp", None)
    specs = (
        P("dp", None, "tensor"),
        P("tensor", "dp"),
        P("dp", "tensor"),
        P("tensor", "dp"),
    )
    vec, head, unit = P(None, "dp"), P(None, "tensor", "dp"), P("tensor", "dp")
    return jax.shard_map(
        shards,
        mesh=mesh,
        in_specs=(token, token)
        + specs
        + (vec, head, unit)
        + specs
        + (vec, vec, head, head, unit, unit),
        out_specs=(token, token) + specs * 3 + (vec,) * 3 + (head,) * 3 + (unit,) * 3,
        check_vma=False,
    )
```

```python
from functools import partial

import jax
import jax.numpy as jnp
from jax import lax
from jax.experimental import pallas as pl
from jax.experimental.pallas import tpu as pltpu
from jax.sharding import PartitionSpec as P

HD = 64
SEQ = 1370
STEP = 10
PAD = 1408
HALF = 704
BLOCK = 352
MASKED = -1e30
LANES = 128

COEFF_A = 3.4445
COEFF_B = -4.775
COEFF_C = 2.0315
STEP_RATES = (2.7, 4.4, 2.2, 1.1)
MOMENTUM_DECAY = 0.95
WEIGHT_KEEP = 0.999
ADAM_ONE = 0.9
ADAM_TWO = 0.999
ADAM_RATE = 0.6
AXES = ("dp", "tensor")
F32 = jnp.float32
BF16 = jnp.bfloat16
NT = (((1,), (1,)), ((), ()))
TN = (((0,), (0,)), ((), ()))
VMEM_LIMIT = 56 * 1024 * 1024
QUICK = pl.CostEstimate(flops=1000, bytes_accessed=1000, transcendentals=0)


def params():
    return pltpu.CompilerParams(vmem_limit_bytes=VMEM_LIMIT)


def dot(a, b, dims=(((1,), (0,)), ((), ()))):
    return lax.dot_general(a, b, dims, preferred_element_type=F32)


def normalize(values, gain_row, shift_row):
    center = values - jnp.mean(values, axis=-1, keepdims=True)
    spread = jnp.mean(center * center, axis=-1, keepdims=True)
    return center * lax.rsqrt(spread + 1e-06) * gain_row + shift_row


def adam_update(parameter, gradient, first, second):
    first_new = ADAM_ONE * first + (1.0 - ADAM_ONE) * gradient
    second_new = ADAM_TWO * second + (1.0 - ADAM_TWO) * gradient * gradient
    first_hat = first_new / (1.0 - ADAM_ONE**STEP)
    second_hat = second_new / (1.0 - ADAM_TWO**STEP)
    return (second_new, parameter - ADAM_RATE * first_hat / (jnp.sqrt(second_hat) + 1e-08))


def three_pieces(column):
    high = column.astype(BF16)
    rest = column - high.astype(F32)
    middle = rest.astype(BF16)
    low = (rest - middle.astype(F32)).astype(BF16)
    return high.astype(F32), middle.astype(F32), low.astype(F32)


def lanes_of(rows):
    return lax.broadcasted_iota(jnp.int32, (rows, HD), 1)


def with_column(extra, rows):
    lane = lanes_of(rows)
    high, middle, low = three_pieces(extra)
    return jnp.where(lane == 1, high, jnp.where(lane == 2, middle, jnp.where(lane == 3, low, 0.0)))


def whole_spec(shape):
    return pl.BlockSpec(shape, lambda *_: (0,) * len(shape))


def qkv_kernel(core_ref, x_ref, w_ref, vec_ref, bias_ref, q_ref, k_ref, v_ref):
    heads = q_ref.shape[0]
    width = heads * HD
    rows = x_ref.shape[0]
    normed = normalize(x_ref[...].astype(F32), vec_ref[0:1, :], vec_ref[1:2, :]).astype(BF16)
    projected = dot(normed, w_ref[0, :, : 3 * width])
    lane = lanes_of(rows)
    token = pl.program_id(0) * rows + lax.broadcasted_iota(jnp.int32, (rows, HD), 0)
    token = token + core_ref[0] * HALF
    token = jnp.where(token >= PAD, token - PAD, token)
    one = jnp.where(lane == 0, 1.0, 0.0)
    pieces = jnp.where((lane >= 1) & (lane <= 3), 1.0, 0.0)
    mask = jnp.where((lane == 0) & (token >= SEQ), MASKED, pieces)
    for head in range(heads):
        at = head * HD
        query = projected[:, at : at + HD] + bias_ref[0, 0:1, at : at + HD]
        key = projected[:, width + at : width + at + HD]
        value = projected[:, 2 * width + at : 2 * width + at + HD] + bias_ref[0, 1:2, at : at + HD]
        query = query.astype(BF16).astype(F32) * 0.125
        q_ref[head] = jnp.concatenate([query, one], axis=1).astype(BF16)
        k_ref[head] = jnp.concatenate([key, mask], axis=1).astype(BF16)
        v_ref[head] = jnp.concatenate([value, one + pieces], axis=1).astype(BF16)


def qkv_call(core, x, weights, vectors, bias):
    heads = bias.shape[2] // HD
    out = jax.ShapeDtypeStruct((heads, PAD, LANES), BF16)
    spec = pl.BlockSpec((heads, BLOCK, LANES), lambda i, core: (0, i, 0))
    return pl.pallas_call(
        qkv_kernel,
        grid_spec=pltpu.PrefetchScalarGridSpec(
            num_scalar_prefetch=1,
            grid=(PAD // BLOCK,),
            in_specs=[
                pl.BlockSpec((BLOCK, x.shape[1]), lambda i, core: (i, 0)),
                pl.BlockSpec((1,) + weights.shape[1:], lambda i, core: (core[0], 0, 0)),
                whole_spec(vectors.shape),
                pl.BlockSpec((1,) + bias.shape[1:], lambda i, core: (core[0], 0, 0)),
            ],
            out_specs=[spec] * 3,
        ),
        out_shape=[out] * 3,
        compiler_params=params(),
        cost_estimate=QUICK,
        name="qkv",
    )(core, x, weights, vectors, bias)


def attend_kernel(q_ref, k_ref, v_ref, att_ref, qs_ref):
    heads, rows, _ = q_ref.shape
    parts = []
    for head in range(heads):
        query = q_ref[head]
        scores = dot(query, k_ref[head], NT)
        largest = jnp.max(scores, axis=-1, keepdims=True)
        exponent = jnp.exp(scores - largest).astype(BF16)
        total = dot(exponent, v_ref[head])
        denominator = total[:, HD : HD + 1]
        parts.append((total[:, :HD] / denominator).astype(BF16))
        logsum = largest + jnp.log(denominator)
        extra = with_column(-logsum, rows)
        lane = lanes_of(rows)
        extra = jnp.where(lane == 0, 1.0, extra)
        qs_ref[head] = jnp.concatenate([query[:, :HD].astype(F32), extra], axis=1).astype(BF16)
    att_ref[...] = jnp.concatenate(parts, axis=1)


def attend_call(q, k, v, half):
    heads = q.shape[0]
    steps = HALF // BLOCK
    whole = pl.BlockSpec((heads, PAD, LANES), lambda i: (0, 0, 0))
    return pl.pallas_call(
        attend_kernel,
        grid=(steps,),
        in_specs=[
            pl.BlockSpec((heads, BLOCK, LANES), lambda i: (0, i + half * steps, 0)),
            whole,
            whole,
        ],
        out_specs=[
            pl.BlockSpec((BLOCK, heads * HD), lambda i: (i, 0)),
            pl.BlockSpec((heads, BLOCK, LANES), lambda i: (0, i, 0)),
        ],
        out_shape=[
            jax.ShapeDtypeStruct((HALF, heads * HD), BF16),
            jax.ShapeDtypeStruct((heads, HALF, LANES), BF16),
        ],
        compiler_params=params(),
        cost_estimate=QUICK,
        name="attend",
    )(q, k, v)


def attend_back_kernel(
    qa_ref, qb_ref, k_ref, v_ref, atta_ref, attb_ref, upa_ref, upb_ref, own_ref, other_ref, queries, upstream, total
):
    heads = k_ref.shape[0]
    rows = k_ref.shape[1]
    width = heads * HD
    step = pl.program_id(0)

    @pl.when(step == 0)
    def _():
        for at, q_ref, att_ref, up_ref in ((0, qa_ref, atta_ref, upa_ref), (HALF, qb_ref, attb_ref, upb_ref)):
            for head in range(heads):
                lanes = slice(head * HD, head * HD + HD)
                grad = up_ref[:, lanes].astype(F32)
                dots = jnp.sum(grad * att_ref[:, lanes].astype(F32), axis=1, keepdims=True)
                upstream[head, at : at + HALF, :] = jnp.concatenate(
                    [grad, with_column(-dots, HALF)], axis=1
                ).astype(BF16)
                queries[head, at : at + HALF, :] = q_ref[head]
        total[...] = jnp.zeros_like(total)

    key_parts, value_parts = [], []
    for head in range(heads):
        query, grad = queries[head], upstream[head]
        key, value = k_ref[head], v_ref[head]
        weight = jnp.exp(dot(key, query, NT))
        value_parts.append(dot(weight.astype(BF16), grad)[:, :HD].astype(BF16))
        score = (weight * dot(value, grad, NT)).astype(BF16)
        key_parts.append(dot(score, query)[:, :HD].astype(BF16))
        total[head] += dot(key, score, TN)
    per_half = HALF // rows
    pad = jnp.zeros((rows, own_ref.shape[1] - 3 * width), BF16)
    both = jnp.concatenate(key_parts + value_parts + [pad], axis=1)
    for half, out_ref in enumerate((own_ref, other_ref)):

        @pl.when(step // per_half == half)
        def _():
            out_ref[pl.ds((step % per_half) * rows, rows), width:] = both

    @pl.when(step == pl.num_programs(0) - 1)
    def _():
        for half, out_ref in enumerate((own_ref, other_ref)):
            out_ref[:, :width] = jnp.concatenate(
                [
                    (total[head, :HD, half * HALF : half * HALF + HALF] * 0.125).T.astype(BF16)
                    for head in range(heads)
                ],
                axis=1,
            )


def attend_back_call(qs, k, v, attended, upstream):
    heads = k.shape[0]
    width = heads * HD
    blocked = pl.BlockSpec((heads, BLOCK, LANES), lambda i: (0, i, 0))
    q_spec = whole_spec((heads, HALF, LANES))
    flat = whole_spec((HALF, width))
    wire = (HALF, -(-3 * width // LANES) * LANES)
    return pl.pallas_call(
        attend_back_kernel,
        grid=(PAD // BLOCK,),
        in_specs=[q_spec, q_spec, blocked, blocked, flat, flat, flat, flat],
        out_specs=[whole_spec(wire)] * 2,
        out_shape=[jax.ShapeDtypeStruct(wire, BF16)] * 2,
        scratch_shapes=[
            pltpu.VMEM((heads, PAD, LANES), BF16),
            pltpu.VMEM((heads, PAD, LANES), BF16),
            pltpu.VMEM((heads, LANES, PAD), F32),
        ],
        compiler_params=params(),
        cost_estimate=QUICK,
        name="attend_back",
    )(*qs, k, v, *attended, *upstream)


ERF_SCALE = 0.3275911
ERF_TERMS = (0.254829592, -0.284496736, 1.421413741, -1.453152027, 1.061405429)


def gelu_both(x):
    size = jnp.abs(x) * (0.5**0.5)
    bell = jnp.exp(-0.5 * x * x)
    t = 1.0 / (1.0 + ERF_SCALE * size)
    poly = t * ERF_TERMS[4] + ERF_TERMS[3]
    for term in ERF_TERMS[2::-1]:
        poly = poly * t + term
    tail = (0.5 * t) * poly * bell
    cumulative = jnp.where(x < 0, tail, 1.0 - tail)
    return x * cumulative, cumulative + x * (bell * 0.3989422804014327)


def norm_stats(values):
    center = values - jnp.mean(values, axis=-1, keepdims=True)
    inverse = lax.rsqrt(jnp.mean(center * center, axis=-1, keepdims=True) + 1e-06)
    return center * inverse, inverse


def norm_back(grad, unit, inverse, gain):
    u = gain * grad
    return inverse * (
        u - jnp.mean(u, axis=-1, keepdims=True) - unit * jnp.mean(u * unit, axis=-1, keepdims=True)
    )


def row_sum(value):
    return jnp.sum(value, axis=0, keepdims=True)


def write_wire(core_ref, totals, keep_ref, send_ref, shard_rows):
    even = core_ref[0] == 0
    for chip in range(keep_ref.shape[0]):
        at = chip * 2 * shard_rows
        for t in range(len(totals)):
            low = totals[t][at : at + shard_rows, :]
            high = totals[t][at + shard_rows : at + 2 * shard_rows, :]
            width = low.shape[1]
            keep_ref[chip, t, :, :width] = jnp.where(even, low, high).astype(BF16)
            send_ref[chip, t, :, :width] = jnp.where(even, high, low).astype(BF16)


def middle_kernel(
    core_ref, x_ref, cot_ref, mine_ref, recv_ref, w0_ref, w1_ref, vec_ref, unit_ref,
    out_ref, grad_ref, up_mine_ref, up_send_ref, keep_ref, send_ref, sums_ref, unit_sums_ref,
    total,
):
    step = pl.program_id(0)
    w_refs = (w0_ref, w1_ref)
    even = core_ref[0] == 0
    wide = unit_ref.shape[1]
    shard_rows = keep_ref.shape[2]

    @pl.when(step == 0)
    def _():
        total[...] = jnp.zeros_like(total)
        sums_ref[...] = jnp.zeros_like(sums_ref)
        unit_sums_ref[...] = jnp.zeros_like(unit_sums_ref)

    vec = vec_ref[...]
    out_shift, scale_one, gain_two = vec[2:3], vec[3:4], vec[4:5]
    shift_two, down_shift, scale_two = vec[5:6], vec[6:7], vec[7:8]
    mine, recv = mine_ref[...].astype(F32), recv_ref[...].astype(F32)
    attended = [
        jnp.where(even, mine, recv).astype(BF16),
        jnp.where(even, recv, mine).astype(BF16),
    ]
    attn_out = sum(dot(attended[t], w_refs[t][:, 2 * wide :], NT) for t in range(2)) + out_shift
    middle = x_ref[...].astype(F32) + scale_one * attn_out
    unit, inverse = norm_stats(middle)
    normed = (unit * gain_two + shift_two).astype(BF16)
    incoming = cot_ref[...].astype(F32)
    mlp_grad = scale_two * incoming
    mlp_grad_low = mlp_grad.astype(BF16)
    mlp_out = down_shift
    normed_grad = 0.0
    for t in range(2):
        preact = dot(normed, w_refs[t][:, :wide]) + unit_ref[t : t + 1, :]
        activated, slope = gelu_both(preact)
        activated = activated.astype(BF16)
        mlp_out = mlp_out + dot(activated, w_refs[t][:, wide : 2 * wide], NT)
        preact_grad = dot(mlp_grad_low, w_refs[t][:, wide : 2 * wide]) * slope
        unit_sums_ref[t : t + 1, :] += row_sum(preact_grad)
        preact_low = preact_grad.astype(BF16)
        normed_grad = normed_grad + dot(preact_low, w_refs[t][:, :wide], NT)
        total[t, :, :wide] += dot(normed, preact_low, TN)
        total[t, :, wide : 2 * wide] += dot(mlp_grad_low, activated, TN)
    out_ref[...] = (middle + scale_two * mlp_out).astype(BF16)
    middle_grad = incoming + norm_back(normed_grad, unit, inverse, gain_two)
    grad_ref[...] = middle_grad
    attn_grad = scale_one * middle_grad
    attn_grad_low = attn_grad.astype(BF16)
    sums_ref[2:3, :] += row_sum(attn_grad)
    sums_ref[3:4, :] += row_sum(middle_grad * attn_out)
    sums_ref[4:5, :] += row_sum(normed_grad * unit)
    sums_ref[5:6, :] += row_sum(normed_grad)
    sums_ref[6:7, :] += row_sum(mlp_grad)
    sums_ref[7:8, :] += row_sum(incoming * mlp_out)
    back = []
    for t in range(2):
        total[t, :, 2 * wide :] += dot(attn_grad_low, attended[t], TN)
        back.append(dot(attn_grad_low, w_refs[t][:, 2 * wide :]))
    up_mine_ref[...] = jnp.where(even, back[0], back[1]).astype(BF16)
    up_send_ref[...] = jnp.where(even, back[1], back[0]).astype(BF16)

    @pl.when(step == pl.num_programs(0) - 1)
    def _():
        write_wire(core_ref, [total.at[t] for t in range(2)], keep_ref, send_ref, shard_rows)


ROWS = 352


def middle_call(core, x, cotangent, mine, recv, weights, vectors, units, chips, shard_rows):
    model = x.shape[1]
    width = mine.shape[1]
    row = lambda w: pl.BlockSpec((ROWS, w), lambda i, core: (i, 0))
    wire = (chips, 2, shard_rows, weights[0].shape[1])
    return pl.pallas_call(
        middle_kernel,
        grid_spec=pltpu.PrefetchScalarGridSpec(
            num_scalar_prefetch=1,
            grid=(HALF // ROWS,),
            in_specs=[
                row(model),
                row(model),
                row(width),
                row(width),
                whole_spec(weights[0].shape),
                whole_spec(weights[1].shape),
                whole_spec(vectors.shape),
                whole_spec(units.shape),
            ],
            out_specs=[
                row(model),
                row(model),
                row(width),
                row(width),
                whole_spec(wire),
                whole_spec(wire),
                whole_spec(vectors.shape),
                whole_spec(units.shape),
            ],
            scratch_shapes=[pltpu.VMEM((2,) + weights[0].shape, F32)],
        ),
        out_shape=[
            jax.ShapeDtypeStruct((HALF, model), BF16),
            jax.ShapeDtypeStruct((HALF, model), F32),
            jax.ShapeDtypeStruct((HALF, width), BF16),
            jax.ShapeDtypeStruct((HALF, width), BF16),
            jax.ShapeDtypeStruct(wire, BF16),
            jax.ShapeDtypeStruct(wire, BF16),
            jax.ShapeDtypeStruct(vectors.shape, F32),
            jax.ShapeDtypeStruct(units.shape, F32),
        ],
        compiler_params=params(),
        cost_estimate=QUICK,
        name="middle",
    )(core, x, cotangent, mine, recv, *weights, vectors, units)


def upright(row, size):
    return [row[:, at : at + size] for at in range(0, row.shape[1], size)]


def last_kernel(
    core_ref, x_ref, mine_ref, recv_ref, w_ref, vec_ref, grad_ref, sums_in_ref, unit_ref,
    out_ref, keep_ref, send_ref, sums_ref, head_ref, total,
):
    step = pl.program_id(0)
    even = core_ref[0] == 0
    width = head_ref.shape[1]

    @pl.when(step == 0)
    def _():
        total[...] = jnp.zeros_like(total)
        sums_ref[...] = sums_in_ref[...]
        head_ref[...] = jnp.zeros_like(head_ref)

    gain, shift = vec_ref[0:1, :], vec_ref[1:2, :]
    unit, inverse = norm_stats(x_ref[...].astype(F32))
    normed = (unit * gain + shift).astype(BF16)
    mine, recv = mine_ref[:, :width].astype(F32), recv_ref[:, :width].astype(F32)
    normed_grad = 0.0
    for t in range(2):
        part = jnp.where(even, mine, recv) if t == 0 else jnp.where(even, recv, mine)
        head_ref[t : t + 1, :] += row_sum(part)
        part = part.astype(BF16)
        normed_grad = normed_grad + dot(part, w_ref[t, :, :width], NT)
        total[t, :, :width] += dot(normed, part, TN)
    sums_ref[0:1, :] += row_sum(normed_grad * unit)
    sums_ref[1:2, :] += row_sum(normed_grad)
    out_ref[...] = (grad_ref[...] + norm_back(normed_grad, unit, inverse, gain)).astype(BF16)

    @pl.when(step == pl.num_programs(0) - 1)
    def _():
        shard_rows = keep_ref.shape[2]
        shards_in = total.shape[1] // shard_rows
        third = width // 3
        for t in range(2):
            total[t, :, width : width + 8] = sums_ref[...].T
            heads = upright(head_ref[t : t + 1, :third], HD) + upright(
                head_ref[t : t + 1, 2 * third :], HD
            )
            units = upright(unit_ref[t : t + 1, :], LANES)
            for at, pieces in ((width + 8, heads), (width + 16, units)):
                flipped = jnp.concatenate(
                    pieces + [jnp.zeros((8 - len(pieces), pieces[0].shape[1]), F32)], axis=0
                ).T
                each = flipped.shape[0] // shards_in
                for shard in range(shards_in):
                    total[t, shard * shard_rows : shard * shard_rows + each, at : at + 8] = flipped[
                        shard * each : shard * each + each, :
                    ]
        write_wire(core_ref, [total.at[t] for t in range(2)], keep_ref, send_ref, shard_rows)


def last_call(core, x, mine, recv, weights, vectors, middle_grad, sums, units, heads, chips, shard_rows):
    model = x.shape[1]
    width = 3 * heads * HD
    wide = mine.shape[1]
    row = lambda w: pl.BlockSpec((ROWS, w), lambda i, core: (i, 0))
    packed = weights.shape[2]
    wire = (chips, 2, shard_rows, packed)
    return pl.pallas_call(
        last_kernel,
        grid_spec=pltpu.PrefetchScalarGridSpec(
            num_scalar_prefetch=1,
            grid=(HALF // ROWS,),
            in_specs=[
                row(model),
                row(wide),
                row(wide),
                whole_spec(weights.shape),
                whole_spec(vectors.shape),
                row(model),
                whole_spec(sums.shape),
                whole_spec(units.shape),
            ],
            out_specs=[
                row(model),
                whole_spec(wire),
                whole_spec(wire),
                whole_spec(sums.shape),
                whole_spec((2, width)),
            ],
            scratch_shapes=[pltpu.VMEM((2, model, packed), F32)],
        ),
        out_shape=[
            jax.ShapeDtypeStruct((HALF, model), BF16),
            jax.ShapeDtypeStruct(wire, BF16),
            jax.ShapeDtypeStruct(wire, BF16),
            jax.ShapeDtypeStruct(sums.shape, F32),
            jax.ShapeDtypeStruct((2, width), F32),
        ],
        compiler_params=params(),
        cost_estimate=QUICK,
        name="last",
    )(core, x, mine, recv, weights, vectors, middle_grad, sums, units)


def split_two(value):
    high = value.astype(BF16)
    return high, (value - high.astype(F32)).astype(BF16)


def left_of(value):
    high, low = split_two(value)
    return jnp.concatenate([high, high, low], axis=1)


def right_of(value):
    high, low = split_two(value)
    return jnp.concatenate([high, low, high], axis=0)


def ortho_kernel(place_ref, m_ref, o_ref, final):
    halves, size, _ = m_ref.shape
    gram = sum(dot(m_ref[t], m_ref[t], NT) for t in range(halves))
    row = lax.broadcasted_iota(jnp.int32, (size, size), 0)
    column = lax.broadcasted_iota(jnp.int32, (size, size), 1)
    eye = row == column
    square = jnp.sum(jnp.where(eye, gram, 0.0), axis=(0, 1), keepdims=True)
    scale = 1.0 / (jnp.sqrt(square) + 1e-07)
    gram = gram * scale * scale
    product = None
    for sweep_index in range(5):
        left = left_of(gram)
        poly = COEFF_B * gram + COEFF_C * dot(left, right_of(gram))
        poly = jnp.where(eye, poly + COEFF_A, poly)
        poly_left = left_of(poly)
        following = [] if product is None else [product]
        if sweep_index < 4:
            following.append(dot(left, right_of(poly)))
        following = dot(poly_left, right_of(jnp.concatenate(following, axis=1)))
        product = poly if product is None else following[:, :size]
        gram = following[:, -size:]
    shard_rows = o_ref.shape[1]
    for chip in range(final.shape[0]):
        at = chip * 2 * shard_rows
        final[chip] = product[at : at + 2 * shard_rows, :] * scale
    high, low = split_two(final[place_ref[0]])
    for t in range(halves):
        both = dot(high, m_ref[t]) + dot(low, m_ref[t])
        for core in range(2):
            o_ref[place_ref[1] ^ (core * 2 + t)] = both[
                core * shard_rows : core * shard_rows + shard_rows, :
            ].astype(BF16)


def ortho_call(place, matrix, shard_rows):
    _, size, width = matrix.shape
    return pl.pallas_call(
        ortho_kernel,
        grid_spec=pltpu.PrefetchScalarGridSpec(
            num_scalar_prefetch=1,
            grid=(1,),
            in_specs=[whole_spec(matrix.shape)],
            out_specs=whole_spec((4, shard_rows, width)),
            scratch_shapes=[pltpu.VMEM((size // (2 * shard_rows), 2 * shard_rows, size), F32)],
        ),
        out_shape=jax.ShapeDtypeStruct((4, shard_rows, width), BF16),
        compiler_params=params(),
        cost_estimate=QUICK,
        name="ortho",
    )(place, matrix)


def bit_of(bit):
    index = lax.axis_index(AXES)
    return (index >> bit) & 1


def swap(value, bit, count):
    return lax.ppermute(value, AXES, [(i, i ^ (1 << bit)) for i in range(count)])


def is_home(i):
    return (i & 1) == ((i >> 1) & 1)


def home_send(value, bit, count):
    return lax.ppermute(value, AXES, [(i, i ^ (1 << bit)) for i in range(count) if is_home(i)])


def same_core(count):
    return [[i for i in range(count) if (i >> 1) & 1 == core] for core in range(2)]


def same_place(count):
    return [[i for i in range(count) if i & 3 == place] for place in range(4)]


def exchange(value, groups):
    return lax.all_to_all(value, AXES, 0, 0, axis_index_groups=groups)


def spread(shard, groups):
    return exchange(jnp.broadcast_to(shard[None], (len(groups[0]),) + shard.shape), groups)


def shards(
    inputs,
    cotangent,
    w_qkv,
    w_out,
    w_up,
    w_down,
    vectors,
    head_bias,
    up_bias,
    mom_qkv,
    mom_out,
    mom_up,
    mom_down,
    vec_first,
    vec_second,
    head_first,
    head_second,
    unit_first,
    unit_second,
):
    dp = lax.axis_size("dp")
    tensor = lax.axis_size("tensor")
    count = dp * tensor
    model = inputs.shape[1]
    rows = w_qkv.shape[0]
    third = w_qkv.shape[2]
    qkv_width = 3 * third
    packed_width = -(-(qkv_width + 11) // LANES) * LANES
    up_width = w_up.shape[1]
    out_width = w_out.shape[0]
    group_width = up_width
    core = lax.axis_index("dp") & 1
    home = core == lax.axis_index("tensor")

    chips = dp // 2
    even = core == 0
    core_list = core.astype(jnp.int32).reshape(1)
    core_groups, place_groups = same_core(count), same_place(count)

    def ordered(mine, other, axis):
        return jnp.where(
            even, jnp.stack([mine, other], axis=axis), jnp.stack([other, mine], axis=axis)
        )

    small = jnp.concatenate(
        [vectors.T, head_bias.reshape(rows, 1), up_bias.reshape(rows, 2)], axis=1
    )
    first = jnp.concatenate(
        [
            w_qkv.reshape(rows, qkv_width).astype(BF16),
            jnp.pad(small.astype(BF16), ((0, 0), (0, packed_width - qkv_width - 11))),
        ],
        axis=1,
    )
    first_wide = jnp.broadcast_to(first[None], (dp,) + first.shape)
    first_wide, inputs, cotangent, up_in, down_in, out_in = lax.optimization_barrier(
        (first_wide, inputs, cotangent, w_up, w_down, w_out)
    )
    later = jnp.concatenate(
        [up_in.astype(BF16), down_in.T.astype(BF16), out_in.T.astype(BF16)], axis=1
    )
    later_width = later.shape[1]
    first_mine = exchange(first_wide, core_groups)
    here = lax.axis_index("tensor") == 0
    later_across = swap(later, 0, count)
    later_pair = jnp.where(
        here, jnp.stack([later, later_across]), jnp.stack([later_across, later])
    )
    later_part = spread(later_pair, place_groups)

    def whole_image(value):
        value = jnp.where(home, value, home_send(value, 1, count))
        padded = jnp.pad(value, ((0, PAD - SEQ), (0, 0)))
        return jnp.where(even, padded, jnp.roll(padded, HALF, axis=0))

    image = whole_image(inputs)
    image_cotangent = whole_image(cotangent)

    first_other = swap(first_mine, 1, count)
    first_shape = (chips, tensor, rows, packed_width)
    first_all = (
        ordered(first_mine.reshape(first_shape), first_other.reshape(first_shape), 1)
        .transpose(2, 0, 1, 3, 4)
        .reshape(tensor, model, packed_width)
    )
    vec_full = first_all[0, :, qkv_width : qkv_width + 8].T.astype(F32)
    head_full = (
        first_all[:, :, qkv_width + 8]
        .reshape((tensor, dp) + head_bias.shape)
        .transpose(0, 2, 3, 1, 4)
        .reshape(tensor, 2, third)
        .astype(F32)
    )
    unit_shift = (
        first_all[:, :, qkv_width + 9 : qkv_width + 11]
        .reshape((tensor, dp) + up_bias.shape)
        .transpose(0, 2, 1, 3)
        .reshape(tensor, up_width)
        .astype(F32)
    )

    q, k, v = qkv_call(core_list, image, first_all, vec_full, head_full)
    attended_other, qs_other = attend_call(q, k, v, 1)
    attended_recv = swap(attended_other, 1, count)
    attended, qs = attend_call(q, k, v, 0)

    attended, attended_recv, later_part = lax.optimization_barrier(
        (attended, attended_recv, later_part)
    )
    later_other = swap(later_part, 1, count)
    later_all = [
        ordered(later_part[:, t], later_other[:, t], 1).reshape(model, later_width)
        for t in range(tensor)
    ]

    (
        output_rows, middle_grad, up_mine, up_send, later_keep, later_send, sums, unit_sums,
    ) = middle_call(
        core_list, image, image_cotangent, attended, attended_recv, later_all, vec_full,
        unit_shift, chips, rows,
    )

    def summed(keep, send):
        return keep.astype(F32) + swap(send, 1, count).astype(F32)

    up_recv = swap(up_send, 1, count)
    later_sum = summed(later_keep, later_send).astype(BF16).reshape(-1, rows, later_width)
    later_sum, up_recv = lax.optimization_barrier((later_sum, up_recv))
    later_parts = exchange(later_sum, core_groups)

    back, back_send = attend_back_call((qs, qs_other), k, v, (attended, attended_other), (up_mine, up_recv))
    back_recv = swap(back_send, 1, count)
    grad_in_rows, first_keep, first_send, _, _ = last_call(
        core_list, image, back, back_recv, first_all, vec_full, middle_grad, sums, unit_sums,
        third // HD, chips, rows,
    )
    first_sum = summed(first_keep, first_send).astype(BF16).reshape(-1, rows, packed_width)
    first_sum, later_parts = lax.optimization_barrier((first_sum, later_parts))
    def gathered(value):
        return ordered(value, swap(value, 1, count), 0).reshape(PAD, model)[:SEQ]

    output_full, grad_in_full = gathered(output_rows), gathered(grad_in_rows)
    first_parts = exchange(first_sum, core_groups)
    first_parts, output_full, grad_in_full = lax.optimization_barrier(
        (first_parts, output_full, grad_in_full)
    )
    first_red = jnp.sum(first_parts.astype(F32), axis=0)
    red_qkv = jnp.stack(
        [first_red[:, j * third : (j + 1) * third] for j in range(3)]
    )
    red_vec = first_red[:, qkv_width : qkv_width + 8].T
    head_rows, unit_rows = head_bias.shape[2], up_bias.shape[1]
    at = qkv_width + 8
    red_head = first_red[:head_rows, at : at + 6].T.reshape(head_bias.shape).transpose(1, 0, 2)
    red_unit = first_red[:unit_rows, at + 8 : at + 14].T
    later_red = jnp.sum(later_parts.astype(F32), axis=0)
    red_up = later_red[:, :up_width]
    red_down_t = later_red[:, up_width : 2 * up_width]
    red_out_t = later_red[:, 2 * up_width :]

    def to_image(full):
        return jnp.where(home, full, home_send(full, 0, count))

    red_out, red_down = red_out_t.T, red_down_t.T
    w_qkv, mom_qkv, head_bias, head_first, head_second = (
        value.transpose(1, 0, 2) for value in (w_qkv, mom_qkv, head_bias, head_first, head_second)
    )
    moment_qkv = MOMENTUM_DECAY * mom_qkv + red_qkv
    moment_out = MOMENTUM_DECAY * mom_out + red_out
    moment_up = MOMENTUM_DECAY * mom_up + red_up
    moment_down = MOMENTUM_DECAY * mom_down + red_down

    def widen(value):
        return jnp.pad(value.astype(BF16), ((0, 0), (0, group_width - value.shape[1])))

    chunks = jnp.stack(
        [
            widen(moment_up),
            widen(moment_down.T),
            widen(moment_out.T),
            widen(jnp.concatenate([moment_qkv[j] for j in range(3)], axis=1)),
        ]
    )
    sent = jnp.broadcast_to(chunks[None], (count // 4,) + chunks.shape)
    whole = (
        lax.all_to_all(sent.reshape(count, rows, group_width), AXES, 0, 0)
        .reshape(dp, tensor, rows, group_width)
        .transpose(1, 0, 2, 3)
        .reshape(tensor, model, group_width)
    )
    vec_second_new, vec_new = adam_update(vectors, red_vec, vec_first, vec_second)
    head_second_new, head_new = adam_update(head_bias, red_head, head_first, head_second)
    unit_second_new, unit_new = adam_update(up_bias, red_unit, unit_first, unit_second)
    grad_in = to_image(grad_in_full)
    output = to_image(output_full)
    done = (
        red_qkv,
        red_out,
        red_up,
        red_down,
        moment_qkv,
        moment_out,
        moment_up,
        moment_down,
        red_vec,
        vec_second_new,
        vec_new,
        red_head,
        head_second_new,
        head_new,
        red_unit,
        unit_second_new,
        unit_new,
    )
    whole, done = lax.optimization_barrier((whole, done))
    (
        red_qkv,
        red_out,
        red_up,
        red_down,
        moment_qkv,
        moment_out,
        moment_up,
        moment_down,
        red_vec,
        vec_second_new,
        vec_new,
        red_head,
        head_second_new,
        head_new,
        red_unit,
        unit_second_new,
        unit_new,
    ) = done
    own = core * 2 + lax.axis_index("tensor")
    place = jnp.stack([lax.axis_index("dp") // 2, own]).astype(jnp.int32)
    result = ortho_call(place, whole, rows)
    come = [result[0]] + [
        lax.ppermute(result[offset], AXES, [(i, i ^ offset) for i in range(count)])
        for offset in range(1, 4)
    ]
    pairs = jnp.stack(come).reshape(2, 2, rows, group_width)
    pairs = jnp.where(even, pairs, jnp.flip(pairs, 0))
    pairs = jnp.where(here, pairs, jnp.flip(pairs, 1))
    mine = pairs.reshape(4, rows, group_width).astype(F32)
    new_up = WEIGHT_KEEP * w_up - STEP_RATES[2] * mine[0]
    new_down = WEIGHT_KEEP * w_down - STEP_RATES[3] * mine[1].T
    new_out = WEIGHT_KEEP * w_out - STEP_RATES[1] * mine[2, :, :out_width].T
    ortho_qkv = jnp.stack([mine[3, :, j * third : (j + 1) * third] for j in range(3)])
    new_qkv = WEIGHT_KEEP * w_qkv - STEP_RATES[0] * ortho_qkv
    red_qkv, moment_qkv, new_qkv, red_head, head_second_new, head_new = (
        value.transpose(1, 0, 2)
        for value in (red_qkv, moment_qkv, new_qkv, red_head, head_second_new, head_new)
    )
    return (
        output,
        grad_in,
        red_qkv,
        red_out,
        red_up,
        red_down,
        moment_qkv,
        moment_out,
        moment_up,
        moment_down,
        new_qkv,
        new_out,
        new_up,
        new_down,
        red_vec,
        vec_second_new,
        vec_new,
        red_head,
        head_second_new,
        head_new,
        red_unit,
        unit_second_new,
        unit_new,
    )


def solution(mesh):
    token = P("dp", None)
    specs = (
        P("dp", None, "tensor"),
        P("tensor", "dp"),
        P("dp", "tensor"),
        P("tensor", "dp"),
    )
    vec, head, unit = P(None, "dp"), P(None, "tensor", "dp"), P("tensor", "dp")
    return jax.shard_map(
        shards,
        mesh=mesh,
        in_specs=(token, token)
        + specs
        + (vec, head, unit)
        + specs
        + (vec, vec, head, head, unit, unit),
        out_specs=(token, token) + specs * 3 + (vec,) * 3 + (head,) * 3 + (unit,) * 3,
        check_vma=False,
    )
```

```python
from functools import partial

import jax
import jax.numpy as jnp
from jax import lax
from jax.experimental import pallas as pl
from jax.experimental.pallas import tpu as pltpu
from jax.sharding import PartitionSpec as P

HD = 64
SEQ = 1370
STEP = 10
PAD = 1408
HALF = 704
BLOCK = 704
MASKED = -1e30
LANES = 128

EXACT_SWEEPS = 5
COEFF_A = 3.4445
COEFF_B = -4.775
COEFF_C = 2.0315
STEP_RATES = (2.7, 4.4, 2.2, 1.1)
MOMENTUM_DECAY = 0.95
WEIGHT_KEEP = 0.999
ADAM_ONE = 0.9
ADAM_TWO = 0.999
ADAM_RATE = 0.6
AXES = ("dp", "tensor")
F32 = jnp.float32
BF16 = jnp.bfloat16
NT = (((1,), (1,)), ((), ()))
TN = (((0,), (0,)), ((), ()))
VMEM_LIMIT = 56 * 1024 * 1024
QUICK = pl.CostEstimate(flops=1000, bytes_accessed=1000, transcendentals=0)


def params():
    return pltpu.CompilerParams(vmem_limit_bytes=VMEM_LIMIT)


def dot(a, b, dims=(((1,), (0,)), ((), ()))):
    return lax.dot_general(a, b, dims, preferred_element_type=F32)


def normalize(values, gain_row, shift_row):
    center = values - jnp.mean(values, axis=-1, keepdims=True)
    spread = jnp.mean(center * center, axis=-1, keepdims=True)
    return center * lax.rsqrt(spread + 1e-06) * gain_row + shift_row


def adam_update(parameter, gradient, first, second):
    first_new = ADAM_ONE * first + (1.0 - ADAM_ONE) * gradient
    second_new = ADAM_TWO * second + (1.0 - ADAM_TWO) * gradient * gradient
    first_hat = first_new / (1.0 - ADAM_ONE**STEP)
    second_hat = second_new / (1.0 - ADAM_TWO**STEP)
    return (second_new, parameter - ADAM_RATE * first_hat / (jnp.sqrt(second_hat) + 1e-08))


def three_pieces(column):
    high = column.astype(BF16)
    rest = column - high.astype(F32)
    middle = rest.astype(BF16)
    low = (rest - middle.astype(F32)).astype(BF16)
    return high.astype(F32), middle.astype(F32), low.astype(F32)


def lanes_of(rows):
    return lax.broadcasted_iota(jnp.int32, (rows, HD), 1)


def with_column(extra, rows):
    lane = lanes_of(rows)
    high, middle, low = three_pieces(extra)
    return jnp.where(lane == 1, high, jnp.where(lane == 2, middle, jnp.where(lane == 3, low, 0.0)))


def whole_spec(shape):
    return pl.BlockSpec(shape, lambda *_: (0,) * len(shape))


def upright(row, size):
    return [row[:, at : at + size] for at in range(0, row.shape[1], size)]


def flipped(pieces):
    width = pieces[0].shape[1]
    wide = -(-width // LANES) * LANES
    if wide > width:
        pieces = [jnp.concatenate([p, jnp.zeros((p.shape[0], wide - width), F32)], axis=1) for p in pieces]
    missing = 8 - sum(piece.shape[0] for piece in pieces)
    if missing:
        pieces = pieces + [jnp.zeros((missing, wide), F32)]
    return jnp.concatenate(pieces, axis=0).T


def pack_kernel(w_ref, vec_ref, head_ref, unit_ref, out_ref):
    copies, rows, width = out_ref.shape
    third = w_ref.shape[2]
    heads = [head_ref[head, part : part + 1, :] for part in range(2) for head in range(head_ref.shape[0])]
    blocks = []
    for piece, count in (
        ([vec_ref[...]], rows),
        (heads, head_ref.shape[2]),
        ([unit_ref[...]], unit_ref.shape[1]),
    ):
        column = flipped(piece)[:count, :]
        if count < rows:
            column = jnp.concatenate([column, jnp.zeros((rows - count, 8), F32)], axis=0)
        blocks.append(column)
    blocks.append(jnp.zeros((rows, width - 3 * third - 24), F32))
    packed = jnp.concatenate([w_ref[part] for part in range(3)] + blocks, axis=1).astype(BF16)
    for copy in range(copies):
        out_ref[copy] = packed


def pack_call(weights, vectors, heads, units, copies, width):
    rows = weights.shape[1]
    return pl.pallas_call(
        pack_kernel,
        out_shape=jax.ShapeDtypeStruct((copies, rows, width), BF16),
        compiler_params=params(),
        cost_estimate=QUICK,
        name="pack",
    )(weights, vectors, heads, units)


def qkv_kernel(core_ref, x_ref, w_ref, q_ref, k_ref, v_ref, vec_ref, unit_ref, bias, *, shard_rows):
    heads = q_ref.shape[0]
    width = heads * HD
    rows = x_ref.shape[0]
    model = x_ref.shape[1]
    core = core_ref[0]

    @pl.when(pl.program_id(0) == 0)
    def _():
        shards_in = model // shard_rows
        tail = 3 * width // LANES * LANES
        skip = 3 * width - tail

        def chosen(count):
            each = count // shards_in
            row = lax.broadcasted_iota(jnp.int32, (model, count), 0)
            column = lax.broadcasted_iota(jnp.int32, (model, count), 1)
            if each == shard_rows:
                source = column
            else:
                source = (column >> (each.bit_length() - 1)) * shard_rows + (column & (each - 1))
            return jnp.where(row == source, 1.0, 0.0).astype(BF16)

        vec_ref[...] = dot(w_ref[0, :, tail:], chosen(model), TN)[skip : skip + 8, :]
        bias[...] = dot(w_ref[core, :, tail:], chosen(HD), TN)[skip + 8 : skip + 16, :]
        for t in range(2):
            units = dot(w_ref[t, :, tail:], chosen(LANES), TN)[skip + 16 : skip + 24, :]
            unit_ref[t : t + 1, :] = jnp.concatenate(
                [units[j : j + 1, :] for j in range(unit_ref.shape[1] // LANES)], axis=1
            )

    normed = normalize(x_ref[...].astype(F32), vec_ref[0:1, :], vec_ref[1:2, :]).astype(BF16)
    projected = dot(normed, w_ref[core, :, : 3 * width])
    lane = lanes_of(rows)
    token = pl.program_id(0) * rows + lax.broadcasted_iota(jnp.int32, (rows, HD), 0)
    token = token + core * HALF
    token = jnp.where(token >= PAD, token - PAD, token)
    one = jnp.where(lane == 0, 1.0, 0.0)
    pieces = jnp.where((lane >= 1) & (lane <= 3), 1.0, 0.0)
    mask = jnp.where((lane == 0) & (token >= SEQ), MASKED, pieces)
    for head in range(heads):
        at = head * HD
        query = projected[:, at : at + HD] + bias[head : head + 1, :]
        key = projected[:, width + at : width + at + HD]
        value = projected[:, 2 * width + at : 2 * width + at + HD] + bias[heads + head : heads + head + 1, :]
        query = query.astype(BF16).astype(F32) * 0.125
        q_ref[head] = jnp.concatenate([query, one], axis=1).astype(BF16)
        k_ref[head] = jnp.concatenate([key, mask], axis=1).astype(BF16)
        v_ref[head] = jnp.concatenate([value, one + pieces], axis=1).astype(BF16)


def qkv_call(core, x, weights, heads, hidden, shard_rows):
    model = x.shape[1]
    out = jax.ShapeDtypeStruct((heads, PAD, LANES), BF16)
    spec = pl.BlockSpec((heads, BLOCK, LANES), lambda i, core: (0, i, 0))
    return pl.pallas_call(
        partial(qkv_kernel, shard_rows=shard_rows),
        grid_spec=pltpu.PrefetchScalarGridSpec(
            num_scalar_prefetch=1,
            grid=(PAD // BLOCK,),
            in_specs=[
                pl.BlockSpec((BLOCK, model), lambda i, core: (i, 0)),
                whole_spec(weights.shape),
            ],
            out_specs=[spec] * 3 + [whole_spec((8, model)), whole_spec((2, hidden))],
            scratch_shapes=[pltpu.VMEM((8, HD), F32)],
        ),
        out_shape=[out] * 3
        + [jax.ShapeDtypeStruct((8, model), F32), jax.ShapeDtypeStruct((2, hidden), F32)],
        compiler_params=params(),
        cost_estimate=QUICK,
        name="qkv",
    )(core, x, weights)


def attend_kernel(q_ref, k_ref, v_ref, att_ref, qs_ref):
    heads, rows, _ = q_ref.shape
    parts = []
    for head in range(heads):
        query = q_ref[head]
        scores = dot(query, k_ref[head], NT)
        largest = jnp.max(scores, axis=-1, keepdims=True)
        exponent = jnp.exp(scores - largest).astype(BF16)
        total = dot(exponent, v_ref[head])
        denominator = total[:, HD : HD + 1]
        parts.append((total[:, :HD] / denominator).astype(BF16))
        logsum = largest + jnp.log(denominator)
        extra = with_column(-logsum, rows)
        lane = lanes_of(rows)
        extra = jnp.where(lane == 0, 1.0, extra)
        qs_ref[head] = jnp.concatenate([query[:, :HD].astype(F32), extra], axis=1).astype(BF16)
    att_ref[...] = jnp.concatenate(parts, axis=1)


def attend_call(q, k, v, half):
    heads = q.shape[0]
    steps = HALF // BLOCK
    whole = pl.BlockSpec((heads, PAD, LANES), lambda i: (0, 0, 0))
    return pl.pallas_call(
        attend_kernel,
        grid=(steps,),
        in_specs=[
            pl.BlockSpec((heads, BLOCK, LANES), lambda i: (0, i + half * steps, 0)),
            whole,
            whole,
        ],
        out_specs=[
            pl.BlockSpec((BLOCK, heads * HD), lambda i: (i, 0)),
            pl.BlockSpec((heads, BLOCK, LANES), lambda i: (0, i, 0)),
        ],
        out_shape=[
            jax.ShapeDtypeStruct((HALF, heads * HD), BF16),
            jax.ShapeDtypeStruct((heads, HALF, LANES), BF16),
        ],
        compiler_params=params(),
        cost_estimate=QUICK,
        name="attend",
    )(q, k, v)


def attend_back_kernel(
    qa_ref, qb_ref, k_ref, v_ref, atta_ref, attb_ref, upa_ref, upb_ref, own_ref, other_ref, queries, upstream, total
):
    heads = k_ref.shape[0]
    rows = k_ref.shape[1]
    width = heads * HD
    step = pl.program_id(0)

    @pl.when(step == 0)
    def _():
        for at, q_ref, att_ref, up_ref in ((0, qa_ref, atta_ref, upa_ref), (HALF, qb_ref, attb_ref, upb_ref)):
            for head in range(heads):
                lanes = slice(head * HD, head * HD + HD)
                grad = up_ref[:, lanes].astype(F32)
                dots = jnp.sum(grad * att_ref[:, lanes].astype(F32), axis=1, keepdims=True)
                upstream[head, at : at + HALF, :] = jnp.concatenate(
                    [grad, with_column(-dots, HALF)], axis=1
                ).astype(BF16)
                queries[head, at : at + HALF, :] = q_ref[head]
        total[...] = jnp.zeros_like(total)

    key_parts, value_parts = [], []
    for head in range(heads):
        query, grad = queries[head], upstream[head]
        key, value = k_ref[head], v_ref[head]
        weight = jnp.exp(dot(key, query, NT))
        value_parts.append(dot(weight.astype(BF16), grad)[:, :HD].astype(BF16))
        score = (weight * dot(value, grad, NT)).astype(BF16)
        key_parts.append(dot(score, query)[:, :HD].astype(BF16))
        total[head] += dot(key, score, TN)
    per_half = HALF // rows
    pad = jnp.zeros((rows, own_ref.shape[1] - 3 * width), BF16)
    both = jnp.concatenate(key_parts + value_parts + [pad], axis=1)
    for half, out_ref in enumerate((own_ref, other_ref)):

        @pl.when(step // per_half == half)
        def _():
            out_ref[pl.ds((step % per_half) * rows, rows), width:] = both

    @pl.when(step == pl.num_programs(0) - 1)
    def _():
        for half, out_ref in enumerate((own_ref, other_ref)):
            out_ref[:, :width] = jnp.concatenate(
                [
                    (total[head, :HD, half * HALF : half * HALF + HALF] * 0.125).T.astype(BF16)
                    for head in range(heads)
                ],
                axis=1,
            )


def attend_back_call(qs, k, v, attended, upstream):
    heads = k.shape[0]
    width = heads * HD
    blocked = pl.BlockSpec((heads, BLOCK, LANES), lambda i: (0, i, 0))
    q_spec = whole_spec((heads, HALF, LANES))
    flat = whole_spec((HALF, width))
    wire = (HALF, -(-3 * width // LANES) * LANES)
    return pl.pallas_call(
        attend_back_kernel,
        grid=(PAD // BLOCK,),
        in_specs=[q_spec, q_spec, blocked, blocked, flat, flat, flat, flat],
        out_specs=[whole_spec(wire)] * 2,
        out_shape=[jax.ShapeDtypeStruct(wire, BF16)] * 2,
        scratch_shapes=[
            pltpu.VMEM((heads, PAD, LANES), BF16),
            pltpu.VMEM((heads, PAD, LANES), BF16),
            pltpu.VMEM((heads, LANES, PAD), F32),
        ],
        compiler_params=params(),
        cost_estimate=QUICK,
        name="attend_back",
    )(*qs, k, v, *attended, *upstream)


ERF_SCALE = 0.3275911
ERF_TERMS = (0.254829592, -0.284496736, 1.421413741, -1.453152027, 1.061405429)


def gelu_both(x):
    size = jnp.abs(x) * (0.5**0.5)
    bell = jnp.exp(-0.5 * x * x)
    t = 1.0 / (1.0 + ERF_SCALE * size)
    poly = t * ERF_TERMS[4] + ERF_TERMS[3]
    for term in ERF_TERMS[2::-1]:
        poly = poly * t + term
    tail = (0.5 * t) * poly * bell
    cumulative = jnp.where(x < 0, tail, 1.0 - tail)
    return x * cumulative, cumulative + x * (bell * 0.3989422804014327)


def norm_stats(values):
    center = values - jnp.mean(values, axis=-1, keepdims=True)
    inverse = lax.rsqrt(jnp.mean(center * center, axis=-1, keepdims=True) + 1e-06)
    return center * inverse, inverse


def norm_back(grad, unit, inverse, gain):
    u = gain * grad
    return inverse * (
        u - jnp.mean(u, axis=-1, keepdims=True) - unit * jnp.mean(u * unit, axis=-1, keepdims=True)
    )


def row_sum(value):
    return jnp.sum(value, axis=0, keepdims=True)


def write_wire(core_ref, totals, keep_ref, send_ref, shard_rows):
    even = core_ref[0] == 0
    for chip in range(keep_ref.shape[0]):
        at = chip * 2 * shard_rows
        for t in range(len(totals)):
            low = totals[t][at : at + shard_rows, :]
            high = totals[t][at + shard_rows : at + 2 * shard_rows, :]
            width = low.shape[1]
            keep_ref[chip, t, :, :width] = jnp.where(even, low, high).astype(BF16)
            send_ref[chip, t, :, :width] = jnp.where(even, high, low).astype(BF16)


def middle_kernel(
    core_ref, x_ref, cot_ref, mine_ref, recv_ref, w0_ref, w1_ref, vec_ref, unit_ref,
    out_ref, grad_ref, up_mine_ref, up_send_ref, keep_ref, send_ref, sums_ref, unit_sums_ref,
    total,
):
    step = pl.program_id(0)
    w_refs = (w0_ref, w1_ref)
    even = core_ref[0] == 0
    wide = unit_ref.shape[1]
    shard_rows = keep_ref.shape[2]

    @pl.when(step == 0)
    def _():
        total[...] = jnp.zeros_like(total)
        sums_ref[...] = jnp.zeros_like(sums_ref)
        unit_sums_ref[...] = jnp.zeros_like(unit_sums_ref)

    vec = vec_ref[...]
    out_shift, scale_one, gain_two = vec[2:3], vec[3:4], vec[4:5]
    shift_two, down_shift, scale_two = vec[5:6], vec[6:7], vec[7:8]
    mine, recv = mine_ref[...].astype(F32), recv_ref[...].astype(F32)
    attended = [
        jnp.where(even, mine, recv).astype(BF16),
        jnp.where(even, recv, mine).astype(BF16),
    ]
    attn_out = sum(dot(attended[t], w_refs[t][:, 2 * wide :], NT) for t in range(2)) + out_shift
    middle = x_ref[...].astype(F32) + scale_one * attn_out
    unit, inverse = norm_stats(middle)
    normed = (unit * gain_two + shift_two).astype(BF16)
    incoming = cot_ref[...].astype(F32)
    mlp_grad = scale_two * incoming
    mlp_grad_low = mlp_grad.astype(BF16)
    mlp_out = down_shift
    normed_grad = 0.0
    for t in range(2):
        preact = dot(normed, w_refs[t][:, :wide]) + unit_ref[t : t + 1, :]
        activated, slope = gelu_both(preact)
        activated = activated.astype(BF16)
        mlp_out = mlp_out + dot(activated, w_refs[t][:, wide : 2 * wide], NT)
        preact_grad = dot(mlp_grad_low, w_refs[t][:, wide : 2 * wide]) * slope
        unit_sums_ref[t : t + 1, :] += row_sum(preact_grad)
        preact_low = preact_grad.astype(BF16)
        normed_grad = normed_grad + dot(preact_low, w_refs[t][:, :wide], NT)
        total[t, :, :wide] += dot(normed, preact_low, TN)
        total[t, :, wide : 2 * wide] += dot(mlp_grad_low, activated, TN)
    out_ref[...] = (middle + scale_two * mlp_out).astype(BF16)
    middle_grad = incoming + norm_back(normed_grad, unit, inverse, gain_two)
    grad_ref[...] = middle_grad
    attn_grad = scale_one * middle_grad
    attn_grad_low = attn_grad.astype(BF16)
    sums_ref[2:3, :] += row_sum(attn_grad)
    sums_ref[3:4, :] += row_sum(middle_grad * attn_out)
    sums_ref[4:5, :] += row_sum(normed_grad * unit)
    sums_ref[5:6, :] += row_sum(normed_grad)
    sums_ref[6:7, :] += row_sum(mlp_grad)
    sums_ref[7:8, :] += row_sum(incoming * mlp_out)
    back = []
    for t in range(2):
        total[t, :, 2 * wide :] += dot(attn_grad_low, attended[t], TN)
        back.append(dot(attn_grad_low, w_refs[t][:, 2 * wide :]))
    up_mine_ref[...] = jnp.where(even, back[0], back[1]).astype(BF16)
    up_send_ref[...] = jnp.where(even, back[1], back[0]).astype(BF16)

    @pl.when(step == pl.num_programs(0) - 1)
    def _():
        write_wire(core_ref, [total.at[t] for t in range(2)], keep_ref, send_ref, shard_rows)


ROWS = 704


def middle_call(core, x, cotangent, mine, recv, weights, vectors, units, chips, shard_rows):
    model = x.shape[1]
    width = mine.shape[1]
    row = lambda w: pl.BlockSpec((ROWS, w), lambda i, core: (i, 0))
    wire = (chips, 2, shard_rows, weights[0].shape[1])
    return pl.pallas_call(
        middle_kernel,
        grid_spec=pltpu.PrefetchScalarGridSpec(
            num_scalar_prefetch=1,
            grid=(HALF // ROWS,),
            in_specs=[
                row(model),
                row(model),
                row(width),
                row(width),
                whole_spec(weights[0].shape),
                whole_spec(weights[1].shape),
                whole_spec(vectors.shape),
                whole_spec(units.shape),
            ],
            out_specs=[
                row(model),
                row(model),
                row(width),
                row(width),
                whole_spec(wire),
                whole_spec(wire),
                whole_spec(vectors.shape),
                whole_spec(units.shape),
            ],
            scratch_shapes=[pltpu.VMEM((2,) + weights[0].shape, F32)],
        ),
        out_shape=[
            jax.ShapeDtypeStruct((HALF, model), BF16),
            jax.ShapeDtypeStruct((HALF, model), F32),
            jax.ShapeDtypeStruct((HALF, width), BF16),
            jax.ShapeDtypeStruct((HALF, width), BF16),
            jax.ShapeDtypeStruct(wire, BF16),
            jax.ShapeDtypeStruct(wire, BF16),
            jax.ShapeDtypeStruct(vectors.shape, F32),
            jax.ShapeDtypeStruct(units.shape, F32),
        ],
        compiler_params=params(),
        cost_estimate=QUICK,
        name="middle",
    )(core, x, cotangent, mine, recv, *weights, vectors, units)


def last_kernel(
    core_ref, x_ref, mine_ref, recv_ref, w_ref, vec_ref, grad_ref, sums_in_ref, unit_ref,
    out_ref, keep_ref, send_ref, sums_ref, head_ref, total,
):
    step = pl.program_id(0)
    even = core_ref[0] == 0
    width = head_ref.shape[1]

    @pl.when(step == 0)
    def _():
        total[...] = jnp.zeros_like(total)
        sums_ref[...] = sums_in_ref[...]
        head_ref[...] = jnp.zeros_like(head_ref)

    gain, shift = vec_ref[0:1, :], vec_ref[1:2, :]
    unit, inverse = norm_stats(x_ref[...].astype(F32))
    normed = (unit * gain + shift).astype(BF16)
    mine, recv = mine_ref[:, :width].astype(F32), recv_ref[:, :width].astype(F32)
    normed_grad = 0.0
    for t in range(2):
        part = jnp.where(even, mine, recv) if t == 0 else jnp.where(even, recv, mine)
        head_ref[t : t + 1, :] += row_sum(part)
        part = part.astype(BF16)
        normed_grad = normed_grad + dot(part, w_ref[t, :, :width], NT)
        total[t, :, :width] += dot(normed, part, TN)
    sums_ref[0:1, :] += row_sum(normed_grad * unit)
    sums_ref[1:2, :] += row_sum(normed_grad)
    out_ref[...] = (grad_ref[...] + norm_back(normed_grad, unit, inverse, gain)).astype(BF16)

    @pl.when(step == pl.num_programs(0) - 1)
    def _():
        shard_rows = keep_ref.shape[2]
        shards_in = total.shape[1] // shard_rows
        third = width // 3
        for t in range(2):
            total[t, :, width : width + 8] = sums_ref[...].T
            heads = upright(head_ref[t : t + 1, :third], HD) + upright(
                head_ref[t : t + 1, 2 * third :], HD
            )
            units = upright(unit_ref[t : t + 1, :], LANES)
            for at, column in ((width + 8, flipped(heads)), (width + 16, flipped(units))):
                count = HD if at == width + 8 else LANES
                each = count // shards_in
                for shard in range(shards_in):
                    total[t, shard * shard_rows : shard * shard_rows + each, at : at + 8] = column[
                        shard * each : shard * each + each, :
                    ]
        write_wire(core_ref, [total.at[t] for t in range(2)], keep_ref, send_ref, shard_rows)


def last_call(core, x, mine, recv, weights, vectors, middle_grad, sums, units, heads, chips, shard_rows):
    model = x.shape[1]
    width = 3 * heads * HD
    wide = mine.shape[1]
    row = lambda w: pl.BlockSpec((ROWS, w), lambda i, core: (i, 0))
    packed = weights.shape[2]
    wire = (chips, 2, shard_rows, packed)
    return pl.pallas_call(
        last_kernel,
        grid_spec=pltpu.PrefetchScalarGridSpec(
            num_scalar_prefetch=1,
            grid=(HALF // ROWS,),
            in_specs=[
                row(model),
                row(wide),
                row(wide),
                whole_spec(weights.shape),
                whole_spec(vectors.shape),
                row(model),
                whole_spec(sums.shape),
                whole_spec(units.shape),
            ],
            out_specs=[
                row(model),
                whole_spec(wire),
                whole_spec(wire),
                whole_spec(sums.shape),
                whole_spec((2, width)),
            ],
            scratch_shapes=[pltpu.VMEM((2, model, packed), F32)],
        ),
        out_shape=[
            jax.ShapeDtypeStruct((HALF, model), BF16),
            jax.ShapeDtypeStruct(wire, BF16),
            jax.ShapeDtypeStruct(wire, BF16),
            jax.ShapeDtypeStruct(sums.shape, F32),
            jax.ShapeDtypeStruct((2, width), F32),
        ],
        compiler_params=params(),
        cost_estimate=QUICK,
        name="last",
    )(core, x, mine, recv, weights, vectors, middle_grad, sums, units)


def split_two(value):
    high = value.astype(BF16)
    return high, (value - high.astype(F32)).astype(BF16)


def left_of(value, exact):
    if not exact:
        return value.astype(BF16)
    high, low = split_two(value)
    return jnp.concatenate([high, high, low], axis=1)


def right_of(value, exact):
    if not exact:
        return value.astype(BF16)
    high, low = split_two(value)
    return jnp.concatenate([high, low, high], axis=0)


def ortho_kernel(place_ref, m_ref, o_ref, final):
    halves, size, _ = m_ref.shape
    gram = sum(dot(m_ref[t], m_ref[t], NT) for t in range(halves))
    row = lax.broadcasted_iota(jnp.int32, (size, size), 0)
    column = lax.broadcasted_iota(jnp.int32, (size, size), 1)
    eye = row == column
    square = jnp.sum(jnp.where(eye, gram, 0.0), axis=(0, 1), keepdims=True)
    scale = 1.0 / (jnp.sqrt(square) + 1e-07)
    gram = gram * scale * scale
    product = None
    for sweep_index in range(5):
        exact = sweep_index < EXACT_SWEEPS
        left = left_of(gram, exact)
        poly = COEFF_B * gram + COEFF_C * dot(left, right_of(gram, exact))
        poly = jnp.where(eye, poly + COEFF_A, poly)
        poly_left = left_of(poly, exact)
        following = [] if product is None else [product]
        if sweep_index < 4:
            following.append(dot(left, right_of(poly, exact)))
        following = dot(poly_left, right_of(jnp.concatenate(following, axis=1), exact))
        product = poly if product is None else following[:, :size]
        gram = following[:, -size:]
    shard_rows = o_ref.shape[1]
    for chip in range(final.shape[0]):
        at = chip * 2 * shard_rows
        final[chip] = product[at : at + 2 * shard_rows, :] * scale
    high, low = split_two(final[place_ref[0]])
    for t in range(halves):
        both = dot(high, m_ref[t]) + dot(low, m_ref[t])
        for core in range(2):
            o_ref[place_ref[1] ^ (core * 2 + t)] = both[
                core * shard_rows : core * shard_rows + shard_rows, :
            ].astype(BF16)


def ortho_call(place, matrix, shard_rows):
    _, size, width = matrix.shape
    return pl.pallas_call(
        ortho_kernel,
        grid_spec=pltpu.PrefetchScalarGridSpec(
            num_scalar_prefetch=1,
            grid=(1,),
            in_specs=[whole_spec(matrix.shape)],
            out_specs=whole_spec((4, shard_rows, width)),
            scratch_shapes=[pltpu.VMEM((size // (2 * shard_rows), 2 * shard_rows, size), F32)],
        ),
        out_shape=jax.ShapeDtypeStruct((4, shard_rows, width), BF16),
        compiler_params=params(),
        cost_estimate=QUICK,
        name="ortho",
    )(place, matrix)


def bit_of(bit):
    index = lax.axis_index(AXES)
    return (index >> bit) & 1


def swap(value, bit, count):
    return lax.ppermute(value, AXES, [(i, i ^ (1 << bit)) for i in range(count)])


def is_home(i):
    return (i & 1) == ((i >> 1) & 1)


def home_send(value, bit, count):
    return lax.ppermute(value, AXES, [(i, i ^ (1 << bit)) for i in range(count) if is_home(i)])


def same_core(count):
    return [[i for i in range(count) if (i >> 1) & 1 == core] for core in range(2)]


def same_place(count):
    return [[i for i in range(count) if i & 3 == place] for place in range(4)]


def exchange(value, groups):
    return lax.all_to_all(value, AXES, 0, 0, axis_index_groups=groups)


def shards(
    inputs,
    cotangent,
    w_qkv,
    w_out,
    w_up,
    w_down,
    vectors,
    head_bias,
    up_bias,
    mom_qkv,
    mom_out,
    mom_up,
    mom_down,
    vec_first,
    vec_second,
    head_first,
    head_second,
    unit_first,
    unit_second,
):
    dp = lax.axis_size("dp")
    tensor = lax.axis_size("tensor")
    count = dp * tensor
    model = inputs.shape[1]
    rows = w_qkv.shape[0]
    third = w_qkv.shape[2]
    qkv_width = 3 * third
    packed_width = -(-(qkv_width + 24) // LANES) * LANES
    up_width = w_up.shape[1]
    out_width = w_out.shape[0]
    group_width = up_width
    core = lax.axis_index("dp") & 1
    home = core == lax.axis_index("tensor")

    chips = dp // 2
    even = core == 0
    core_list = core.astype(jnp.int32).reshape(1)
    core_groups, place_groups = same_core(count), same_place(count)

    def ordered(mine, other, axis):
        return jnp.where(
            even, jnp.stack([mine, other], axis=axis), jnp.stack([other, mine], axis=axis)
        )

    first_wide = pack_call(
        w_qkv.transpose(1, 0, 2), vectors, head_bias.transpose(1, 0, 2), up_bias, dp, packed_width
    )
    first_wide, inputs, cotangent, up_in, down_in, out_in = lax.optimization_barrier(
        (first_wide, inputs, cotangent, w_up, w_down, w_out)
    )
    later = jnp.concatenate(
        [up_in.astype(BF16), down_in.T.astype(BF16), out_in.T.astype(BF16)], axis=1
    )
    later_width = later.shape[1]
    here = lax.axis_index("tensor") == 0
    later_across = swap(later, 0, count)
    later_pair = jnp.where(
        here, jnp.stack([later, later_across]), jnp.stack([later_across, later])
    )
    later_wide = jnp.broadcast_to(later_pair[None], (chips,) + later_pair.shape)
    first_mine = exchange(first_wide, core_groups)
    later_part = exchange(later_wide, place_groups)

    def whole_image(value):
        value = jnp.where(home, value, home_send(value, 1, count))
        padded = jnp.pad(value, ((0, PAD - SEQ), (0, 0)))
        return jnp.where(even, padded, jnp.roll(padded, HALF, axis=0))

    image = whole_image(inputs)
    image_cotangent = whole_image(cotangent)
    image, image_cotangent = lax.optimization_barrier((image, image_cotangent))

    first_other = swap(first_mine, 1, count)
    first_shape = (chips, tensor, rows, packed_width)
    first_all = (
        ordered(first_mine.reshape(first_shape), first_other.reshape(first_shape), 1)
        .transpose(2, 0, 1, 3, 4)
        .reshape(tensor, model, packed_width)
    )
    q, k, v, vec_full, unit_shift = qkv_call(
        core_list, image, first_all, third // HD, up_width, rows
    )
    attended_other, qs_other = attend_call(q, k, v, 1)
    attended_recv = swap(attended_other, 1, count)
    attended, qs = attend_call(q, k, v, 0)

    attended, attended_recv, later_part = lax.optimization_barrier(
        (attended, attended_recv, later_part)
    )
    later_other = swap(later_part, 1, count)
    later_all = [
        ordered(later_part[:, t], later_other[:, t], 1).reshape(model, later_width)
        for t in range(tensor)
    ]

    (
        output_rows, middle_grad, up_mine, up_send, later_keep, later_send, sums, unit_sums,
    ) = middle_call(
        core_list, image, image_cotangent, attended, attended_recv, later_all, vec_full,
        unit_shift, chips, rows,
    )

    def summed(keep, send):
        return keep.astype(F32) + swap(send, 1, count).astype(F32)

    up_recv = swap(up_send, 1, count)
    later_sum = summed(later_keep, later_send).astype(BF16).reshape(-1, rows, later_width)
    later_sum, up_recv = lax.optimization_barrier((later_sum, up_recv))
    later_parts = exchange(later_sum, core_groups)

    back, back_send = attend_back_call((qs, qs_other), k, v, (attended, attended_other), (up_mine, up_recv))
    back_recv = swap(back_send, 1, count)
    grad_in_rows, first_keep, first_send, _, _ = last_call(
        core_list, image, back, back_recv, first_all, vec_full, middle_grad, sums, unit_sums,
        third // HD, chips, rows,
    )
    first_sum = summed(first_keep, first_send).astype(BF16).reshape(-1, rows, packed_width)
    first_sum, later_parts = lax.optimization_barrier((first_sum, later_parts))
    def gathered(value):
        return ordered(value, swap(value, 1, count), 0).reshape(PAD, model)[:SEQ]

    output_full, grad_in_full = gathered(output_rows), gathered(grad_in_rows)
    first_parts = exchange(first_sum, core_groups)
    first_parts, output_full, grad_in_full = lax.optimization_barrier(
        (first_parts, output_full, grad_in_full)
    )
    first_red = jnp.sum(first_parts.astype(F32), axis=0)
    red_qkv = jnp.stack(
        [first_red[:, j * third : (j + 1) * third] for j in range(3)]
    )
    red_vec = first_red[:, qkv_width : qkv_width + 8].T
    head_rows, unit_rows = head_bias.shape[2], up_bias.shape[1]
    at = qkv_width + 8
    red_head = first_red[:head_rows, at : at + 6].T.reshape(head_bias.shape).transpose(1, 0, 2)
    red_unit = first_red[:unit_rows, at + 8 : at + 14].T
    later_red = jnp.sum(later_parts.astype(F32), axis=0)
    red_up = later_red[:, :up_width]
    red_down_t = later_red[:, up_width : 2 * up_width]
    red_out_t = later_red[:, 2 * up_width :]

    def to_image(full):
        return jnp.where(home, full, home_send(full, 0, count))

    red_out, red_down = red_out_t.T, red_down_t.T
    w_qkv, mom_qkv, head_bias, head_first, head_second = (
        value.transpose(1, 0, 2) for value in (w_qkv, mom_qkv, head_bias, head_first, head_second)
    )
    moment_qkv = MOMENTUM_DECAY * mom_qkv + red_qkv
    moment_out = MOMENTUM_DECAY * mom_out + red_out
    moment_up = MOMENTUM_DECAY * mom_up + red_up
    moment_down = MOMENTUM_DECAY * mom_down + red_down

    def widen(value):
        return jnp.pad(value.astype(BF16), ((0, 0), (0, group_width - value.shape[1])))

    chunks = jnp.stack(
        [
            widen(moment_up),
            widen(moment_down.T),
            widen(moment_out.T),
            widen(jnp.concatenate([moment_qkv[j] for j in range(3)], axis=1)),
        ]
    )
    sent = jnp.broadcast_to(chunks[None], (count // 4,) + chunks.shape)
    whole = (
        lax.all_to_all(sent.reshape(count, rows, group_width), AXES, 0, 0)
        .reshape(dp, tensor, rows, group_width)
        .transpose(1, 0, 2, 3)
        .reshape(tensor, model, group_width)
    )
    vec_second_new, vec_new = adam_update(vectors, red_vec, vec_first, vec_second)
    head_second_new, head_new = adam_update(head_bias, red_head, head_first, head_second)
    unit_second_new, unit_new = adam_update(up_bias, red_unit, unit_first, unit_second)
    grad_in = to_image(grad_in_full)
    output = to_image(output_full)
    done = (
        red_qkv,
        red_out,
        red_up,
        red_down,
        moment_qkv,
        moment_out,
        moment_up,
        moment_down,
        red_vec,
        vec_second_new,
        vec_new,
        red_head,
        head_second_new,
        head_new,
        red_unit,
        unit_second_new,
        unit_new,
    )
    whole, done = lax.optimization_barrier((whole, done))
    (
        red_qkv,
        red_out,
        red_up,
        red_down,
        moment_qkv,
        moment_out,
        moment_up,
        moment_down,
        red_vec,
        vec_second_new,
        vec_new,
        red_head,
        head_second_new,
        head_new,
        red_unit,
        unit_second_new,
        unit_new,
    ) = done
    own = core * 2 + lax.axis_index("tensor")
    place = jnp.stack([lax.axis_index("dp") // 2, own]).astype(jnp.int32)
    result = ortho_call(place, whole, rows)
    come = [result[0]] + [
        lax.ppermute(result[offset], AXES, [(i, i ^ offset) for i in range(count)])
        for offset in range(1, 4)
    ]
    pairs = jnp.stack(come).reshape(2, 2, rows, group_width)
    pairs = jnp.where(even, pairs, jnp.flip(pairs, 0))
    pairs = jnp.where(here, pairs, jnp.flip(pairs, 1))
    mine = pairs.reshape(4, rows, group_width).astype(F32)
    new_up = WEIGHT_KEEP * w_up - STEP_RATES[2] * mine[0]
    new_down = WEIGHT_KEEP * w_down - STEP_RATES[3] * mine[1].T
    new_out = WEIGHT_KEEP * w_out - STEP_RATES[1] * mine[2, :, :out_width].T
    ortho_qkv = jnp.stack([mine[3, :, j * third : (j + 1) * third] for j in range(3)])
    new_qkv = WEIGHT_KEEP * w_qkv - STEP_RATES[0] * ortho_qkv
    red_qkv, moment_qkv, new_qkv, red_head, head_second_new, head_new = (
        value.transpose(1, 0, 2)
        for value in (red_qkv, moment_qkv, new_qkv, red_head, head_second_new, head_new)
    )
    return (
        output,
        grad_in,
        red_qkv,
        red_out,
        red_up,
        red_down,
        moment_qkv,
        moment_out,
        moment_up,
        moment_down,
        new_qkv,
        new_out,
        new_up,
        new_down,
        red_vec,
        vec_second_new,
        vec_new,
        red_head,
        head_second_new,
        head_new,
        red_unit,
        unit_second_new,
        unit_new,
    )


def solution(mesh):
    token = P("dp", None)
    specs = (
        P("dp", None, "tensor"),
        P("tensor", "dp"),
        P("dp", "tensor"),
        P("tensor", "dp"),
    )
    vec, head, unit = P(None, "dp"), P(None, "tensor", "dp"), P("tensor", "dp")
    return jax.shard_map(
        shards,
        mesh=mesh,
        in_specs=(token, token)
        + specs
        + (vec, head, unit)
        + specs
        + (vec, vec, head, head, unit, unit),
        out_specs=(token, token) + specs * 3 + (vec,) * 3 + (head,) * 3 + (unit,) * 3,
        check_vma=False,
    )
```

```python
from functools import partial

import jax
import jax.numpy as jnp
from jax import lax
from jax.experimental import pallas as pl
from jax.experimental.layout import Layout, with_layout_constraint
from jax.experimental.pallas import tpu as pltpu
from jax.sharding import PartitionSpec as P

HD = 64
SEQ = 1370
STEP = 10
PAD = 1408
HALF = 704
BLOCK = 704
MASKED = -1e30
LANES = 128

COEFF_A = 3.4445
COEFF_B = -4.775
COEFF_C = 2.0315
STEP_RATES = (2.7, 4.4, 2.2, 1.1)
MOMENTUM_DECAY = 0.95
WEIGHT_KEEP = 0.999
ADAM_ONE = 0.9
ADAM_TWO = 0.999
ADAM_RATE = 0.6
AXES = ("dp", "tensor")
F32 = jnp.float32
BF16 = jnp.bfloat16
NT = (((1,), (1,)), ((), ()))
TN = (((0,), (0,)), ((), ()))
VMEM_LIMIT = 56 * 1024 * 1024
QUICK = pl.CostEstimate(flops=1000, bytes_accessed=1000, transcendentals=0)


def params():
    return pltpu.CompilerParams(vmem_limit_bytes=VMEM_LIMIT)


def dot(a, b, dims=(((1,), (0,)), ((), ()))):
    return lax.dot_general(a, b, dims, preferred_element_type=F32)


def normalize(values, gain_row, shift_row):
    center = values - jnp.mean(values, axis=-1, keepdims=True)
    spread = jnp.mean(center * center, axis=-1, keepdims=True)
    return center * lax.rsqrt(spread + 1e-06) * gain_row + shift_row


def adam_update(parameter, gradient, first, second):
    first_new = ADAM_ONE * first + (1.0 - ADAM_ONE) * gradient
    second_new = ADAM_TWO * second + (1.0 - ADAM_TWO) * gradient * gradient
    first_hat = first_new / (1.0 - ADAM_ONE**STEP)
    second_hat = second_new / (1.0 - ADAM_TWO**STEP)
    return (second_new, parameter - ADAM_RATE * first_hat / (jnp.sqrt(second_hat) + 1e-08))


def three_pieces(column):
    high = column.astype(BF16)
    rest = column - high.astype(F32)
    middle = rest.astype(BF16)
    low = (rest - middle.astype(F32)).astype(BF16)
    return high.astype(F32), middle.astype(F32), low.astype(F32)


def lanes_of(rows):
    return lax.broadcasted_iota(jnp.int32, (rows, HD), 1)


def with_column(extra, rows):
    lane = lanes_of(rows)
    high, middle, low = three_pieces(extra)
    return jnp.where(lane == 1, high, jnp.where(lane == 2, middle, jnp.where(lane == 3, low, 0.0)))


def whole_spec(shape):
    return pl.BlockSpec(shape, lambda *_: (0,) * len(shape))


def upright(row, size):
    return [row[:, at : at + size] for at in range(0, row.shape[1], size)]


def flipped(pieces):
    width = pieces[0].shape[1]
    wide = -(-width // LANES) * LANES
    if wide > width:
        pieces = [jnp.concatenate([p, jnp.zeros((p.shape[0], wide - width), F32)], axis=1) for p in pieces]
    missing = 8 - sum(piece.shape[0] for piece in pieces)
    if missing:
        pieces = pieces + [jnp.zeros((missing, wide), F32)]
    return jnp.concatenate(pieces, axis=0).T


def pack_kernel(w_ref, vec_ref, head_ref, unit_ref, out_ref):
    copies, rows, width = out_ref.shape
    third = w_ref.shape[2]
    heads = [head_ref[head, part : part + 1, :] for part in range(2) for head in range(head_ref.shape[0])]
    blocks = []
    for piece, count in (
        ([vec_ref[...]], rows),
        (heads, head_ref.shape[2]),
        ([unit_ref[...]], unit_ref.shape[1]),
    ):
        column = flipped(piece)[:count, :]
        if count < rows:
            column = jnp.concatenate([column, jnp.zeros((rows - count, 8), F32)], axis=0)
        blocks.append(column)
    blocks.append(jnp.zeros((rows, width - 3 * third - 24), F32))
    packed = jnp.concatenate([w_ref[part] for part in range(3)] + blocks, axis=1).astype(BF16)
    for copy in range(copies):
        out_ref[copy] = packed


def pack_call(weights, vectors, heads, units, copies, width):
    rows = weights.shape[1]
    return pl.pallas_call(
        pack_kernel,
        out_shape=jax.ShapeDtypeStruct((copies, rows, width), BF16),
        compiler_params=params(),
        cost_estimate=QUICK,
        name="pack",
    )(weights, vectors, heads, units)


def qkv_kernel(core_ref, x_ref, w_ref, q_ref, k_ref, v_ref, vec_ref, unit_ref, bias, *, shard_rows):
    heads = q_ref.shape[0]
    width = heads * HD
    rows = x_ref.shape[0]
    model = x_ref.shape[1]
    core = core_ref[0]

    @pl.when(pl.program_id(0) == 0)
    def _():
        shards_in = model // shard_rows
        tail = 3 * width // LANES * LANES
        skip = 3 * width - tail

        def chosen(count):
            each = count // shards_in
            row = lax.broadcasted_iota(jnp.int32, (model, count), 0)
            column = lax.broadcasted_iota(jnp.int32, (model, count), 1)
            if each == shard_rows:
                source = column
            else:
                source = (column >> (each.bit_length() - 1)) * shard_rows + (column & (each - 1))
            return jnp.where(row == source, 1.0, 0.0).astype(BF16)

        vec_ref[...] = dot(w_ref[0, :, tail:], chosen(model), TN)[skip : skip + 8, :]
        bias[...] = dot(w_ref[core, :, tail:], chosen(HD), TN)[skip + 8 : skip + 16, :]
        for t in range(2):
            units = dot(w_ref[t, :, tail:], chosen(LANES), TN)[skip + 16 : skip + 24, :]
            unit_ref[t : t + 1, :] = jnp.concatenate(
                [units[j : j + 1, :] for j in range(unit_ref.shape[1] // LANES)], axis=1
            )

    normed = normalize(x_ref[...].astype(F32), vec_ref[0:1, :], vec_ref[1:2, :]).astype(BF16)
    projected = dot(normed, w_ref[core, :, : 3 * width])
    lane = lanes_of(rows)
    token = pl.program_id(0) * rows + lax.broadcasted_iota(jnp.int32, (rows, HD), 0)
    token = token + core * HALF
    token = jnp.where(token >= PAD, token - PAD, token)
    one = jnp.where(lane == 0, 1.0, 0.0)
    pieces = jnp.where((lane >= 1) & (lane <= 3), 1.0, 0.0)
    mask = jnp.where((lane == 0) & (token >= SEQ), MASKED, pieces)
    for head in range(heads):
        at = head * HD
        query = projected[:, at : at + HD] + bias[head : head + 1, :]
        key = projected[:, width + at : width + at + HD]
        value = projected[:, 2 * width + at : 2 * width + at + HD] + bias[heads + head : heads + head + 1, :]
        query = query.astype(BF16).astype(F32) * 0.125
        q_ref[head] = jnp.concatenate([query, one], axis=1).astype(BF16)
        k_ref[head] = jnp.concatenate([key, mask], axis=1).astype(BF16)
        v_ref[head] = jnp.concatenate([value, one + pieces], axis=1).astype(BF16)


def qkv_call(core, x, weights, heads, hidden, shard_rows):
    model = x.shape[1]
    out = jax.ShapeDtypeStruct((heads, PAD, LANES), BF16)
    spec = pl.BlockSpec((heads, BLOCK, LANES), lambda i, core: (0, i, 0))
    return pl.pallas_call(
        partial(qkv_kernel, shard_rows=shard_rows),
        grid_spec=pltpu.PrefetchScalarGridSpec(
            num_scalar_prefetch=1,
            grid=(PAD // BLOCK,),
            in_specs=[
                pl.BlockSpec((BLOCK, model), lambda i, core: (i, 0)),
                whole_spec(weights.shape),
            ],
            out_specs=[spec] * 3 + [whole_spec((8, model)), whole_spec((2, hidden))],
            scratch_shapes=[pltpu.VMEM((8, HD), F32)],
        ),
        out_shape=[out] * 3
        + [jax.ShapeDtypeStruct((8, model), F32), jax.ShapeDtypeStruct((2, hidden), F32)],
        compiler_params=params(),
        cost_estimate=QUICK,
        name="qkv",
    )(core, x, weights)


def attend_kernel(q_ref, k_ref, v_ref, att_ref, qs_ref):
    heads, rows, _ = q_ref.shape
    parts = []
    for head in range(heads):
        query = q_ref[head]
        scores = dot(query, k_ref[head], NT)
        largest = jnp.max(scores, axis=-1, keepdims=True)
        exponent = jnp.exp(scores - largest).astype(BF16)
        total = dot(exponent, v_ref[head])
        denominator = total[:, HD : HD + 1]
        parts.append((total[:, :HD] / denominator).astype(BF16))
        logsum = largest + jnp.log(denominator)
        extra = with_column(-logsum, rows)
        lane = lanes_of(rows)
        extra = jnp.where(lane == 0, 1.0, extra)
        qs_ref[head] = jnp.concatenate([query[:, :HD].astype(F32), extra], axis=1).astype(BF16)
    att_ref[...] = jnp.concatenate(parts, axis=1)


def attend_call(q, k, v, half):
    heads = q.shape[0]
    steps = HALF // BLOCK
    whole = pl.BlockSpec((heads, PAD, LANES), lambda i: (0, 0, 0))
    return pl.pallas_call(
        attend_kernel,
        grid=(steps,),
        in_specs=[
            pl.BlockSpec((heads, BLOCK, LANES), lambda i: (0, i + half * steps, 0)),
            whole,
            whole,
        ],
        out_specs=[
            pl.BlockSpec((BLOCK, heads * HD), lambda i: (i, 0)),
            pl.BlockSpec((heads, BLOCK, LANES), lambda i: (0, i, 0)),
        ],
        out_shape=[
            jax.ShapeDtypeStruct((HALF, heads * HD), BF16),
            jax.ShapeDtypeStruct((heads, HALF, LANES), BF16),
        ],
        compiler_params=params(),
        cost_estimate=QUICK,
        name="attend",
    )(q, k, v)


def attend_back_kernel(
    qa_ref, qb_ref, k_ref, v_ref, atta_ref, attb_ref, upa_ref, upb_ref, own_ref, other_ref, queries, upstream, total
):
    heads = k_ref.shape[0]
    rows = k_ref.shape[1]
    width = heads * HD
    step = pl.program_id(0)

    @pl.when(step == 0)
    def _():
        for at, q_ref, att_ref, up_ref in ((0, qa_ref, atta_ref, upa_ref), (HALF, qb_ref, attb_ref, upb_ref)):
            for head in range(heads):
                lanes = slice(head * HD, head * HD + HD)
                grad = up_ref[:, lanes].astype(F32)
                dots = jnp.sum(grad * att_ref[:, lanes].astype(F32), axis=1, keepdims=True)
                upstream[head, at : at + HALF, :] = jnp.concatenate(
                    [grad, with_column(-dots, HALF)], axis=1
                ).astype(BF16)
                queries[head, at : at + HALF, :] = q_ref[head]
        total[...] = jnp.zeros_like(total)

    key_parts, value_parts = [], []
    for head in range(heads):
        query, grad = queries[head], upstream[head]
        key, value = k_ref[head], v_ref[head]
        weight = jnp.exp(dot(key, query, NT))
        value_parts.append(dot(weight.astype(BF16), grad)[:, :HD].astype(BF16))
        score = (weight * dot(value, grad, NT)).astype(BF16)
        key_parts.append(dot(score, query)[:, :HD].astype(BF16))
        total[head] += dot(key, score, TN)
    per_half = HALF // rows
    pad = jnp.zeros((rows, own_ref.shape[1] - 3 * width), BF16)
    both = jnp.concatenate(key_parts + value_parts + [pad], axis=1)
    for half, out_ref in enumerate((own_ref, other_ref)):

        @pl.when(step // per_half == half)
        def _():
            out_ref[pl.ds((step % per_half) * rows, rows), width:] = both

    @pl.when(step == pl.num_programs(0) - 1)
    def _():
        for half, out_ref in enumerate((own_ref, other_ref)):
            out_ref[:, :width] = jnp.concatenate(
                [
                    (total[head, :HD, half * HALF : half * HALF + HALF] * 0.125).T.astype(BF16)
                    for head in range(heads)
                ],
                axis=1,
            )


def attend_back_call(qs, k, v, attended, upstream):
    heads = k.shape[0]
    width = heads * HD
    blocked = pl.BlockSpec((heads, BLOCK, LANES), lambda i: (0, i, 0))
    q_spec = whole_spec((heads, HALF, LANES))
    flat = whole_spec((HALF, width))
    wire = (HALF, -(-3 * width // LANES) * LANES)
    return pl.pallas_call(
        attend_back_kernel,
        grid=(PAD // BLOCK,),
        in_specs=[q_spec, q_spec, blocked, blocked, flat, flat, flat, flat],
        out_specs=[whole_spec(wire)] * 2,
        out_shape=[jax.ShapeDtypeStruct(wire, BF16)] * 2,
        scratch_shapes=[
            pltpu.VMEM((heads, PAD, LANES), BF16),
            pltpu.VMEM((heads, PAD, LANES), BF16),
            pltpu.VMEM((heads, LANES, PAD), F32),
        ],
        compiler_params=params(),
        cost_estimate=QUICK,
        name="attend_back",
    )(*qs, k, v, *attended, *upstream)


ERF_SCALE = 0.3275911
ERF_TERMS = (0.254829592, -0.284496736, 1.421413741, -1.453152027, 1.061405429)


def gelu_both(x):
    size = jnp.abs(x) * (0.5**0.5)
    bell = jnp.exp(-0.5 * x * x)
    t = 1.0 / (1.0 + ERF_SCALE * size)
    poly = t * ERF_TERMS[4] + ERF_TERMS[3]
    for term in ERF_TERMS[2::-1]:
        poly = poly * t + term
    tail = (0.5 * t) * poly * bell
    cumulative = jnp.where(x < 0, tail, 1.0 - tail)
    return x * cumulative, cumulative + x * (bell * 0.3989422804014327)


def norm_stats(values):
    center = values - jnp.mean(values, axis=-1, keepdims=True)
    inverse = lax.rsqrt(jnp.mean(center * center, axis=-1, keepdims=True) + 1e-06)
    return center * inverse, inverse


def norm_back(grad, unit, inverse, gain):
    u = gain * grad
    return inverse * (
        u - jnp.mean(u, axis=-1, keepdims=True) - unit * jnp.mean(u * unit, axis=-1, keepdims=True)
    )


def row_sum(value):
    return jnp.sum(value, axis=0, keepdims=True)


def write_wire(core_ref, totals, keep_ref, send_ref, shard_rows):
    even = core_ref[0] == 0
    for chip in range(keep_ref.shape[0]):
        at = chip * 2 * shard_rows
        for t in range(len(totals)):
            low = totals[t][at : at + shard_rows, :]
            high = totals[t][at + shard_rows : at + 2 * shard_rows, :]
            width = low.shape[1]
            keep_ref[chip, t, :, :width] = jnp.where(even, low, high).astype(BF16)
            send_ref[chip, t, :, :width] = jnp.where(even, high, low).astype(BF16)


def middle_kernel(
    core_ref, x_ref, cot_ref, mine_ref, recv_ref, w0_ref, w1_ref, vec_ref, unit_ref,
    out_ref, grad_ref, up_mine_ref, up_send_ref, keep_ref, send_ref, sums_ref, unit_sums_ref,
    total,
):
    step = pl.program_id(0)
    w_refs = (w0_ref, w1_ref)
    even = core_ref[0] == 0
    wide = unit_ref.shape[1]
    shard_rows = keep_ref.shape[2]

    @pl.when(step == 0)
    def _():
        total[...] = jnp.zeros_like(total)
        sums_ref[...] = jnp.zeros_like(sums_ref)
        unit_sums_ref[...] = jnp.zeros_like(unit_sums_ref)

    vec = vec_ref[...]
    out_shift, scale_one, gain_two = vec[2:3], vec[3:4], vec[4:5]
    shift_two, down_shift, scale_two = vec[5:6], vec[6:7], vec[7:8]
    mine, recv = mine_ref[...].astype(F32), recv_ref[...].astype(F32)
    attended = [
        jnp.where(even, mine, recv).astype(BF16),
        jnp.where(even, recv, mine).astype(BF16),
    ]
    attn_out = sum(dot(attended[t], w_refs[t][:, 2 * wide :], NT) for t in range(2)) + out_shift
    middle = x_ref[...].astype(F32) + scale_one * attn_out
    unit, inverse = norm_stats(middle)
    normed = (unit * gain_two + shift_two).astype(BF16)
    incoming = cot_ref[...].astype(F32)
    mlp_grad = scale_two * incoming
    mlp_grad_low = mlp_grad.astype(BF16)
    mlp_out = down_shift
    normed_grad = 0.0
    for t in range(2):
        preact = dot(normed, w_refs[t][:, :wide]) + unit_ref[t : t + 1, :]
        activated, slope = gelu_both(preact)
        activated = activated.astype(BF16)
        mlp_out = mlp_out + dot(activated, w_refs[t][:, wide : 2 * wide], NT)
        preact_grad = dot(mlp_grad_low, w_refs[t][:, wide : 2 * wide]) * slope
        unit_sums_ref[t : t + 1, :] += row_sum(preact_grad)
        preact_low = preact_grad.astype(BF16)
        normed_grad = normed_grad + dot(preact_low, w_refs[t][:, :wide], NT)
        total[t, :, :wide] += dot(normed, preact_low, TN)
        total[t, :, wide : 2 * wide] += dot(mlp_grad_low, activated, TN)
    out_ref[...] = (middle + scale_two * mlp_out).astype(BF16)
    middle_grad = incoming + norm_back(normed_grad, unit, inverse, gain_two)
    grad_ref[...] = middle_grad
    attn_grad = scale_one * middle_grad
    attn_grad_low = attn_grad.astype(BF16)
    sums_ref[2:3, :] += row_sum(attn_grad)
    sums_ref[3:4, :] += row_sum(middle_grad * attn_out)
    sums_ref[4:5, :] += row_sum(normed_grad * unit)
    sums_ref[5:6, :] += row_sum(normed_grad)
    sums_ref[6:7, :] += row_sum(mlp_grad)
    sums_ref[7:8, :] += row_sum(incoming * mlp_out)
    back = []
    for t in range(2):
        total[t, :, 2 * wide :] += dot(attn_grad_low, attended[t], TN)
        back.append(dot(attn_grad_low, w_refs[t][:, 2 * wide :]))
    up_mine_ref[...] = jnp.where(even, back[0], back[1]).astype(BF16)
    up_send_ref[...] = jnp.where(even, back[1], back[0]).astype(BF16)

    @pl.when(step == pl.num_programs(0) - 1)
    def _():
        write_wire(core_ref, [total.at[t] for t in range(2)], keep_ref, send_ref, shard_rows)


ROWS = 704


def middle_call(core, x, cotangent, mine, recv, weights, vectors, units, chips, shard_rows):
    model = x.shape[1]
    width = mine.shape[1]
    row = lambda w: pl.BlockSpec((ROWS, w), lambda i, core: (i, 0))
    wire = (chips, 2, shard_rows, weights[0].shape[1])
    return pl.pallas_call(
        middle_kernel,
        grid_spec=pltpu.PrefetchScalarGridSpec(
            num_scalar_prefetch=1,
            grid=(HALF // ROWS,),
            in_specs=[
                row(model),
                row(model),
                row(width),
                row(width),
                whole_spec(weights[0].shape),
                whole_spec(weights[1].shape),
                whole_spec(vectors.shape),
                whole_spec(units.shape),
            ],
            out_specs=[
                row(model),
                row(model),
                row(width),
                row(width),
                whole_spec(wire),
                whole_spec(wire),
                whole_spec(vectors.shape),
                whole_spec(units.shape),
            ],
            scratch_shapes=[pltpu.VMEM((2,) + weights[0].shape, F32)],
        ),
        out_shape=[
            jax.ShapeDtypeStruct((HALF, model), BF16),
            jax.ShapeDtypeStruct((HALF, model), F32),
            jax.ShapeDtypeStruct((HALF, width), BF16),
            jax.ShapeDtypeStruct((HALF, width), BF16),
            jax.ShapeDtypeStruct(wire, BF16),
            jax.ShapeDtypeStruct(wire, BF16),
            jax.ShapeDtypeStruct(vectors.shape, F32),
            jax.ShapeDtypeStruct(units.shape, F32),
        ],
        compiler_params=params(),
        cost_estimate=QUICK,
        name="middle",
    )(core, x, cotangent, mine, recv, *weights, vectors, units)


def last_kernel(
    core_ref, x_ref, mine_ref, recv_ref, w_ref, vec_ref, grad_ref, sums_in_ref, unit_ref,
    out_ref, keep_ref, send_ref, sums_ref, head_ref, total,
):
    step = pl.program_id(0)
    even = core_ref[0] == 0
    width = head_ref.shape[1]

    @pl.when(step == 0)
    def _():
        total[...] = jnp.zeros_like(total)
        sums_ref[...] = sums_in_ref[...]
        head_ref[...] = jnp.zeros_like(head_ref)

    gain, shift = vec_ref[0:1, :], vec_ref[1:2, :]
    unit, inverse = norm_stats(x_ref[...].astype(F32))
    normed = (unit * gain + shift).astype(BF16)
    mine, recv = mine_ref[:, :width].astype(F32), recv_ref[:, :width].astype(F32)
    normed_grad = 0.0
    for t in range(2):
        part = jnp.where(even, mine, recv) if t == 0 else jnp.where(even, recv, mine)
        head_ref[t : t + 1, :] += row_sum(part)
        part = part.astype(BF16)
        normed_grad = normed_grad + dot(part, w_ref[t, :, :width], NT)
        total[t, :, :width] += dot(normed, part, TN)
    sums_ref[0:1, :] += row_sum(normed_grad * unit)
    sums_ref[1:2, :] += row_sum(normed_grad)
    out_ref[...] = (grad_ref[...] + norm_back(normed_grad, unit, inverse, gain)).astype(BF16)

    @pl.when(step == pl.num_programs(0) - 1)
    def _():
        shard_rows = keep_ref.shape[2]
        shards_in = total.shape[1] // shard_rows
        third = width // 3
        for t in range(2):
            total[t, :, width : width + 8] = sums_ref[...].T
            heads = upright(head_ref[t : t + 1, :third], HD) + upright(
                head_ref[t : t + 1, 2 * third :], HD
            )
            units = upright(unit_ref[t : t + 1, :], LANES)
            for at, column in ((width + 8, flipped(heads)), (width + 16, flipped(units))):
                count = HD if at == width + 8 else LANES
                each = count // shards_in
                for shard in range(shards_in):
                    total[t, shard * shard_rows : shard * shard_rows + each, at : at + 8] = column[
                        shard * each : shard * each + each, :
                    ]
        write_wire(core_ref, [total.at[t] for t in range(2)], keep_ref, send_ref, shard_rows)


def last_call(core, x, mine, recv, weights, vectors, middle_grad, sums, units, heads, chips, shard_rows):
    model = x.shape[1]
    width = 3 * heads * HD
    wide = mine.shape[1]
    row = lambda w: pl.BlockSpec((ROWS, w), lambda i, core: (i, 0))
    packed = weights.shape[2]
    wire = (chips, 2, shard_rows, packed)
    return pl.pallas_call(
        last_kernel,
        grid_spec=pltpu.PrefetchScalarGridSpec(
            num_scalar_prefetch=1,
            grid=(HALF // ROWS,),
            in_specs=[
                row(model),
                row(wide),
                row(wide),
                whole_spec(weights.shape),
                whole_spec(vectors.shape),
                row(model),
                whole_spec(sums.shape),
                whole_spec(units.shape),
            ],
            out_specs=[
                row(model),
                whole_spec(wire),
                whole_spec(wire),
                whole_spec(sums.shape),
                whole_spec((2, width)),
            ],
            scratch_shapes=[pltpu.VMEM((2, model, packed), F32)],
        ),
        out_shape=[
            jax.ShapeDtypeStruct((HALF, model), BF16),
            jax.ShapeDtypeStruct(wire, BF16),
            jax.ShapeDtypeStruct(wire, BF16),
            jax.ShapeDtypeStruct(sums.shape, F32),
            jax.ShapeDtypeStruct((2, width), F32),
        ],
        compiler_params=params(),
        cost_estimate=QUICK,
        name="last",
    )(core, x, mine, recv, weights, vectors, middle_grad, sums, units)


def split_two(value):
    high = value.astype(BF16)
    return high, (value - high.astype(F32)).astype(BF16)


def left_of(value):
    high, low = split_two(value)
    return jnp.concatenate([high, high, low], axis=1)


def right_of(value):
    high, low = split_two(value)
    return jnp.concatenate([high, low, high], axis=0)


def ortho_kernel(place_ref, mine_ref, other_ref, o_ref, final):
    halves, size, wide = mine_ref.shape
    even = place_ref[2] == 0
    gram = sum(
        dot(m_ref[t], m_ref[t], NT) for m_ref in (mine_ref, other_ref) for t in range(halves)
    )
    row = lax.broadcasted_iota(jnp.int32, (size, size), 0)
    column = lax.broadcasted_iota(jnp.int32, (size, size), 1)
    eye = row == column
    square = jnp.sum(jnp.where(eye, gram, 0.0), axis=(0, 1), keepdims=True)
    scale = 1.0 / (jnp.sqrt(square) + 1e-07)
    gram = gram * scale * scale
    product = None
    for sweep_index in range(5):
        left = left_of(gram)
        poly = COEFF_B * gram + COEFF_C * dot(left, right_of(gram))
        poly = jnp.where(eye, poly + COEFF_A, poly)
        poly_left = left_of(poly)
        following = [] if product is None else [product]
        if sweep_index < 4:
            following.append(dot(left, right_of(poly)))
        following = dot(poly_left, right_of(jnp.concatenate(following, axis=1)))
        product = poly if product is None else following[:, :size]
        gram = following[:, -size:]
    shard_rows = o_ref.shape[1]
    for shard in range(final.shape[0]):
        at = shard * shard_rows
        final[shard] = product[at : at + shard_rows, :] * scale
    near = [split_two(final[place_ref[0] + 2 * chip]) for chip in range(2)]
    high, low = (jnp.concatenate([near[0][part], near[1][part]], axis=0) for part in range(2))
    for t in range(halves):
        mine, other = (dot(high, m_ref[t]) + dot(low, m_ref[t]) for m_ref in (mine_ref, other_ref))
        both = jnp.concatenate(
            [jnp.where(even, mine, other), jnp.where(even, other, mine)], axis=1
        )
        for chip in range(2):
            o_ref[place_ref[1] ^ (chip * 2 + t)] = both[
                chip * shard_rows : chip * shard_rows + shard_rows, :
            ].astype(BF16)


def ortho_call(place, mine, other, shard_rows):
    halves, size, wide = mine.shape
    out = (4, shard_rows, 2 * wide)
    return pl.pallas_call(
        ortho_kernel,
        grid_spec=pltpu.PrefetchScalarGridSpec(
            num_scalar_prefetch=1,
            grid=(1,),
            in_specs=[whole_spec(mine.shape)] * 2,
            out_specs=whole_spec(out),
            scratch_shapes=[pltpu.VMEM((size // shard_rows, shard_rows, size), F32)],
        ),
        out_shape=jax.ShapeDtypeStruct(out, BF16),
        compiler_params=params(),
        cost_estimate=QUICK,
        name="ortho",
    )(place, mine, other)


def bit_of(bit):
    index = lax.axis_index(AXES)
    return (index >> bit) & 1


def swap(value, bit, count):
    return lax.ppermute(value, AXES, [(i, i ^ (1 << bit)) for i in range(count)])


def is_home(i):
    return (i & 1) == ((i >> 1) & 1)


def home_send(value, bit, count):
    return lax.ppermute(value, AXES, [(i, i ^ (1 << bit)) for i in range(count) if is_home(i)])


def same_core(count):
    return [[i for i in range(count) if (i >> 1) & 1 == core] for core in range(2)]


def same_place(count):
    return [[i for i in range(count) if i & 3 == place] for place in range(4)]


def exchange(value, groups):
    return lax.all_to_all(value, AXES, 0, 0, axis_index_groups=groups)


def shards(
    inputs,
    cotangent,
    w_qkv,
    w_out,
    w_up,
    w_down,
    vectors,
    head_bias,
    up_bias,
    mom_qkv,
    mom_out,
    mom_up,
    mom_down,
    vec_first,
    vec_second,
    head_first,
    head_second,
    unit_first,
    unit_second,
):
    dp = lax.axis_size("dp")
    tensor = lax.axis_size("tensor")
    count = dp * tensor
    model = inputs.shape[1]
    rows = w_qkv.shape[0]
    third = w_qkv.shape[2]
    qkv_width = 3 * third
    packed_width = -(-(qkv_width + 24) // LANES) * LANES
    up_width = w_up.shape[1]
    out_width = w_out.shape[0]
    group_width = up_width
    core = lax.axis_index("dp") & 1
    home = core == lax.axis_index("tensor")

    chips = dp // 2
    even = core == 0
    core_list = core.astype(jnp.int32).reshape(1)
    core_groups, place_groups = same_core(count), same_place(count)

    def ordered(mine, other, axis):
        return jnp.where(
            even, jnp.stack([mine, other], axis=axis), jnp.stack([other, mine], axis=axis)
        )

    first_wide = pack_call(
        w_qkv.transpose(1, 0, 2), vectors, head_bias.transpose(1, 0, 2), up_bias, dp, packed_width
    )
    first_wide, inputs, cotangent, up_in, down_in, out_in = lax.optimization_barrier(
        (first_wide, inputs, cotangent, w_up, w_down, w_out)
    )
    later = jnp.concatenate(
        [up_in.astype(BF16), down_in.T.astype(BF16), out_in.T.astype(BF16)], axis=1
    )
    later_width = later.shape[1]
    here = lax.axis_index("tensor") == 0
    later_across = swap(later, 0, count)
    later_pair = jnp.where(
        here, jnp.stack([later, later_across]), jnp.stack([later_across, later])
    )
    later_wide = jnp.broadcast_to(later_pair[None], (chips,) + later_pair.shape)
    first_mine = exchange(first_wide, core_groups)
    later_part = exchange(later_wide, place_groups)

    def whole_image(value):
        value = jnp.where(home, value, home_send(value, 1, count))
        padded = jnp.pad(value, ((0, PAD - SEQ), (0, 0)))
        return jnp.where(even, padded, jnp.roll(padded, HALF, axis=0))

    image = whole_image(inputs)
    image_cotangent = whole_image(cotangent)
    image, image_cotangent = lax.optimization_barrier((image, image_cotangent))

    first_other = swap(first_mine, 1, count)
    first_shape = (chips, tensor, rows, packed_width)
    first_all = (
        ordered(first_mine.reshape(first_shape), first_other.reshape(first_shape), 1)
        .transpose(2, 0, 1, 3, 4)
        .reshape(tensor, model, packed_width)
    )
    q, k, v, vec_full, unit_shift = qkv_call(
        core_list, image, first_all, third // HD, up_width, rows
    )
    attended_other, qs_other = attend_call(q, k, v, 1)
    attended_recv = swap(attended_other, 1, count)
    attended, qs = attend_call(q, k, v, 0)

    attended, attended_recv, later_part = lax.optimization_barrier(
        (attended, attended_recv, later_part)
    )
    later_other = swap(later_part, 1, count)
    later_all = [
        ordered(later_part[:, t], later_other[:, t], 1).reshape(model, later_width)
        for t in range(tensor)
    ]

    (
        output_rows, middle_grad, up_mine, up_send, later_keep, later_send, sums, unit_sums,
    ) = middle_call(
        core_list, image, image_cotangent, attended, attended_recv, later_all, vec_full,
        unit_shift, chips, rows,
    )

    def summed(keep, send):
        return keep.astype(F32) + swap(send, 1, count).astype(F32)

    up_recv = swap(up_send, 1, count)
    later_sum = summed(later_keep, later_send).astype(BF16).reshape(-1, rows, later_width)
    later_sum, up_recv = lax.optimization_barrier((later_sum, up_recv))
    later_parts = exchange(later_sum, core_groups)

    back, back_send = attend_back_call((qs, qs_other), k, v, (attended, attended_other), (up_mine, up_recv))
    back_recv = swap(back_send, 1, count)
    grad_in_rows, first_keep, first_send, _, _ = last_call(
        core_list, image, back, back_recv, first_all, vec_full, middle_grad, sums, unit_sums,
        third // HD, chips, rows,
    )
    first_sum = summed(first_keep, first_send).astype(BF16).reshape(-1, rows, packed_width)
    first_sum, later_parts = lax.optimization_barrier((first_sum, later_parts))
    def gathered(value):
        return ordered(value, swap(value, 1, count), 0).reshape(PAD, model)[:SEQ]

    output_full, grad_in_full = gathered(output_rows), gathered(grad_in_rows)
    first_parts = exchange(first_sum, core_groups)
    first_parts, output_full, grad_in_full = lax.optimization_barrier(
        (first_parts, output_full, grad_in_full)
    )
    first_red = jnp.sum(first_parts.astype(F32), axis=0)
    red_qkv = jnp.stack(
        [first_red[:, j * third : (j + 1) * third] for j in range(3)]
    )
    red_vec = first_red[:, qkv_width : qkv_width + 8].T
    head_rows, unit_rows = head_bias.shape[2], up_bias.shape[1]
    at = qkv_width + 8
    red_head = first_red[:head_rows, at : at + 6].T.reshape(head_bias.shape).transpose(1, 0, 2)
    red_unit = with_layout_constraint(
        first_red[:unit_rows, at + 8 : at + 14].T, Layout(major_to_minor=(0, 1))
    )
    later_red = jnp.sum(later_parts.astype(F32), axis=0)
    red_up = later_red[:, :up_width]
    red_down_t = later_red[:, up_width : 2 * up_width]
    red_out_t = later_red[:, 2 * up_width :]

    def to_image(full):
        return jnp.where(home, full, home_send(full, 0, count))

    red_out, red_down = red_out_t.T, red_down_t.T
    w_qkv, mom_qkv, head_bias, head_first, head_second = (
        value.transpose(1, 0, 2) for value in (w_qkv, mom_qkv, head_bias, head_first, head_second)
    )
    moment_qkv = MOMENTUM_DECAY * mom_qkv + red_qkv
    moment_out = MOMENTUM_DECAY * mom_out + red_out
    moment_up = MOMENTUM_DECAY * mom_up + red_up
    moment_down = MOMENTUM_DECAY * mom_down + red_down

    def widen(value):
        return jnp.pad(value.astype(BF16), ((0, 0), (0, group_width - value.shape[1])))

    chunks = (
        widen(moment_up),
        widen(moment_down.T),
        widen(moment_out.T),
        widen(jnp.concatenate([moment_qkv[j] for j in range(3)], axis=1)),
    )
    part = group_width // 2
    sent = jnp.stack(
        [
            chunks[chip * 2 + t][:, half * part : half * part + part]
            for chip in range(2)
            for half in range(2)
            for t in range(2)
        ]
    )
    sent = jnp.broadcast_to(sent[None], (count // 8,) + sent.shape)
    whole = (
        lax.all_to_all(sent.reshape(count, rows, part), AXES, 0, 0)
        .reshape(dp, tensor, rows, part)
        .transpose(1, 0, 2, 3)
        .reshape(tensor, model, part)
    )
    whole_other = swap(whole, 1, count)
    vec_second_new, vec_new = adam_update(vectors, red_vec, vec_first, vec_second)
    head_second_new, head_new = adam_update(head_bias, red_head, head_first, head_second)
    unit_second_new, unit_new = adam_update(up_bias, red_unit, unit_first, unit_second)
    grad_in = to_image(grad_in_full)
    output = to_image(output_full)
    done = (
        red_qkv,
        red_out,
        red_up,
        red_down,
        moment_qkv,
        moment_out,
        moment_up,
        moment_down,
        red_vec,
        vec_second_new,
        vec_new,
        red_head,
        head_second_new,
        head_new,
        red_unit,
        unit_second_new,
        unit_new,
    )
    whole, whole_other, done = lax.optimization_barrier((whole, whole_other, done))
    (
        red_qkv,
        red_out,
        red_up,
        red_down,
        moment_qkv,
        moment_out,
        moment_up,
        moment_down,
        red_vec,
        vec_second_new,
        vec_new,
        red_head,
        head_second_new,
        head_new,
        red_unit,
        unit_second_new,
        unit_new,
    ) = done
    near = bit_of(2)
    own = near * 2 + lax.axis_index("tensor")
    first_place = lax.axis_index("dp") - 2 * near
    place = jnp.stack([first_place, own, core]).astype(jnp.int32)
    result = ortho_call(place, whole, whole_other, rows)
    come = [result[0]] + [
        lax.ppermute(
            result[offset],
            AXES,
            [(i, i ^ ((offset & 1) | ((offset & 2) << 1))) for i in range(count)],
        )
        for offset in range(1, 4)
    ]
    pairs = jnp.stack(come).reshape(2, 2, rows, group_width)
    pairs = jnp.where(near == 0, pairs, jnp.flip(pairs, 0))
    pairs = jnp.where(here, pairs, jnp.flip(pairs, 1))
    mine = pairs.reshape(4, rows, group_width).astype(F32)
    new_up = WEIGHT_KEEP * w_up - STEP_RATES[2] * mine[0]
    new_down = WEIGHT_KEEP * w_down - STEP_RATES[3] * mine[1].T
    new_out = WEIGHT_KEEP * w_out - STEP_RATES[1] * mine[2, :, :out_width].T
    ortho_qkv = jnp.stack([mine[3, :, j * third : (j + 1) * third] for j in range(3)])
    new_qkv = WEIGHT_KEEP * w_qkv - STEP_RATES[0] * ortho_qkv
    red_qkv, moment_qkv, new_qkv, red_head, head_second_new, head_new = (
        value.transpose(1, 0, 2)
        for value in (red_qkv, moment_qkv, new_qkv, red_head, head_second_new, head_new)
    )
    return (
        output,
        grad_in,
        red_qkv,
        red_out,
        red_up,
        red_down,
        moment_qkv,
        moment_out,
        moment_up,
        moment_down,
        new_qkv,
        new_out,
        new_up,
        new_down,
        red_vec,
        vec_second_new,
        vec_new,
        red_head,
        head_second_new,
        head_new,
        red_unit,
        unit_second_new,
        unit_new,
    )


def solution(mesh):
    token = P("dp", None)
    specs = (
        P("dp", None, "tensor"),
        P("tensor", "dp"),
        P("dp", "tensor"),
        P("tensor", "dp"),
    )
    vec, head, unit = P(None, "dp"), P(None, "tensor", "dp"), P("tensor", "dp")
    return jax.shard_map(
        shards,
        mesh=mesh,
        in_specs=(token, token)
        + specs
        + (vec, head, unit)
        + specs
        + (vec, vec, head, head, unit, unit),
        out_specs=(token, token) + specs * 3 + (vec,) * 3 + (head,) * 3 + (unit,) * 3,
        check_vma=False,
    )
```

```python
from functools import partial

import jax
import jax.numpy as jnp
from jax import lax
from jax.experimental import pallas as pl
from jax.experimental.layout import Layout, with_layout_constraint
from jax.experimental.pallas import tpu as pltpu
from jax.sharding import PartitionSpec as P

HD = 64
SEQ = 1370
STEP = 10
PAD = 1408
HALF = 704
BLOCK = 704
MASKED = -1e30
LANES = 128

COEFF_A = 3.4445
COEFF_B = -4.775
COEFF_C = 2.0315
STEP_RATES = (2.7, 4.4, 2.2, 1.1)
MOMENTUM_DECAY = 0.95
WEIGHT_KEEP = 0.999
ADAM_ONE = 0.9
ADAM_TWO = 0.999
ADAM_RATE = 0.6
AXES = ("dp", "tensor")
F32 = jnp.float32
BF16 = jnp.bfloat16
NT = (((1,), (1,)), ((), ()))
TN = (((0,), (0,)), ((), ()))
VMEM_LIMIT = 56 * 1024 * 1024
QUICK = pl.CostEstimate(flops=1000, bytes_accessed=1000, transcendentals=0)


def params():
    return pltpu.CompilerParams(vmem_limit_bytes=VMEM_LIMIT)


def dot(a, b, dims=(((1,), (0,)), ((), ()))):
    return lax.dot_general(a, b, dims, preferred_element_type=F32)


def normalize(values, gain_row, shift_row):
    center = values - jnp.mean(values, axis=-1, keepdims=True)
    spread = jnp.mean(center * center, axis=-1, keepdims=True)
    return center * lax.rsqrt(spread + 1e-06) * gain_row + shift_row


def adam_update(parameter, gradient, first, second):
    first_new = ADAM_ONE * first + (1.0 - ADAM_ONE) * gradient
    second_new = ADAM_TWO * second + (1.0 - ADAM_TWO) * gradient * gradient
    first_hat = first_new / (1.0 - ADAM_ONE**STEP)
    second_hat = second_new / (1.0 - ADAM_TWO**STEP)
    return (second_new, parameter - ADAM_RATE * first_hat / (jnp.sqrt(second_hat) + 1e-08))


def three_pieces(column):
    high = column.astype(BF16)
    rest = column - high.astype(F32)
    middle = rest.astype(BF16)
    low = (rest - middle.astype(F32)).astype(BF16)
    return high.astype(F32), middle.astype(F32), low.astype(F32)


def lanes_of(rows):
    return lax.broadcasted_iota(jnp.int32, (rows, HD), 1)


def with_column(extra, rows):
    lane = lanes_of(rows)
    high, middle, low = three_pieces(extra)
    return jnp.where(lane == 1, high, jnp.where(lane == 2, middle, jnp.where(lane == 3, low, 0.0)))


def whole_spec(shape):
    return pl.BlockSpec(shape, lambda *_: (0,) * len(shape))


def upright(row, size):
    return [row[:, at : at + size] for at in range(0, row.shape[1], size)]


def flipped(pieces):
    width = pieces[0].shape[1]
    wide = -(-width // LANES) * LANES
    if wide > width:
        pieces = [jnp.concatenate([p, jnp.zeros((p.shape[0], wide - width), F32)], axis=1) for p in pieces]
    missing = 8 - sum(piece.shape[0] for piece in pieces)
    if missing:
        pieces = pieces + [jnp.zeros((missing, wide), F32)]
    return jnp.concatenate(pieces, axis=0).T


def pack_kernel(w_ref, vec_ref, head_ref, unit_ref, out_ref):
    copies, rows, width = out_ref.shape
    third = w_ref.shape[2]
    heads = [head_ref[head, part : part + 1, :] for part in range(2) for head in range(head_ref.shape[0])]
    blocks = []
    for piece, count in (
        ([vec_ref[...]], rows),
        (heads, head_ref.shape[2]),
        ([unit_ref[...]], unit_ref.shape[1]),
    ):
        column = flipped(piece)[:count, :]
        if count < rows:
            column = jnp.concatenate([column, jnp.zeros((rows - count, 8), F32)], axis=0)
        blocks.append(column)
    blocks.append(jnp.zeros((rows, width - 3 * third - 24), F32))
    packed = jnp.concatenate([w_ref[part] for part in range(3)] + blocks, axis=1).astype(BF16)
    for copy in range(copies):
        out_ref[copy] = packed


def pack_call(weights, vectors, heads, units, copies, width):
    rows = weights.shape[1]
    return pl.pallas_call(
        pack_kernel,
        out_shape=jax.ShapeDtypeStruct((copies, rows, width), BF16),
        compiler_params=params(),
        cost_estimate=QUICK,
        name="pack",
    )(weights, vectors, heads, units)


def qkv_kernel(core_ref, x_ref, w_ref, q_ref, k_ref, v_ref, vec_ref, unit_ref, bias, *, shard_rows):
    heads = q_ref.shape[0]
    width = heads * HD
    rows = x_ref.shape[0]
    model = x_ref.shape[1]
    core = core_ref[0]

    @pl.when(pl.program_id(0) == 0)
    def _():
        shards_in = model // shard_rows
        tail = 3 * width // LANES * LANES
        skip = 3 * width - tail

        def chosen(count):
            each = count // shards_in
            row = lax.broadcasted_iota(jnp.int32, (model, count), 0)
            column = lax.broadcasted_iota(jnp.int32, (model, count), 1)
            if each == shard_rows:
                source = column
            else:
                source = (column >> (each.bit_length() - 1)) * shard_rows + (column & (each - 1))
            return jnp.where(row == source, 1.0, 0.0).astype(BF16)

        vec_ref[...] = dot(w_ref[0, :, tail:], chosen(model), TN)[skip : skip + 8, :]
        bias[...] = dot(w_ref[core, :, tail:], chosen(HD), TN)[skip + 8 : skip + 16, :]
        for t in range(2):
            units = dot(w_ref[t, :, tail:], chosen(LANES), TN)[skip + 16 : skip + 24, :]
            unit_ref[t : t + 1, :] = jnp.concatenate(
                [units[j : j + 1, :] for j in range(unit_ref.shape[1] // LANES)], axis=1
            )

    normed = normalize(x_ref[...].astype(F32), vec_ref[0:1, :], vec_ref[1:2, :]).astype(BF16)
    projected = dot(normed, w_ref[core, :, : 3 * width])
    lane = lanes_of(rows)
    token = pl.program_id(0) * rows + lax.broadcasted_iota(jnp.int32, (rows, HD), 0)
    token = token + core * HALF
    token = jnp.where(token >= PAD, token - PAD, token)
    one = jnp.where(lane == 0, 1.0, 0.0)
    pieces = jnp.where((lane >= 1) & (lane <= 3), 1.0, 0.0)
    mask = jnp.where((lane == 0) & (token >= SEQ), MASKED, pieces)
    for head in range(heads):
        at = head * HD
        query = projected[:, at : at + HD] + bias[head : head + 1, :]
        key = projected[:, width + at : width + at + HD]
        value = projected[:, 2 * width + at : 2 * width + at + HD] + bias[heads + head : heads + head + 1, :]
        query = query.astype(BF16).astype(F32) * 0.125
        q_ref[head] = jnp.concatenate([query, one], axis=1).astype(BF16)
        k_ref[head] = jnp.concatenate([key, mask], axis=1).astype(BF16)
        v_ref[head] = jnp.concatenate([value, one + pieces], axis=1).astype(BF16)


def qkv_call(core, x, weights, heads, hidden, shard_rows):
    model = x.shape[1]
    out = jax.ShapeDtypeStruct((heads, PAD, LANES), BF16)
    spec = pl.BlockSpec((heads, BLOCK, LANES), lambda i, core: (0, i, 0))
    return pl.pallas_call(
        partial(qkv_kernel, shard_rows=shard_rows),
        grid_spec=pltpu.PrefetchScalarGridSpec(
            num_scalar_prefetch=1,
            grid=(PAD // BLOCK,),
            in_specs=[
                pl.BlockSpec((BLOCK, model), lambda i, core: (i, 0)),
                whole_spec(weights.shape),
            ],
            out_specs=[spec] * 3 + [whole_spec((8, model)), whole_spec((2, hidden))],
            scratch_shapes=[pltpu.VMEM((8, HD), F32)],
        ),
        out_shape=[out] * 3
        + [jax.ShapeDtypeStruct((8, model), F32), jax.ShapeDtypeStruct((2, hidden), F32)],
        compiler_params=params(),
        cost_estimate=QUICK,
        name="qkv",
    )(core, x, weights)


def attend_kernel(q_ref, k_ref, v_ref, att_ref, qs_ref):
    heads, rows, _ = q_ref.shape
    parts = []
    for head in range(heads):
        query = q_ref[head]
        scores = dot(query, k_ref[head], NT)
        largest = jnp.max(scores, axis=-1, keepdims=True)
        exponent = jnp.exp(scores - largest).astype(BF16)
        total = dot(exponent, v_ref[head])
        denominator = total[:, HD : HD + 1]
        parts.append((total[:, :HD] / denominator).astype(BF16))
        logsum = largest + jnp.log(denominator)
        extra = with_column(-logsum, rows)
        lane = lanes_of(rows)
        extra = jnp.where(lane == 0, 1.0, extra)
        qs_ref[head] = jnp.concatenate([query[:, :HD].astype(F32), extra], axis=1).astype(BF16)
    att_ref[...] = jnp.concatenate(parts, axis=1)


def attend_call(q, k, v, half):
    heads = q.shape[0]
    steps = HALF // BLOCK
    whole = pl.BlockSpec((heads, PAD, LANES), lambda i: (0, 0, 0))
    return pl.pallas_call(
        attend_kernel,
        grid=(steps,),
        in_specs=[
            pl.BlockSpec((heads, BLOCK, LANES), lambda i: (0, i + half * steps, 0)),
            whole,
            whole,
        ],
        out_specs=[
            pl.BlockSpec((BLOCK, heads * HD), lambda i: (i, 0)),
            pl.BlockSpec((heads, BLOCK, LANES), lambda i: (0, i, 0)),
        ],
        out_shape=[
            jax.ShapeDtypeStruct((HALF, heads * HD), BF16),
            jax.ShapeDtypeStruct((heads, HALF, LANES), BF16),
        ],
        compiler_params=params(),
        cost_estimate=QUICK,
        name="attend",
    )(q, k, v)


def attend_back_kernel(
    qa_ref, qb_ref, k_ref, v_ref, atta_ref, attb_ref, upa_ref, upb_ref, own_ref, other_ref, queries, upstream, total
):
    heads = k_ref.shape[0]
    rows = k_ref.shape[1]
    width = heads * HD
    step = pl.program_id(0)

    @pl.when(step == 0)
    def _():
        for at, q_ref, att_ref, up_ref in ((0, qa_ref, atta_ref, upa_ref), (HALF, qb_ref, attb_ref, upb_ref)):
            for head in range(heads):
                lanes = slice(head * HD, head * HD + HD)
                grad = up_ref[:, lanes].astype(F32)
                dots = jnp.sum(grad * att_ref[:, lanes].astype(F32), axis=1, keepdims=True)
                upstream[head, at : at + HALF, :] = jnp.concatenate(
                    [grad, with_column(-dots, HALF)], axis=1
                ).astype(BF16)
                queries[head, at : at + HALF, :] = q_ref[head]
        total[...] = jnp.zeros_like(total)

    key_parts, value_parts = [], []
    for head in range(heads):
        query, grad = queries[head], upstream[head]
        key, value = k_ref[head], v_ref[head]
        weight = jnp.exp(dot(key, query, NT))
        value_parts.append(dot(weight.astype(BF16), grad)[:, :HD].astype(BF16))
        score = (weight * dot(value, grad, NT)).astype(BF16)
        key_parts.append(dot(score, query)[:, :HD].astype(BF16))
        total[head] += dot(key, score, TN)
    per_half = HALF // rows
    pad = jnp.zeros((rows, own_ref.shape[1] - 3 * width), BF16)
    both = jnp.concatenate(key_parts + value_parts + [pad], axis=1)
    for half, out_ref in enumerate((own_ref, other_ref)):

        @pl.when(step // per_half == half)
        def _():
            out_ref[pl.ds((step % per_half) * rows, rows), width:] = both

    @pl.when(step == pl.num_programs(0) - 1)
    def _():
        for half, out_ref in enumerate((own_ref, other_ref)):
            out_ref[:, :width] = jnp.concatenate(
                [
                    (total[head, :HD, half * HALF : half * HALF + HALF] * 0.125).T.astype(BF16)
                    for head in range(heads)
                ],
                axis=1,
            )


def attend_back_call(qs, k, v, attended, upstream):
    heads = k.shape[0]
    width = heads * HD
    blocked = pl.BlockSpec((heads, BLOCK, LANES), lambda i: (0, i, 0))
    q_spec = whole_spec((heads, HALF, LANES))
    flat = whole_spec((HALF, width))
    wire = (HALF, -(-3 * width // LANES) * LANES)
    return pl.pallas_call(
        attend_back_kernel,
        grid=(PAD // BLOCK,),
        in_specs=[q_spec, q_spec, blocked, blocked, flat, flat, flat, flat],
        out_specs=[whole_spec(wire)] * 2,
        out_shape=[jax.ShapeDtypeStruct(wire, BF16)] * 2,
        scratch_shapes=[
            pltpu.VMEM((heads, PAD, LANES), BF16),
            pltpu.VMEM((heads, PAD, LANES), BF16),
            pltpu.VMEM((heads, LANES, PAD), F32),
        ],
        compiler_params=params(),
        cost_estimate=QUICK,
        name="attend_back",
    )(*qs, k, v, *attended, *upstream)


ERF_SCALE = 0.3275911
ERF_TERMS = (0.254829592, -0.284496736, 1.421413741, -1.453152027, 1.061405429)


def gelu_both(x):
    size = jnp.abs(x) * (0.5**0.5)
    bell = jnp.exp(-0.5 * x * x)
    t = 1.0 / (1.0 + ERF_SCALE * size)
    poly = t * ERF_TERMS[4] + ERF_TERMS[3]
    for term in ERF_TERMS[2::-1]:
        poly = poly * t + term
    tail = (0.5 * t) * poly * bell
    cumulative = jnp.where(x < 0, tail, 1.0 - tail)
    return x * cumulative, cumulative + x * (bell * 0.3989422804014327)


def norm_stats(values):
    center = values - jnp.mean(values, axis=-1, keepdims=True)
    inverse = lax.rsqrt(jnp.mean(center * center, axis=-1, keepdims=True) + 1e-06)
    return center * inverse, inverse


def norm_back(grad, unit, inverse, gain):
    u = gain * grad
    return inverse * (
        u - jnp.mean(u, axis=-1, keepdims=True) - unit * jnp.mean(u * unit, axis=-1, keepdims=True)
    )


def row_sum(value):
    return jnp.sum(value, axis=0, keepdims=True)


def write_wire(core_ref, totals, keep_ref, send_ref, shard_rows):
    even = core_ref[0] == 0
    for chip in range(keep_ref.shape[0]):
        at = chip * 2 * shard_rows
        for t in range(len(totals)):
            low = totals[t][at : at + shard_rows, :]
            high = totals[t][at + shard_rows : at + 2 * shard_rows, :]
            width = low.shape[1]
            keep_ref[chip, t, :, :width] = jnp.where(even, low, high).astype(BF16)
            send_ref[chip, t, :, :width] = jnp.where(even, high, low).astype(BF16)


def middle_kernel(
    core_ref, x_ref, cot_ref, mine_ref, recv_ref, w0_ref, w1_ref, vec_ref, unit_ref,
    out_ref, grad_ref, up_mine_ref, up_send_ref, keep_ref, send_ref, sums_ref, unit_sums_ref,
    total,
):
    step = pl.program_id(0)
    w_refs = (w0_ref, w1_ref)
    even = core_ref[0] == 0
    wide = unit_ref.shape[1]
    shard_rows = keep_ref.shape[2]

    @pl.when(step == 0)
    def _():
        total[...] = jnp.zeros_like(total)
        sums_ref[...] = jnp.zeros_like(sums_ref)
        unit_sums_ref[...] = jnp.zeros_like(unit_sums_ref)

    vec = vec_ref[...]
    out_shift, scale_one, gain_two = vec[2:3], vec[3:4], vec[4:5]
    shift_two, down_shift, scale_two = vec[5:6], vec[6:7], vec[7:8]
    mine, recv = mine_ref[...].astype(F32), recv_ref[...].astype(F32)
    attended = [
        jnp.where(even, mine, recv).astype(BF16),
        jnp.where(even, recv, mine).astype(BF16),
    ]
    attn_out = sum(dot(attended[t], w_refs[t][:, 2 * wide :], NT) for t in range(2)) + out_shift
    middle = x_ref[...].astype(F32) + scale_one * attn_out
    unit, inverse = norm_stats(middle)
    normed = (unit * gain_two + shift_two).astype(BF16)
    incoming = cot_ref[...].astype(F32)
    mlp_grad = scale_two * incoming
    mlp_grad_low = mlp_grad.astype(BF16)
    mlp_out = down_shift
    normed_grad = 0.0
    for t in range(2):
        preact = dot(normed, w_refs[t][:, :wide]) + unit_ref[t : t + 1, :]
        activated, slope = gelu_both(preact)
        activated = activated.astype(BF16)
        mlp_out = mlp_out + dot(activated, w_refs[t][:, wide : 2 * wide], NT)
        preact_grad = dot(mlp_grad_low, w_refs[t][:, wide : 2 * wide]) * slope
        unit_sums_ref[t : t + 1, :] += row_sum(preact_grad)
        preact_low = preact_grad.astype(BF16)
        normed_grad = normed_grad + dot(preact_low, w_refs[t][:, :wide], NT)
        total[t, :, :wide] += dot(normed, preact_low, TN)
        total[t, :, wide : 2 * wide] += dot(mlp_grad_low, activated, TN)
    out_ref[...] = (middle + scale_two * mlp_out).astype(BF16)
    middle_grad = incoming + norm_back(normed_grad, unit, inverse, gain_two)
    grad_ref[...] = middle_grad
    attn_grad = scale_one * middle_grad
    attn_grad_low = attn_grad.astype(BF16)
    sums_ref[2:3, :] += row_sum(attn_grad)
    sums_ref[3:4, :] += row_sum(middle_grad * attn_out)
    sums_ref[4:5, :] += row_sum(normed_grad * unit)
    sums_ref[5:6, :] += row_sum(normed_grad)
    sums_ref[6:7, :] += row_sum(mlp_grad)
    sums_ref[7:8, :] += row_sum(incoming * mlp_out)
    back = []
    for t in range(2):
        total[t, :, 2 * wide :] += dot(attn_grad_low, attended[t], TN)
        back.append(dot(attn_grad_low, w_refs[t][:, 2 * wide :]))
    up_mine_ref[...] = jnp.where(even, back[0], back[1]).astype(BF16)
    up_send_ref[...] = jnp.where(even, back[1], back[0]).astype(BF16)

    @pl.when(step == pl.num_programs(0) - 1)
    def _():
        write_wire(core_ref, [total.at[t] for t in range(2)], keep_ref, send_ref, shard_rows)


ROWS = 704


def middle_call(core, x, cotangent, mine, recv, weights, vectors, units, chips, shard_rows):
    model = x.shape[1]
    width = mine.shape[1]
    row = lambda w: pl.BlockSpec((ROWS, w), lambda i, core: (i, 0))
    wire = (chips, 2, shard_rows, weights[0].shape[1])
    return pl.pallas_call(
        middle_kernel,
        grid_spec=pltpu.PrefetchScalarGridSpec(
            num_scalar_prefetch=1,
            grid=(HALF // ROWS,),
            in_specs=[
                row(model),
                row(model),
                row(width),
                row(width),
                whole_spec(weights[0].shape),
                whole_spec(weights[1].shape),
                whole_spec(vectors.shape),
                whole_spec(units.shape),
            ],
            out_specs=[
                row(model),
                row(model),
                row(width),
                row(width),
                whole_spec(wire),
                whole_spec(wire),
                whole_spec(vectors.shape),
                whole_spec(units.shape),
            ],
            scratch_shapes=[pltpu.VMEM((2,) + weights[0].shape, F32)],
        ),
        out_shape=[
            jax.ShapeDtypeStruct((HALF, model), BF16),
            jax.ShapeDtypeStruct((HALF, model), F32),
            jax.ShapeDtypeStruct((HALF, width), BF16),
            jax.ShapeDtypeStruct((HALF, width), BF16),
            jax.ShapeDtypeStruct(wire, BF16),
            jax.ShapeDtypeStruct(wire, BF16),
            jax.ShapeDtypeStruct(vectors.shape, F32),
            jax.ShapeDtypeStruct(units.shape, F32),
        ],
        compiler_params=params(),
        cost_estimate=QUICK,
        name="middle",
    )(core, x, cotangent, mine, recv, *weights, vectors, units)


def last_kernel(
    core_ref, x_ref, mine_ref, recv_ref, w_ref, vec_ref, grad_ref, sums_in_ref, unit_ref,
    out_ref, keep_ref, send_ref, sums_ref, head_ref, total,
):
    step = pl.program_id(0)
    even = core_ref[0] == 0
    width = head_ref.shape[1]

    @pl.when(step == 0)
    def _():
        total[...] = jnp.zeros_like(total)
        sums_ref[...] = sums_in_ref[...]
        head_ref[...] = jnp.zeros_like(head_ref)

    gain, shift = vec_ref[0:1, :], vec_ref[1:2, :]
    unit, inverse = norm_stats(x_ref[...].astype(F32))
    normed = (unit * gain + shift).astype(BF16)
    mine, recv = mine_ref[:, :width].astype(F32), recv_ref[:, :width].astype(F32)
    normed_grad = 0.0
    for t in range(2):
        part = jnp.where(even, mine, recv) if t == 0 else jnp.where(even, recv, mine)
        head_ref[t : t + 1, :] += row_sum(part)
        part = part.astype(BF16)
        normed_grad = normed_grad + dot(part, w_ref[t, :, :width], NT)
        total[t, :, :width] += dot(normed, part, TN)
    sums_ref[0:1, :] += row_sum(normed_grad * unit)
    sums_ref[1:2, :] += row_sum(normed_grad)
    out_ref[...] = (grad_ref[...] + norm_back(normed_grad, unit, inverse, gain)).astype(BF16)

    @pl.when(step == pl.num_programs(0) - 1)
    def _():
        shard_rows = keep_ref.shape[2]
        shards_in = total.shape[1] // shard_rows
        third = width // 3
        for t in range(2):
            total[t, :, width : width + 8] = sums_ref[...].T
            heads = upright(head_ref[t : t + 1, :third], HD) + upright(
                head_ref[t : t + 1, 2 * third :], HD
            )
            units = upright(unit_ref[t : t + 1, :], LANES)
            for at, column in ((width + 8, flipped(heads)), (width + 16, flipped(units))):
                count = HD if at == width + 8 else LANES
                each = count // shards_in
                for shard in range(shards_in):
                    total[t, shard * shard_rows : shard * shard_rows + each, at : at + 8] = column[
                        shard * each : shard * each + each, :
                    ]
        write_wire(core_ref, [total.at[t] for t in range(2)], keep_ref, send_ref, shard_rows)


def last_call(core, x, mine, recv, weights, vectors, middle_grad, sums, units, heads, chips, shard_rows):
    model = x.shape[1]
    width = 3 * heads * HD
    wide = mine.shape[1]
    row = lambda w: pl.BlockSpec((ROWS, w), lambda i, core: (i, 0))
    packed = weights.shape[2]
    wire = (chips, 2, shard_rows, packed)
    return pl.pallas_call(
        last_kernel,
        grid_spec=pltpu.PrefetchScalarGridSpec(
            num_scalar_prefetch=1,
            grid=(HALF // ROWS,),
            in_specs=[
                row(model),
                row(wide),
                row(wide),
                whole_spec(weights.shape),
                whole_spec(vectors.shape),
                row(model),
                whole_spec(sums.shape),
                whole_spec(units.shape),
            ],
            out_specs=[
                row(model),
                whole_spec(wire),
                whole_spec(wire),
                whole_spec(sums.shape),
                whole_spec((2, width)),
            ],
            scratch_shapes=[pltpu.VMEM((2, model, packed), F32)],
        ),
        out_shape=[
            jax.ShapeDtypeStruct((HALF, model), BF16),
            jax.ShapeDtypeStruct(wire, BF16),
            jax.ShapeDtypeStruct(wire, BF16),
            jax.ShapeDtypeStruct(sums.shape, F32),
            jax.ShapeDtypeStruct((2, width), F32),
        ],
        compiler_params=params(),
        cost_estimate=QUICK,
        name="last",
    )(core, x, mine, recv, weights, vectors, middle_grad, sums, units)


def split_two(value):
    high = value.astype(BF16)
    return high, (value - high.astype(F32)).astype(BF16)


def left_of(value):
    high, low = split_two(value)
    return jnp.concatenate([high, high, low], axis=1)


def right_of(value):
    high, low = split_two(value)
    return jnp.concatenate([high, low, high], axis=0)


def ortho_kernel(place_ref, mine_ref, other_ref, o_ref, final):
    halves, size, wide = mine_ref.shape
    even = place_ref[2] == 0
    gram = sum(
        dot(m_ref[t], m_ref[t], NT) for m_ref in (mine_ref, other_ref) for t in range(halves)
    )
    row = lax.broadcasted_iota(jnp.int32, (size, size), 0)
    column = lax.broadcasted_iota(jnp.int32, (size, size), 1)
    eye = row == column
    square = jnp.sum(jnp.where(eye, gram, 0.0), axis=(0, 1), keepdims=True)
    scale = 1.0 / (jnp.sqrt(square) + 1e-07)
    gram = gram * scale * scale
    product = None
    for sweep_index in range(5):
        left = left_of(gram)
        poly = COEFF_B * gram + COEFF_C * dot(left, right_of(gram))
        poly = jnp.where(eye, poly + COEFF_A, poly)
        poly_left = left_of(poly)
        following = [] if product is None else [product]
        if sweep_index < 4:
            following.append(dot(left, right_of(poly)))
        following = dot(poly_left, right_of(jnp.concatenate(following, axis=1)))
        product = poly if product is None else following[:, :size]
        gram = following[:, -size:]
    shard_rows = o_ref.shape[1]
    for shard in range(final.shape[0]):
        at = shard * shard_rows
        final[shard] = product[at : at + shard_rows, :] * scale
    near = [split_two(final[place_ref[0] + 2 * chip]) for chip in range(2)]
    high, low = (jnp.concatenate([near[0][part], near[1][part]], axis=0) for part in range(2))
    for t in range(halves):
        mine, other = (dot(high, m_ref[t]) + dot(low, m_ref[t]) for m_ref in (mine_ref, other_ref))
        both = jnp.concatenate(
            [jnp.where(even, mine, other), jnp.where(even, other, mine)], axis=1
        )
        for chip in range(2):
            o_ref[place_ref[1] ^ (chip * 2 + t)] = both[
                chip * shard_rows : chip * shard_rows + shard_rows, :
            ].astype(BF16)


def ortho_call(place, mine, other, shard_rows):
    halves, size, wide = mine.shape
    out = (4, shard_rows, 2 * wide)
    return pl.pallas_call(
        ortho_kernel,
        grid_spec=pltpu.PrefetchScalarGridSpec(
            num_scalar_prefetch=1,
            grid=(1,),
            in_specs=[whole_spec(mine.shape)] * 2,
            out_specs=whole_spec(out),
            scratch_shapes=[pltpu.VMEM((size // shard_rows, shard_rows, size), F32)],
        ),
        out_shape=jax.ShapeDtypeStruct(out, BF16),
        compiler_params=params(),
        cost_estimate=QUICK,
        name="ortho",
    )(place, mine, other)


def bit_of(bit):
    index = lax.axis_index(AXES)
    return (index >> bit) & 1


def swap(value, bit, count):
    return lax.ppermute(value, AXES, [(i, i ^ (1 << bit)) for i in range(count)])


def is_home(i):
    return (i & 1) == ((i >> 1) & 1)


def home_send(value, bit, count):
    return lax.ppermute(value, AXES, [(i, i ^ (1 << bit)) for i in range(count) if is_home(i)])


def same_core(count):
    return [[i for i in range(count) if (i >> 1) & 1 == core] for core in range(2)]


def same_place(count):
    return [[i for i in range(count) if i & 3 == place] for place in range(4)]


def exchange(value, groups):
    return lax.all_to_all(value, AXES, 0, 0, axis_index_groups=groups)


def shards(
    inputs,
    cotangent,
    w_qkv,
    w_out,
    w_up,
    w_down,
    vectors,
    head_bias,
    up_bias,
    mom_qkv,
    mom_out,
    mom_up,
    mom_down,
    vec_first,
    vec_second,
    head_first,
    head_second,
    unit_first,
    unit_second,
):
    dp = lax.axis_size("dp")
    tensor = lax.axis_size("tensor")
    count = dp * tensor
    model = inputs.shape[1]
    rows = w_qkv.shape[0]
    third = w_qkv.shape[2]
    qkv_width = 3 * third
    packed_width = -(-(qkv_width + 24) // LANES) * LANES
    up_width = w_up.shape[1]
    out_width = w_out.shape[0]
    group_width = up_width
    core = lax.axis_index("dp") & 1
    home = core == lax.axis_index("tensor")

    chips = dp // 2
    even = core == 0
    core_list = core.astype(jnp.int32).reshape(1)
    core_groups, place_groups = same_core(count), same_place(count)

    def ordered(mine, other, axis):
        return jnp.where(
            even, jnp.stack([mine, other], axis=axis), jnp.stack([other, mine], axis=axis)
        )

    first_wide = pack_call(
        w_qkv.transpose(1, 0, 2), vectors, head_bias.transpose(1, 0, 2), up_bias, dp, packed_width
    )
    first_wide, inputs, cotangent, up_in, down_in, out_in = lax.optimization_barrier(
        (first_wide, inputs, cotangent, w_up, w_down, w_out)
    )
    later = jnp.concatenate(
        [up_in.astype(BF16), down_in.T.astype(BF16), out_in.T.astype(BF16)], axis=1
    )
    later_width = later.shape[1]
    here = lax.axis_index("tensor") == 0
    later_across = swap(later, 0, count)
    later_pair = jnp.where(
        here, jnp.stack([later, later_across]), jnp.stack([later_across, later])
    )
    later_wide = jnp.broadcast_to(later_pair[None], (chips,) + later_pair.shape)
    first_mine = exchange(first_wide, core_groups)
    later_part = exchange(later_wide, place_groups)

    def whole_image(value):
        value = jnp.where(home, value, home_send(value, 1, count))
        padded = jnp.pad(value, ((0, PAD - SEQ), (0, 0)))
        return jnp.where(even, padded, jnp.roll(padded, HALF, axis=0))

    image = whole_image(inputs)
    image_cotangent = whole_image(cotangent)
    image, image_cotangent = lax.optimization_barrier((image, image_cotangent))

    first_other = swap(first_mine, 1, count)
    first_shape = (chips, tensor, rows, packed_width)
    first_all = (
        ordered(first_mine.reshape(first_shape), first_other.reshape(first_shape), 1)
        .transpose(2, 0, 1, 3, 4)
        .reshape(tensor, model, packed_width)
    )
    q, k, v, vec_full, unit_shift = qkv_call(
        core_list, image, first_all, third // HD, up_width, rows
    )
    attended_other, qs_other = attend_call(q, k, v, 1)
    attended_recv = swap(attended_other, 1, count)
    attended, qs = attend_call(q, k, v, 0)

    attended, attended_recv, later_part = lax.optimization_barrier(
        (attended, attended_recv, later_part)
    )
    later_other = swap(later_part, 1, count)
    later_all = [
        ordered(later_part[:, t], later_other[:, t], 1).reshape(model, later_width)
        for t in range(tensor)
    ]

    (
        output_rows, middle_grad, up_mine, up_send, later_keep, later_send, sums, unit_sums,
    ) = middle_call(
        core_list, image, image_cotangent, attended, attended_recv, later_all, vec_full,
        unit_shift, chips, rows,
    )

    def summed(keep, send):
        return keep.astype(F32) + swap(send, 1, count).astype(F32)

    up_recv = swap(up_send, 1, count)
    later_sum = summed(later_keep, later_send).astype(BF16).reshape(-1, rows, later_width)
    later_sum, up_recv = lax.optimization_barrier((later_sum, up_recv))
    later_parts = exchange(later_sum, core_groups)

    back, back_send = attend_back_call((qs, qs_other), k, v, (attended, attended_other), (up_mine, up_recv))
    back_recv = swap(back_send, 1, count)
    grad_in_rows, first_keep, first_send, _, _ = last_call(
        core_list, image, back, back_recv, first_all, vec_full, middle_grad, sums, unit_sums,
        third // HD, chips, rows,
    )
    first_sum = summed(first_keep, first_send).astype(BF16).reshape(-1, rows, packed_width)
    first_sum, later_parts = lax.optimization_barrier((first_sum, later_parts))
    def gathered(value):
        return ordered(value, swap(value, 1, count), 0).reshape(PAD, model)[:SEQ]

    output_full, grad_in_full = gathered(output_rows), gathered(grad_in_rows)
    first_parts = exchange(first_sum, core_groups)
    first_parts, output_full, grad_in_full = lax.optimization_barrier(
        (first_parts, output_full, grad_in_full)
    )
    first_red = jnp.sum(first_parts.astype(F32), axis=0)
    red_qkv = jnp.stack(
        [first_red[:, j * third : (j + 1) * third] for j in range(3)]
    )
    red_vec = first_red[:, qkv_width : qkv_width + 8].T
    head_rows, unit_rows = head_bias.shape[2], up_bias.shape[1]
    at = qkv_width + 8
    red_head = first_red[:head_rows, at : at + 6].T.reshape(head_bias.shape).transpose(1, 0, 2)
    red_unit = with_layout_constraint(
        first_red[:unit_rows, at + 8 : at + 14].T, Layout(major_to_minor=(0, 1))
    )
    later_red = jnp.sum(later_parts.astype(F32), axis=0)
    red_up = later_red[:, :up_width]
    red_down_t = later_red[:, up_width : 2 * up_width]
    red_out_t = later_red[:, 2 * up_width :]

    red_out, red_down = red_out_t.T, red_down_t.T
    w_qkv, mom_qkv, head_bias, head_first, head_second = (
        value.transpose(1, 0, 2) for value in (w_qkv, mom_qkv, head_bias, head_first, head_second)
    )
    moment_qkv = MOMENTUM_DECAY * mom_qkv + red_qkv
    moment_out = MOMENTUM_DECAY * mom_out + red_out
    moment_up = MOMENTUM_DECAY * mom_up + red_up
    moment_down = MOMENTUM_DECAY * mom_down + red_down

    def widen(value):
        return jnp.pad(value.astype(BF16), ((0, 0), (0, group_width - value.shape[1])))

    chunks = (
        widen(moment_up),
        widen(moment_down.T),
        widen(moment_out.T),
        widen(jnp.concatenate([moment_qkv[j] for j in range(3)], axis=1)),
    )
    part = group_width // 2
    sent = jnp.stack(
        [
            chunks[chip * 2 + t][:, half * part : half * part + part]
            for chip in range(2)
            for half in range(2)
            for t in range(2)
        ]
    )
    sent = jnp.broadcast_to(sent[None], (count // 8,) + sent.shape)
    whole = (
        lax.all_to_all(sent.reshape(count, rows, part), AXES, 0, 0)
        .reshape(dp, tensor, rows, part)
        .transpose(1, 0, 2, 3)
        .reshape(tensor, model, part)
    )
    whole_other = swap(whole, 1, count)
    vec_second_new, vec_new = adam_update(vectors, red_vec, vec_first, vec_second)
    head_second_new, head_new = adam_update(head_bias, red_head, head_first, head_second)
    unit_second_new, unit_new = adam_update(up_bias, red_unit, unit_first, unit_second)
    grad_in_come = home_send(grad_in_full, 0, count)
    output_come = home_send(output_full, 0, count)
    done = (
        red_qkv,
        red_out,
        red_up,
        red_down,
        moment_qkv,
        moment_out,
        moment_up,
        moment_down,
        red_vec,
        vec_second_new,
        vec_new,
        red_head,
        head_second_new,
        head_new,
        red_unit,
        unit_second_new,
        unit_new,
    )
    whole, whole_other, done = lax.optimization_barrier((whole, whole_other, done))
    (
        red_qkv,
        red_out,
        red_up,
        red_down,
        moment_qkv,
        moment_out,
        moment_up,
        moment_down,
        red_vec,
        vec_second_new,
        vec_new,
        red_head,
        head_second_new,
        head_new,
        red_unit,
        unit_second_new,
        unit_new,
    ) = done
    near = bit_of(2)
    own = near * 2 + lax.axis_index("tensor")
    first_place = lax.axis_index("dp") - 2 * near
    place = jnp.stack([first_place, own, core]).astype(jnp.int32)
    result = ortho_call(place, whole, whole_other, rows)
    result, output_come, grad_in_come = lax.optimization_barrier(
        (result, output_come, grad_in_come)
    )
    output = jnp.where(home, output_full, output_come)
    grad_in = jnp.where(home, grad_in_full, grad_in_come)
    come = [result[0]] + [
        lax.ppermute(
            result[offset],
            AXES,
            [(i, i ^ ((offset & 1) | ((offset & 2) << 1))) for i in range(count)],
        )
        for offset in range(1, 4)
    ]
    pairs = jnp.stack(come).reshape(2, 2, rows, group_width)
    pairs = jnp.where(near == 0, pairs, jnp.flip(pairs, 0))
    pairs = jnp.where(here, pairs, jnp.flip(pairs, 1))
    mine = pairs.reshape(4, rows, group_width).astype(F32)
    new_up = WEIGHT_KEEP * w_up - STEP_RATES[2] * mine[0]
    new_down = WEIGHT_KEEP * w_down - STEP_RATES[3] * mine[1].T
    new_out = WEIGHT_KEEP * w_out - STEP_RATES[1] * mine[2, :, :out_width].T
    ortho_qkv = jnp.stack([mine[3, :, j * third : (j + 1) * third] for j in range(3)])
    new_qkv = WEIGHT_KEEP * w_qkv - STEP_RATES[0] * ortho_qkv
    red_qkv, moment_qkv, new_qkv, red_head, head_second_new, head_new = (
        value.transpose(1, 0, 2)
        for value in (red_qkv, moment_qkv, new_qkv, red_head, head_second_new, head_new)
    )
    return (
        output,
        grad_in,
        red_qkv,
        red_out,
        red_up,
        red_down,
        moment_qkv,
        moment_out,
        moment_up,
        moment_down,
        new_qkv,
        new_out,
        new_up,
        new_down,
        red_vec,
        vec_second_new,
        vec_new,
        red_head,
        head_second_new,
        head_new,
        red_unit,
        unit_second_new,
        unit_new,
    )


def solution(mesh):
    token = P("dp", None)
    specs = (
        P("dp", None, "tensor"),
        P("tensor", "dp"),
        P("dp", "tensor"),
        P("tensor", "dp"),
    )
    vec, head, unit = P(None, "dp"), P(None, "tensor", "dp"), P("tensor", "dp")
    return jax.shard_map(
        shards,
        mesh=mesh,
        in_specs=(token, token)
        + specs
        + (vec, head, unit)
        + specs
        + (vec, vec, head, head, unit, unit),
        out_specs=(token, token) + specs * 3 + (vec,) * 3 + (head,) * 3 + (unit,) * 3,
        check_vma=False,
    )
```

```python
from functools import partial

import jax
import jax.numpy as jnp
from jax import lax
from jax.experimental import pallas as pl
from jax.experimental.layout import Layout, with_layout_constraint
from jax.experimental.pallas import tpu as pltpu
from jax.sharding import PartitionSpec as P

HD = 64
SEQ = 1370
STEP = 10
PAD = 1408
HALF = 704
BLOCK = 704
MASKED = -1e30
LANES = 128

COEFF_A = 3.4445
COEFF_B = -4.775
COEFF_C = 2.0315
STEP_RATES = (2.7, 4.4, 2.2, 1.1)
MOMENTUM_DECAY = 0.95
WEIGHT_KEEP = 0.999
ADAM_ONE = 0.9
ADAM_TWO = 0.999
ADAM_RATE = 0.6
AXES = ("dp", "tensor")
F32 = jnp.float32
BF16 = jnp.bfloat16
NT = (((1,), (1,)), ((), ()))
TN = (((0,), (0,)), ((), ()))
VMEM_LIMIT = 56 * 1024 * 1024
QUICK = pl.CostEstimate(flops=1000, bytes_accessed=1000, transcendentals=0)


def params():
    return pltpu.CompilerParams(vmem_limit_bytes=VMEM_LIMIT)


def dot(a, b, dims=(((1,), (0,)), ((), ()))):
    return lax.dot_general(a, b, dims, preferred_element_type=F32)


def normalize(values, gain_row, shift_row):
    center = values - jnp.mean(values, axis=-1, keepdims=True)
    spread = jnp.mean(center * center, axis=-1, keepdims=True)
    return center * lax.rsqrt(spread + 1e-06) * gain_row + shift_row


def adam_update(parameter, gradient, first, second):
    first_new = ADAM_ONE * first + (1.0 - ADAM_ONE) * gradient
    second_new = ADAM_TWO * second + (1.0 - ADAM_TWO) * gradient * gradient
    first_hat = first_new / (1.0 - ADAM_ONE**STEP)
    second_hat = second_new / (1.0 - ADAM_TWO**STEP)
    return (second_new, parameter - ADAM_RATE * first_hat / (jnp.sqrt(second_hat) + 1e-08))


def three_pieces(column):
    high = column.astype(BF16)
    rest = column - high.astype(F32)
    middle = rest.astype(BF16)
    low = (rest - middle.astype(F32)).astype(BF16)
    return high.astype(F32), middle.astype(F32), low.astype(F32)


def lanes_of(rows):
    return lax.broadcasted_iota(jnp.int32, (rows, HD), 1)


def with_column(extra, rows):
    lane = lanes_of(rows)
    high, middle, low = three_pieces(extra)
    return jnp.where(lane == 1, high, jnp.where(lane == 2, middle, jnp.where(lane == 3, low, 0.0)))


def whole_spec(shape):
    return pl.BlockSpec(shape, lambda *_: (0,) * len(shape))


def upright(row, size):
    return [row[:, at : at + size] for at in range(0, row.shape[1], size)]


def flipped(pieces):
    width = pieces[0].shape[1]
    wide = -(-width // LANES) * LANES
    if wide > width:
        pieces = [jnp.concatenate([p, jnp.zeros((p.shape[0], wide - width), F32)], axis=1) for p in pieces]
    missing = 8 - sum(piece.shape[0] for piece in pieces)
    if missing:
        pieces = pieces + [jnp.zeros((missing, wide), F32)]
    return jnp.concatenate(pieces, axis=0).T


def pack_kernel(w_ref, vec_ref, head_ref, unit_ref, out_ref):
    copies, rows, width = out_ref.shape
    third = w_ref.shape[2]
    heads = [head_ref[head, part : part + 1, :] for part in range(2) for head in range(head_ref.shape[0])]
    blocks = []
    for piece, count in (
        ([vec_ref[...]], rows),
        (heads, head_ref.shape[2]),
        ([unit_ref[...]], unit_ref.shape[1]),
    ):
        column = flipped(piece)[:count, :]
        if count < rows:
            column = jnp.concatenate([column, jnp.zeros((rows - count, 8), F32)], axis=0)
        blocks.append(column)
    blocks.append(jnp.zeros((rows, width - 3 * third - 24), F32))
    packed = jnp.concatenate([w_ref[part] for part in range(3)] + blocks, axis=1).astype(BF16)
    for copy in range(copies):
        out_ref[copy] = packed


def pack_call(weights, vectors, heads, units, copies, width):
    rows = weights.shape[1]
    return pl.pallas_call(
        pack_kernel,
        out_shape=jax.ShapeDtypeStruct((copies, rows, width), BF16),
        compiler_params=params(),
        cost_estimate=QUICK,
        name="pack",
    )(weights, vectors, heads, units)


def qkv_kernel(core_ref, x_ref, w_ref, q_ref, k_ref, v_ref, vec_ref, unit_ref, bias, *, shard_rows):
    heads = q_ref.shape[0]
    width = heads * HD
    rows = x_ref.shape[0]
    model = x_ref.shape[1]
    core = core_ref[0]

    @pl.when(pl.program_id(0) == 0)
    def _():
        shards_in = model // shard_rows
        tail = 3 * width // LANES * LANES
        skip = 3 * width - tail

        def chosen(count):
            each = count // shards_in
            row = lax.broadcasted_iota(jnp.int32, (model, count), 0)
            column = lax.broadcasted_iota(jnp.int32, (model, count), 1)
            if each == shard_rows:
                source = column
            else:
                source = (column >> (each.bit_length() - 1)) * shard_rows + (column & (each - 1))
            return jnp.where(row == source, 1.0, 0.0).astype(BF16)

        vec_ref[...] = dot(w_ref[0, :, tail:], chosen(model), TN)[skip : skip + 8, :]
        bias[...] = dot(w_ref[core, :, tail:], chosen(HD), TN)[skip + 8 : skip + 16, :]
        for t in range(2):
            units = dot(w_ref[t, :, tail:], chosen(LANES), TN)[skip + 16 : skip + 24, :]
            unit_ref[t : t + 1, :] = jnp.concatenate(
                [units[j : j + 1, :] for j in range(unit_ref.shape[1] // LANES)], axis=1
            )

    normed = normalize(x_ref[...].astype(F32), vec_ref[0:1, :], vec_ref[1:2, :]).astype(BF16)
    projected = dot(normed, w_ref[core, :, : 3 * width])
    lane = lanes_of(rows)
    token = pl.program_id(0) * rows + lax.broadcasted_iota(jnp.int32, (rows, HD), 0)
    token = token + core * HALF
    token = jnp.where(token >= PAD, token - PAD, token)
    one = jnp.where(lane == 0, 1.0, 0.0)
    pieces = jnp.where((lane >= 1) & (lane <= 3), 1.0, 0.0)
    mask = jnp.where((lane == 0) & (token >= SEQ), MASKED, pieces)
    for head in range(heads):
        at = head * HD
        query = projected[:, at : at + HD] + bias[head : head + 1, :]
        key = projected[:, width + at : width + at + HD]
        value = projected[:, 2 * width + at : 2 * width + at + HD] + bias[heads + head : heads + head + 1, :]
        query = query.astype(BF16).astype(F32) * 0.125
        q_ref[head] = jnp.concatenate([query, one], axis=1).astype(BF16)
        k_ref[head] = jnp.concatenate([key, mask], axis=1).astype(BF16)
        v_ref[head] = jnp.concatenate([value, one + pieces], axis=1).astype(BF16)


def qkv_call(core, x, weights, heads, hidden, shard_rows):
    model = x.shape[1]
    out = jax.ShapeDtypeStruct((heads, PAD, LANES), BF16)
    spec = pl.BlockSpec((heads, BLOCK, LANES), lambda i, core: (0, i, 0))
    return pl.pallas_call(
        partial(qkv_kernel, shard_rows=shard_rows),
        grid_spec=pltpu.PrefetchScalarGridSpec(
            num_scalar_prefetch=1,
            grid=(PAD // BLOCK,),
            in_specs=[
                pl.BlockSpec((BLOCK, model), lambda i, core: (i, 0)),
                whole_spec(weights.shape),
            ],
            out_specs=[spec] * 3 + [whole_spec((8, model)), whole_spec((2, hidden))],
            scratch_shapes=[pltpu.VMEM((8, HD), F32)],
        ),
        out_shape=[out] * 3
        + [jax.ShapeDtypeStruct((8, model), F32), jax.ShapeDtypeStruct((2, hidden), F32)],
        compiler_params=params(),
        cost_estimate=QUICK,
        name="qkv",
    )(core, x, weights)


def attend_kernel(q_ref, k_ref, v_ref, att_ref, qs_ref):
    heads, rows, _ = q_ref.shape
    parts = []
    for head in range(heads):
        query = q_ref[head]
        scores = dot(query, k_ref[head], NT)
        largest = jnp.max(scores, axis=-1, keepdims=True)
        exponent = jnp.exp(scores - largest).astype(BF16)
        total = dot(exponent, v_ref[head])
        denominator = total[:, HD : HD + 1]
        parts.append((total[:, :HD] / denominator).astype(BF16))
        logsum = largest + jnp.log(denominator)
        extra = with_column(-logsum, rows)
        lane = lanes_of(rows)
        extra = jnp.where(lane == 0, 1.0, extra)
        qs_ref[head] = jnp.concatenate([query[:, :HD].astype(F32), extra], axis=1).astype(BF16)
    att_ref[...] = jnp.concatenate(parts, axis=1)


def attend_call(q, k, v, half):
    heads = q.shape[0]
    steps = HALF // BLOCK
    whole = pl.BlockSpec((heads, PAD, LANES), lambda i: (0, 0, 0))
    return pl.pallas_call(
        attend_kernel,
        grid=(steps,),
        in_specs=[
            pl.BlockSpec((heads, BLOCK, LANES), lambda i: (0, i + half * steps, 0)),
            whole,
            whole,
        ],
        out_specs=[
            pl.BlockSpec((BLOCK, heads * HD), lambda i: (i, 0)),
            pl.BlockSpec((heads, BLOCK, LANES), lambda i: (0, i, 0)),
        ],
        out_shape=[
            jax.ShapeDtypeStruct((HALF, heads * HD), BF16),
            jax.ShapeDtypeStruct((heads, HALF, LANES), BF16),
        ],
        compiler_params=params(),
        cost_estimate=QUICK,
        name="attend",
    )(q, k, v)


def attend_back_kernel(
    qa_ref, qb_ref, k_ref, v_ref, atta_ref, attb_ref, upa_ref, upb_ref, own_ref, other_ref, queries, upstream, total
):
    heads = k_ref.shape[0]
    rows = k_ref.shape[1]
    width = heads * HD
    step = pl.program_id(0)

    @pl.when(step == 0)
    def _():
        for at, q_ref, att_ref, up_ref in ((0, qa_ref, atta_ref, upa_ref), (HALF, qb_ref, attb_ref, upb_ref)):
            for head in range(heads):
                lanes = slice(head * HD, head * HD + HD)
                grad = up_ref[:, lanes].astype(F32)
                dots = jnp.sum(grad * att_ref[:, lanes].astype(F32), axis=1, keepdims=True)
                upstream[head, at : at + HALF, :] = jnp.concatenate(
                    [grad, with_column(-dots, HALF)], axis=1
                ).astype(BF16)
                queries[head, at : at + HALF, :] = q_ref[head]
        total[...] = jnp.zeros_like(total)

    key_parts, value_parts = [], []
    for head in range(heads):
        query, grad = queries[head], upstream[head]
        key, value = k_ref[head], v_ref[head]
        weight = jnp.exp(dot(key, query, NT))
        value_parts.append(dot(weight.astype(BF16), grad)[:, :HD].astype(BF16))
        score = (weight * dot(value, grad, NT)).astype(BF16)
        key_parts.append(dot(score, query)[:, :HD].astype(BF16))
        total[head] += dot(key, score, TN)
    per_half = HALF // rows
    pad = jnp.zeros((rows, own_ref.shape[1] - 3 * width), BF16)
    both = jnp.concatenate(key_parts + value_parts + [pad], axis=1)
    for half, out_ref in enumerate((own_ref, other_ref)):

        @pl.when(step // per_half == half)
        def _():
            out_ref[pl.ds((step % per_half) * rows, rows), width:] = both

    @pl.when(step == pl.num_programs(0) - 1)
    def _():
        for half, out_ref in enumerate((own_ref, other_ref)):
            out_ref[:, :width] = jnp.concatenate(
                [
                    (total[head, :HD, half * HALF : half * HALF + HALF] * 0.125).T.astype(BF16)
                    for head in range(heads)
                ],
                axis=1,
            )


def attend_back_call(qs, k, v, attended, upstream):
    heads = k.shape[0]
    width = heads * HD
    blocked = pl.BlockSpec((heads, BLOCK, LANES), lambda i: (0, i, 0))
    q_spec = whole_spec((heads, HALF, LANES))
    flat = whole_spec((HALF, width))
    wire = (HALF, -(-3 * width // LANES) * LANES)
    return pl.pallas_call(
        attend_back_kernel,
        grid=(PAD // BLOCK,),
        in_specs=[q_spec, q_spec, blocked, blocked, flat, flat, flat, flat],
        out_specs=[whole_spec(wire)] * 2,
        out_shape=[jax.ShapeDtypeStruct(wire, BF16)] * 2,
        scratch_shapes=[
            pltpu.VMEM((heads, PAD, LANES), BF16),
            pltpu.VMEM((heads, PAD, LANES), BF16),
            pltpu.VMEM((heads, LANES, PAD), F32),
        ],
        compiler_params=params(),
        cost_estimate=QUICK,
        name="attend_back",
    )(*qs, k, v, *attended, *upstream)


ERF_SCALE = 0.3275911
ERF_TERMS = (0.254829592, -0.284496736, 1.421413741, -1.453152027, 1.061405429)


def gelu_both(x):
    size = jnp.abs(x) * (0.5**0.5)
    bell = jnp.exp(-0.5 * x * x)
    t = 1.0 / (1.0 + ERF_SCALE * size)
    poly = t * ERF_TERMS[4] + ERF_TERMS[3]
    for term in ERF_TERMS[2::-1]:
        poly = poly * t + term
    tail = (0.5 * t) * poly * bell
    cumulative = jnp.where(x < 0, tail, 1.0 - tail)
    return x * cumulative, cumulative + x * (bell * 0.3989422804014327)


def norm_stats(values):
    center = values - jnp.mean(values, axis=-1, keepdims=True)
    inverse = lax.rsqrt(jnp.mean(center * center, axis=-1, keepdims=True) + 1e-06)
    return center * inverse, inverse


def norm_back(grad, unit, inverse, gain):
    u = gain * grad
    return inverse * (
        u - jnp.mean(u, axis=-1, keepdims=True) - unit * jnp.mean(u * unit, axis=-1, keepdims=True)
    )


def row_sum(value):
    return jnp.sum(value, axis=0, keepdims=True)


def write_wire(core_ref, totals, keep_ref, send_ref, shard_rows):
    even = core_ref[0] == 0
    for chip in range(keep_ref.shape[0]):
        at = chip * 2 * shard_rows
        for t in range(len(totals)):
            low = totals[t][at : at + shard_rows, :]
            high = totals[t][at + shard_rows : at + 2 * shard_rows, :]
            width = low.shape[1]
            keep_ref[chip, t, :, :width] = jnp.where(even, low, high).astype(BF16)
            send_ref[chip, t, :, :width] = jnp.where(even, high, low).astype(BF16)


def middle_kernel(
    core_ref, x_ref, cot_ref, mine_ref, recv_ref, w0_ref, w1_ref, vec_ref, unit_ref,
    out_ref, grad_ref, up_mine_ref, up_send_ref, keep_ref, send_ref, sums_ref, unit_sums_ref,
    total,
):
    step = pl.program_id(0)
    w_refs = (w0_ref, w1_ref)
    even = core_ref[0] == 0
    wide = unit_ref.shape[1]
    shard_rows = keep_ref.shape[2]

    @pl.when(step == 0)
    def _():
        total[...] = jnp.zeros_like(total)
        sums_ref[...] = jnp.zeros_like(sums_ref)
        unit_sums_ref[...] = jnp.zeros_like(unit_sums_ref)

    vec = vec_ref[...]
    out_shift, scale_one, gain_two = vec[2:3], vec[3:4], vec[4:5]
    shift_two, down_shift, scale_two = vec[5:6], vec[6:7], vec[7:8]
    mine, recv = mine_ref[...].astype(F32), recv_ref[...].astype(F32)
    attended = [
        jnp.where(even, mine, recv).astype(BF16),
        jnp.where(even, recv, mine).astype(BF16),
    ]
    attn_out = sum(dot(attended[t], w_refs[t][:, 2 * wide :], NT) for t in range(2)) + out_shift
    middle = x_ref[...].astype(F32) + scale_one * attn_out
    unit, inverse = norm_stats(middle)
    normed = (unit * gain_two + shift_two).astype(BF16)
    incoming = cot_ref[...].astype(F32)
    mlp_grad = scale_two * incoming
    mlp_grad_low = mlp_grad.astype(BF16)
    mlp_out = down_shift
    normed_grad = 0.0
    for t in range(2):
        preact = dot(normed, w_refs[t][:, :wide]) + unit_ref[t : t + 1, :]
        activated, slope = gelu_both(preact)
        activated = activated.astype(BF16)
        mlp_out = mlp_out + dot(activated, w_refs[t][:, wide : 2 * wide], NT)
        preact_grad = dot(mlp_grad_low, w_refs[t][:, wide : 2 * wide]) * slope
        unit_sums_ref[t : t + 1, :] += row_sum(preact_grad)
        preact_low = preact_grad.astype(BF16)
        normed_grad = normed_grad + dot(preact_low, w_refs[t][:, :wide], NT)
        total[t, :, :wide] += dot(normed, preact_low, TN)
        total[t, :, wide : 2 * wide] += dot(mlp_grad_low, activated, TN)
    out_ref[...] = (middle + scale_two * mlp_out).astype(BF16)
    middle_grad = incoming + norm_back(normed_grad, unit, inverse, gain_two)
    grad_ref[...] = middle_grad
    attn_grad = scale_one * middle_grad
    attn_grad_low = attn_grad.astype(BF16)
    sums_ref[2:3, :] += row_sum(attn_grad)
    sums_ref[3:4, :] += row_sum(middle_grad * attn_out)
    sums_ref[4:5, :] += row_sum(normed_grad * unit)
    sums_ref[5:6, :] += row_sum(normed_grad)
    sums_ref[6:7, :] += row_sum(mlp_grad)
    sums_ref[7:8, :] += row_sum(incoming * mlp_out)
    back = []
    for t in range(2):
        total[t, :, 2 * wide :] += dot(attn_grad_low, attended[t], TN)
        back.append(dot(attn_grad_low, w_refs[t][:, 2 * wide :]))
    up_mine_ref[...] = jnp.where(even, back[0], back[1]).astype(BF16)
    up_send_ref[...] = jnp.where(even, back[1], back[0]).astype(BF16)

    @pl.when(step == pl.num_programs(0) - 1)
    def _():
        write_wire(core_ref, [total.at[t] for t in range(2)], keep_ref, send_ref, shard_rows)


ROWS = 704


def middle_call(core, x, cotangent, mine, recv, weights, vectors, units, chips, shard_rows):
    model = x.shape[1]
    width = mine.shape[1]
    row = lambda w: pl.BlockSpec((ROWS, w), lambda i, core: (i, 0))
    wire = (chips, 2, shard_rows, weights[0].shape[1])
    return pl.pallas_call(
        middle_kernel,
        grid_spec=pltpu.PrefetchScalarGridSpec(
            num_scalar_prefetch=1,
            grid=(HALF // ROWS,),
            in_specs=[
                row(model),
                row(model),
                row(width),
                row(width),
                whole_spec(weights[0].shape),
                whole_spec(weights[1].shape),
                whole_spec(vectors.shape),
                whole_spec(units.shape),
            ],
            out_specs=[
                row(model),
                row(model),
                row(width),
                row(width),
                whole_spec(wire),
                whole_spec(wire),
                whole_spec(vectors.shape),
                whole_spec(units.shape),
            ],
            scratch_shapes=[pltpu.VMEM((2,) + weights[0].shape, F32)],
        ),
        out_shape=[
            jax.ShapeDtypeStruct((HALF, model), BF16),
            jax.ShapeDtypeStruct((HALF, model), F32),
            jax.ShapeDtypeStruct((HALF, width), BF16),
            jax.ShapeDtypeStruct((HALF, width), BF16),
            jax.ShapeDtypeStruct(wire, BF16),
            jax.ShapeDtypeStruct(wire, BF16),
            jax.ShapeDtypeStruct(vectors.shape, F32),
            jax.ShapeDtypeStruct(units.shape, F32),
        ],
        compiler_params=params(),
        cost_estimate=QUICK,
        name="middle",
    )(core, x, cotangent, mine, recv, *weights, vectors, units)


def last_kernel(
    core_ref, x_ref, mine_ref, recv_ref, w_ref, vec_ref, grad_ref, sums_in_ref, unit_ref,
    out_ref, keep_ref, send_ref, sums_ref, head_ref, total,
):
    step = pl.program_id(0)
    even = core_ref[0] == 0
    width = head_ref.shape[1]

    @pl.when(step == 0)
    def _():
        total[...] = jnp.zeros_like(total)
        sums_ref[...] = sums_in_ref[...]
        head_ref[...] = jnp.zeros_like(head_ref)

    gain, shift = vec_ref[0:1, :], vec_ref[1:2, :]
    unit, inverse = norm_stats(x_ref[...].astype(F32))
    normed = (unit * gain + shift).astype(BF16)
    mine, recv = mine_ref[:, :width].astype(F32), recv_ref[:, :width].astype(F32)
    normed_grad = 0.0
    for t in range(2):
        part = jnp.where(even, mine, recv) if t == 0 else jnp.where(even, recv, mine)
        head_ref[t : t + 1, :] += row_sum(part)
        part = part.astype(BF16)
        normed_grad = normed_grad + dot(part, w_ref[t, :, :width], NT)
        total[t, :, :width] += dot(normed, part, TN)
    sums_ref[0:1, :] += row_sum(normed_grad * unit)
    sums_ref[1:2, :] += row_sum(normed_grad)
    out_ref[...] = (grad_ref[...] + norm_back(normed_grad, unit, inverse, gain)).astype(BF16)

    @pl.when(step == pl.num_programs(0) - 1)
    def _():
        shard_rows = keep_ref.shape[2]
        shards_in = total.shape[1] // shard_rows
        third = width // 3
        for t in range(2):
            total[t, :, width : width + 8] = sums_ref[...].T
            heads = upright(head_ref[t : t + 1, :third], HD) + upright(
                head_ref[t : t + 1, 2 * third :], HD
            )
            units = upright(unit_ref[t : t + 1, :], LANES)
            for at, column in ((width + 8, flipped(heads)), (width + 16, flipped(units))):
                count = HD if at == width + 8 else LANES
                each = count // shards_in
                for shard in range(shards_in):
                    total[t, shard * shard_rows : shard * shard_rows + each, at : at + 8] = column[
                        shard * each : shard * each + each, :
                    ]
        write_wire(core_ref, [total.at[t] for t in range(2)], keep_ref, send_ref, shard_rows)


def last_call(core, x, mine, recv, weights, vectors, middle_grad, sums, units, heads, chips, shard_rows):
    model = x.shape[1]
    width = 3 * heads * HD
    wide = mine.shape[1]
    row = lambda w: pl.BlockSpec((ROWS, w), lambda i, core: (i, 0))
    packed = weights.shape[2]
    wire = (chips, 2, shard_rows, packed)
    return pl.pallas_call(
        last_kernel,
        grid_spec=pltpu.PrefetchScalarGridSpec(
            num_scalar_prefetch=1,
            grid=(HALF // ROWS,),
            in_specs=[
                row(model),
                row(wide),
                row(wide),
                whole_spec(weights.shape),
                whole_spec(vectors.shape),
                row(model),
                whole_spec(sums.shape),
                whole_spec(units.shape),
            ],
            out_specs=[
                row(model),
                whole_spec(wire),
                whole_spec(wire),
                whole_spec(sums.shape),
                whole_spec((2, width)),
            ],
            scratch_shapes=[pltpu.VMEM((2, model, packed), F32)],
        ),
        out_shape=[
            jax.ShapeDtypeStruct((HALF, model), BF16),
            jax.ShapeDtypeStruct(wire, BF16),
            jax.ShapeDtypeStruct(wire, BF16),
            jax.ShapeDtypeStruct(sums.shape, F32),
            jax.ShapeDtypeStruct((2, width), F32),
        ],
        compiler_params=params(),
        cost_estimate=QUICK,
        name="last",
    )(core, x, mine, recv, weights, vectors, middle_grad, sums, units)


def split_two(value):
    high = value.astype(BF16)
    return high, (value - high.astype(F32)).astype(BF16)


def left_of(value):
    high, low = split_two(value)
    return jnp.concatenate([high, high, low], axis=1)


def right_of(value):
    high, low = split_two(value)
    return jnp.concatenate([high, low, high], axis=0)


def ortho_kernel(place_ref, mine_ref, other_ref, o0_ref, o1_ref, o2_ref, o3_ref, final, pieces):
    halves, size, wide = mine_ref.shape
    even = place_ref[2] == 0
    gram = sum(
        dot(m_ref[t], m_ref[t], NT) for m_ref in (mine_ref, other_ref) for t in range(halves)
    )
    row = lax.broadcasted_iota(jnp.int32, (size, size), 0)
    column = lax.broadcasted_iota(jnp.int32, (size, size), 1)
    eye = row == column
    square = jnp.sum(jnp.where(eye, gram, 0.0), axis=(0, 1), keepdims=True)
    scale = 1.0 / (jnp.sqrt(square) + 1e-07)
    gram = gram * scale * scale
    product = None
    for sweep_index in range(5):
        left = left_of(gram)
        poly = COEFF_B * gram + COEFF_C * dot(left, right_of(gram))
        poly = jnp.where(eye, poly + COEFF_A, poly)
        poly_left = left_of(poly)
        following = [] if product is None else [product]
        if sweep_index < 4:
            following.append(dot(left, right_of(poly)))
        following = dot(poly_left, right_of(jnp.concatenate(following, axis=1)))
        product = poly if product is None else following[:, :size]
        gram = following[:, -size:]
    shard_rows = o0_ref.shape[0]
    for shard in range(final.shape[0]):
        at = shard * shard_rows
        final[shard] = product[at : at + shard_rows, :] * scale
    near = [split_two(final[place_ref[0] + 2 * chip]) for chip in range(2)]
    high, low = (jnp.concatenate([near[0][part], near[1][part]], axis=0) for part in range(2))
    for t in range(halves):
        mine, other = (dot(high, m_ref[t]) + dot(low, m_ref[t]) for m_ref in (mine_ref, other_ref))
        both = jnp.concatenate(
            [jnp.where(even, mine, other), jnp.where(even, other, mine)], axis=1
        )
        for chip in range(2):
            pieces[chip * 2 + t] = both[chip * shard_rows : chip * shard_rows + shard_rows, :]
    for offset, o_ref in enumerate((o0_ref, o1_ref, o2_ref, o3_ref)):
        o_ref[...] = pieces[place_ref[1] ^ offset].astype(BF16)


def ortho_call(place, mine, other, shard_rows):
    halves, size, wide = mine.shape
    out = (shard_rows, 2 * wide)
    return pl.pallas_call(
        ortho_kernel,
        grid_spec=pltpu.PrefetchScalarGridSpec(
            num_scalar_prefetch=1,
            grid=(1,),
            in_specs=[whole_spec(mine.shape)] * 2,
            out_specs=[whole_spec(out)] * 4,
            scratch_shapes=[
                pltpu.VMEM((size // shard_rows, shard_rows, size), F32),
                pltpu.VMEM((4,) + out, F32),
            ],
        ),
        out_shape=[jax.ShapeDtypeStruct(out, BF16)] * 4,
        compiler_params=params(),
        cost_estimate=QUICK,
        name="ortho",
    )(place, mine, other)


def bit_of(bit):
    index = lax.axis_index(AXES)
    return (index >> bit) & 1


def swap(value, bit, count):
    return lax.ppermute(value, AXES, [(i, i ^ (1 << bit)) for i in range(count)])


def is_home(i):
    return (i & 1) == ((i >> 1) & 1)


def home_send(value, bit, count):
    return lax.ppermute(value, AXES, [(i, i ^ (1 << bit)) for i in range(count) if is_home(i)])


def same_core(count):
    return [[i for i in range(count) if (i >> 1) & 1 == core] for core in range(2)]


def same_place(count):
    return [[i for i in range(count) if i & 3 == place] for place in range(4)]


def exchange(value, groups):
    return lax.all_to_all(value, AXES, 0, 0, axis_index_groups=groups)


def shards(
    inputs,
    cotangent,
    w_qkv,
    w_out,
    w_up,
    w_down,
    vectors,
    head_bias,
    up_bias,
    mom_qkv,
    mom_out,
    mom_up,
    mom_down,
    vec_first,
    vec_second,
    head_first,
    head_second,
    unit_first,
    unit_second,
):
    dp = lax.axis_size("dp")
    tensor = lax.axis_size("tensor")
    count = dp * tensor
    model = inputs.shape[1]
    rows = w_qkv.shape[0]
    third = w_qkv.shape[2]
    qkv_width = 3 * third
    packed_width = -(-(qkv_width + 24) // LANES) * LANES
    up_width = w_up.shape[1]
    out_width = w_out.shape[0]
    group_width = up_width
    core = lax.axis_index("dp") & 1
    home = core == lax.axis_index("tensor")

    chips = dp // 2
    even = core == 0
    core_list = core.astype(jnp.int32).reshape(1)
    core_groups, place_groups = same_core(count), same_place(count)

    def ordered(mine, other, axis):
        return jnp.where(
            even, jnp.stack([mine, other], axis=axis), jnp.stack([other, mine], axis=axis)
        )

    first_wide = pack_call(
        w_qkv.transpose(1, 0, 2), vectors, head_bias.transpose(1, 0, 2), up_bias, dp, packed_width
    )
    first_wide, inputs, cotangent, up_in, down_in, out_in = lax.optimization_barrier(
        (first_wide, inputs, cotangent, w_up, w_down, w_out)
    )
    later = jnp.concatenate(
        [up_in.astype(BF16), down_in.T.astype(BF16), out_in.T.astype(BF16)], axis=1
    )
    later_width = later.shape[1]
    here = lax.axis_index("tensor") == 0
    later_across = swap(later, 0, count)
    later_pair = jnp.where(
        here, jnp.stack([later, later_across]), jnp.stack([later_across, later])
    )
    later_wide = jnp.broadcast_to(later_pair[None], (chips,) + later_pair.shape)
    first_mine = exchange(first_wide, core_groups)
    later_part = exchange(later_wide, place_groups)

    def whole_image(value):
        value = jnp.where(home, value, home_send(value, 1, count))
        padded = jnp.pad(value, ((0, PAD - SEQ), (0, 0)))
        return jnp.where(even, padded, jnp.roll(padded, HALF, axis=0))

    image = whole_image(inputs)
    image_cotangent = whole_image(cotangent)
    image, image_cotangent = lax.optimization_barrier((image, image_cotangent))

    first_other = swap(first_mine, 1, count)
    first_shape = (chips, tensor, rows, packed_width)
    first_all = (
        ordered(first_mine.reshape(first_shape), first_other.reshape(first_shape), 1)
        .transpose(2, 0, 1, 3, 4)
        .reshape(tensor, model, packed_width)
    )
    q, k, v, vec_full, unit_shift = qkv_call(
        core_list, image, first_all, third // HD, up_width, rows
    )
    attended_other, qs_other = attend_call(q, k, v, 1)
    attended_recv = swap(attended_other, 1, count)
    attended, qs = attend_call(q, k, v, 0)

    attended, attended_recv, later_part = lax.optimization_barrier(
        (attended, attended_recv, later_part)
    )
    later_other = swap(later_part, 1, count)
    later_all = [
        ordered(later_part[:, t], later_other[:, t], 1).reshape(model, later_width)
        for t in range(tensor)
    ]

    (
        output_rows, middle_grad, up_mine, up_send, later_keep, later_send, sums, unit_sums,
    ) = middle_call(
        core_list, image, image_cotangent, attended, attended_recv, later_all, vec_full,
        unit_shift, chips, rows,
    )

    def summed(keep, send):
        return keep.astype(F32) + swap(send, 1, count).astype(F32)

    up_recv = swap(up_send, 1, count)
    later_sum = summed(later_keep, later_send).astype(BF16).reshape(-1, rows, later_width)
    later_sum, up_recv = lax.optimization_barrier((later_sum, up_recv))
    later_parts = exchange(later_sum, core_groups)

    back, back_send = attend_back_call((qs, qs_other), k, v, (attended, attended_other), (up_mine, up_recv))
    back_recv = swap(back_send, 1, count)
    grad_in_rows, first_keep, first_send, _, _ = last_call(
        core_list, image, back, back_recv, first_all, vec_full, middle_grad, sums, unit_sums,
        third // HD, chips, rows,
    )
    first_sum = summed(first_keep, first_send).astype(BF16).reshape(-1, rows, packed_width)
    first_sum, later_parts = lax.optimization_barrier((first_sum, later_parts))
    def gathered(value):
        return ordered(value, swap(value, 1, count), 0).reshape(PAD, model)[:SEQ]

    output_full, grad_in_full = gathered(output_rows), gathered(grad_in_rows)
    first_parts = exchange(first_sum, core_groups)
    first_parts, output_full, grad_in_full = lax.optimization_barrier(
        (first_parts, output_full, grad_in_full)
    )
    first_red = jnp.sum(first_parts.astype(F32), axis=0)
    red_qkv = jnp.stack(
        [first_red[:, j * third : (j + 1) * third] for j in range(3)]
    )
    red_vec = first_red[:, qkv_width : qkv_width + 8].T
    head_rows, unit_rows = head_bias.shape[2], up_bias.shape[1]
    at = qkv_width + 8
    red_head = first_red[:head_rows, at : at + 6].T.reshape(head_bias.shape).transpose(1, 0, 2)
    red_unit = with_layout_constraint(
        first_red[:unit_rows, at + 8 : at + 14].T, Layout(major_to_minor=(0, 1))
    )
    later_red = jnp.sum(later_parts.astype(F32), axis=0)
    red_up = later_red[:, :up_width]
    red_down_t = later_red[:, up_width : 2 * up_width]
    red_out_t = later_red[:, 2 * up_width :]

    red_out, red_down = red_out_t.T, red_down_t.T
    w_qkv, mom_qkv, head_bias, head_first, head_second = (
        value.transpose(1, 0, 2) for value in (w_qkv, mom_qkv, head_bias, head_first, head_second)
    )
    moment_qkv = MOMENTUM_DECAY * mom_qkv + red_qkv
    moment_out = MOMENTUM_DECAY * mom_out + red_out
    moment_up = MOMENTUM_DECAY * mom_up + red_up
    moment_down = MOMENTUM_DECAY * mom_down + red_down

    def widen(value):
        return jnp.pad(value.astype(BF16), ((0, 0), (0, group_width - value.shape[1])))

    chunks = (
        widen(moment_up),
        widen(moment_down.T),
        widen(moment_out.T),
        widen(jnp.concatenate([moment_qkv[j] for j in range(3)], axis=1)),
    )
    part = group_width // 2
    sent = jnp.stack(
        [
            chunks[chip * 2 + t][:, half * part : half * part + part]
            for chip in range(2)
            for half in range(2)
            for t in range(2)
        ]
    )
    sent = jnp.broadcast_to(sent[None], (count // 8,) + sent.shape)
    whole = (
        lax.all_to_all(sent.reshape(count, rows, part), AXES, 0, 0)
        .reshape(dp, tensor, rows, part)
        .transpose(1, 0, 2, 3)
        .reshape(tensor, model, part)
    )
    whole_other = swap(whole, 1, count)
    vec_second_new, vec_new = adam_update(vectors, red_vec, vec_first, vec_second)
    head_second_new, head_new = adam_update(head_bias, red_head, head_first, head_second)
    unit_second_new, unit_new = adam_update(up_bias, red_unit, unit_first, unit_second)
    grad_in_come = home_send(grad_in_full, 0, count)
    output_come = home_send(output_full, 0, count)
    done = (
        red_qkv,
        red_out,
        red_up,
        red_down,
        moment_qkv,
        moment_out,
        moment_up,
        moment_down,
        red_vec,
        vec_second_new,
        vec_new,
        red_head,
        head_second_new,
        head_new,
        red_unit,
        unit_second_new,
        unit_new,
    )
    whole, whole_other, done = lax.optimization_barrier((whole, whole_other, done))
    (
        red_qkv,
        red_out,
        red_up,
        red_down,
        moment_qkv,
        moment_out,
        moment_up,
        moment_down,
        red_vec,
        vec_second_new,
        vec_new,
        red_head,
        head_second_new,
        head_new,
        red_unit,
        unit_second_new,
        unit_new,
    ) = done
    near = bit_of(2)
    own = near * 2 + lax.axis_index("tensor")
    first_place = lax.axis_index("dp") - 2 * near
    place = jnp.stack([first_place, own, core]).astype(jnp.int32)
    result = ortho_call(place, whole, whole_other, rows)
    result, output_come, grad_in_come = lax.optimization_barrier(
        (result, output_come, grad_in_come)
    )
    output = jnp.where(home, output_full, output_come)
    grad_in = jnp.where(home, grad_in_full, grad_in_come)
    come = [result[0]] + [
        lax.ppermute(
            result[offset],
            AXES,
            [(i, i ^ ((offset & 1) | ((offset & 2) << 1))) for i in range(count)],
        )
        for offset in range(1, 4)
    ]
    pairs = jnp.stack(come).reshape(2, 2, rows, group_width)
    pairs = jnp.where(near == 0, pairs, jnp.flip(pairs, 0))
    pairs = jnp.where(here, pairs, jnp.flip(pairs, 1))
    mine = pairs.reshape(4, rows, group_width).astype(F32)
    new_up = WEIGHT_KEEP * w_up - STEP_RATES[2] * mine[0]
    new_down = WEIGHT_KEEP * w_down - STEP_RATES[3] * mine[1].T
    new_out = WEIGHT_KEEP * w_out - STEP_RATES[1] * mine[2, :, :out_width].T
    ortho_qkv = jnp.stack([mine[3, :, j * third : (j + 1) * third] for j in range(3)])
    new_qkv = WEIGHT_KEEP * w_qkv - STEP_RATES[0] * ortho_qkv
    red_qkv, moment_qkv, new_qkv, red_head, head_second_new, head_new = (
        value.transpose(1, 0, 2)
        for value in (red_qkv, moment_qkv, new_qkv, red_head, head_second_new, head_new)
    )
    return (
        output,
        grad_in,
        red_qkv,
        red_out,
        red_up,
        red_down,
        moment_qkv,
        moment_out,
        moment_up,
        moment_down,
        new_qkv,
        new_out,
        new_up,
        new_down,
        red_vec,
        vec_second_new,
        vec_new,
        red_head,
        head_second_new,
        head_new,
        red_unit,
        unit_second_new,
        unit_new,
    )


def solution(mesh):
    token = P("dp", None)
    specs = (
        P("dp", None, "tensor"),
        P("tensor", "dp"),
        P("dp", "tensor"),
        P("tensor", "dp"),
    )
    vec, head, unit = P(None, "dp"), P(None, "tensor", "dp"), P("tensor", "dp")
    return jax.shard_map(
        shards,
        mesh=mesh,
        in_specs=(token, token)
        + specs
        + (vec, head, unit)
        + specs
        + (vec, vec, head, head, unit, unit),
        out_specs=(token, token) + specs * 3 + (vec,) * 3 + (head,) * 3 + (unit,) * 3,
        check_vma=False,
    )
```
